128 devices in a mesh: segment: 2 (over core), seq: 16 (over y, x), tp: 4 (over z).
Axes of the slice: x: 4, y: 4, z: 4, core: 2. Of those that a mesh axis runs over, the one named last changes fastest.
Arguments:
- latents: bfloat16 [8, 1024, 3072], P(None, 'seq', 'tp'), may hold values from -6 to 6
- w_qkv: bfloat16 [2, 3072, 3, 1536], P('segment', None, None, 'tp'), may hold values from -0.109375 to 0.109375
- w_out: bfloat16 [2, 1536, 3072], P('segment', 'tp'), may hold values from -0.15625 to 0.15625
- modulation: float32 [2, 3, 3072], P('segment'), may hold values from -3 to 3
- qk_gain: float32 [2, 2, 128], P('segment'), may hold values from 0.5 to 2
- stale_cache: bfloat16 [2, 2, 8, 1024, 1536], P('segment', None, None, 'seq', 'tp'), may hold values from -70 to 70
- kv_tiles: int32 [2, 128, 8], P('segment'), may hold values from 0 to 127, as said below
- tile_counts: int32 [2, 128], P('segment'), may hold values from 2 to 8, as said below
- patch_order: int32 [8], replicated, may hold values from 0 to 7, each once
Outputs:
- handed: bfloat16 [2, 8, 1024, 3072], P('segment', None, 'seq', 'tp')
- new_cache: bfloat16 [2, 2, 8, 1024, 1536], P('segment', None, None, 'seq', 'tp')
The draws below stay inside these ranges and needn't reach their ends.
Inputs may be any that keep to these rules, and one draw needn't show every extreme that they name: `kv_tiles`: slot 0 of a row is the query tile itself; slot 1 is the tile 8192 // 128 + 1024 // 128 tiles further round; the other slots lie within (6) // 2 tiles of the query tile, counting cyclically over the 128 tiles. Tiles of a row may repeat; slots past the row's count are padding. `tile_counts`: how many leading slots of a row are live. `patch_order`: each patch once.
All inputs are finite; a program needn't handle non-finite values.
Results may differ from the reference program's by a relative error of at most 0.029.
Values may be sent and summed in bfloat16 or wider, within the bound.
No kernel may reach another device: no remote copies, remote signals or barrier semaphores. Data moves between devices by JAX's collectives and lax.ppermute only.
A program may use at most 192 MiB of HBM per device.

```python
import math
import jax
import jax.numpy as jnp
from jax import lax

D = 3072
HEADS = 12
HD = 128
TILE = 64
MAXK = 8
PATCHES = 8
PATCH_TOK = 1024
TOKENS = 8192
N_SEGMENT = 2
N_TP = 4


def draw_stale_cache(key, part):
    key = jax.random.fold_in(key, 13)
    shape = (N_SEGMENT, 2, PATCHES, PATCH_TOK, HEADS * HD)
    base = jnp.clip(jax.random.normal(key, shape, jnp.float32), -6.0, 6.0)
    return base.astype(jnp.bfloat16)


def draw_kv_tiles(key, part):
    key = jax.random.fold_in(key, 11)
    count_tiles = TOKENS // TILE
    near_slots = MAXK - 2
    own = jnp.arange(count_tiles, dtype=jnp.int32)
    opposite = (own + count_tiles // 2 + PATCH_TOK // (2 * TILE)) % count_tiles
    own_b = jnp.broadcast_to(own[None, :, None], (N_SEGMENT, count_tiles, 1))
    opp_b = jnp.broadcast_to(opposite[None, :, None], (N_SEGMENT, count_tiles, 1))
    if near_slots == 0:
        return jnp.concatenate([own_b, opp_b], axis=-1).astype(jnp.int32)
    steps_idx = jnp.arange(near_slots, dtype=jnp.int32)
    offsets = (steps_idx // 2 + 1) * (1 - 2 * (steps_idx % 2))
    noise = jax.random.randint(key, (N_SEGMENT, count_tiles, near_slots), 0, 1 << 20)
    ranking = noise * near_slots + steps_idx
    ordering = jnp.argsort(ranking, axis=-1, stable=True)
    near = (own[None, :, None] + offsets[ordering]) % count_tiles
    return jnp.concatenate([own_b, opp_b, near], axis=-1).astype(jnp.int32)


def draw_tile_counts(key, part):
    key = jax.random.fold_in(key, 12)
    count_tiles = TOKENS // TILE
    base = jax.random.randint(jax.random.fold_in(key, 1), (N_SEGMENT, 1), 2, MAXK + 1)
    jitter = jax.random.randint(jax.random.fold_in(key, 2), (N_SEGMENT, count_tiles), -1, 2)
    counts = jnp.clip(base + jitter, 2, MAXK)
    row_top = jax.random.randint(jax.random.fold_in(key, 3), (), 0, N_SEGMENT)
    col_top = jax.random.randint(jax.random.fold_in(key, 4), (), 0, count_tiles)
    counts = counts.at[row_top, col_top].set(MAXK)
    row_low = jax.random.randint(jax.random.fold_in(key, 5), (), 0, N_SEGMENT)
    col_low = (col_top + 1) % count_tiles
    counts = counts.at[row_low, col_low].set(2)
    return counts.astype(jnp.int32)


def block_levels(key, extent, pieces, least, top_value):
    level, own = 1.0, jax.random.fold_in(key, 6)
    for dim, blocks in pieces:
        steps = jnp.exp(jax.random.uniform(jax.random.fold_in(own, dim), (blocks,), jnp.float32, least / len(pieces), top_value / len(pieces)))
        level = level * jnp.repeat(steps, extent[dim] // blocks).reshape([-1 if axis == dim else 1 for axis in range(len(extent))])
    return level


def gaussian(rng, extent, width, reach, pieces=(), held_as=jnp.bfloat16):
    level = block_levels(rng, extent, pieces, -0.22, 0.18) if pieces else 1.0
    values = jax.random.normal(rng, extent, jnp.float32) * width * level
    return jnp.minimum(jnp.maximum(values, -reach), reach).astype(held_as)


def setup_inputs(seed: int = 0) -> dict:
    seeds = jax.random.split(jax.random.key(seed), 10)
    latents = gaussian(seeds[0], (PATCHES, PATCH_TOK, D), 1.0, 6.0, ((1, 16), (2, 4)))
    w_qkv = gaussian(seeds[1], (N_SEGMENT, D, 3, HEADS * HD), D ** -0.5, 0.109375, ((0, 2), (3, 4)))
    w_out = gaussian(seeds[2], (N_SEGMENT, HEADS * HD, D), (HEADS * HD) ** -0.5, 0.15625, ((0, 2), (1, 4)))
    modulation = gaussian(seeds[3], (N_SEGMENT, 3, D), 0.5, 3.0, ((0, 2),), jnp.float32)
    qk_gain = jnp.clip(jnp.exp(math.log(2.0) - 1.3862944 * jax.random.uniform(seeds[4], (N_SEGMENT, 2, HD), jnp.float32) ** block_levels(seeds[4], (N_SEGMENT, 2, HD), ((0, 2),), -0.2, 0.2)), 0.5, 2.0)
    stale_cache = draw_stale_cache(jax.random.fold_in(seeds[9], 71), 0)
    kv_tiles = draw_kv_tiles(jax.random.fold_in(seeds[9], 71), 0)
    tile_counts = draw_tile_counts(jax.random.fold_in(seeds[9], 71), 0)
    patch_order = jax.random.permutation(seeds[8], PATCHES).astype(jnp.int32)
    return {"latents": latents, "w_qkv": w_qkv, "w_out": w_out, "modulation": modulation, "qk_gain": qk_gain, "stale_cache": stale_cache, "kv_tiles": kv_tiles, "tile_counts": tile_counts, "patch_order": patch_order}


def norm_heads(values, norm_gain):
    return values * lax.rsqrt(lax.optimization_barrier(jnp.mean(values * values, axis=-1, keepdims=True)) + 1e-06) * norm_gain

def tile_attention(q_tiles, key_tiles, value_tiles, live_mask):
    score_scale = q_tiles.shape[-1] ** (-0.5)
    scores = jnp.einsum('iqhe,ikthe->ihqkt', q_tiles.astype(jnp.float32), key_tiles.astype(jnp.float32)) * score_scale
    scores = jnp.where(live_mask[:, None, None, :, None], scores, -1e+30)
    row_peak = lax.optimization_barrier(jnp.max(scores, axis=(3, 4), keepdims=True))
    weights_raw = jnp.exp(scores - row_peak)
    totals = lax.optimization_barrier(jnp.sum(weights_raw, axis=(3, 4)))
    rounded = weights_raw.astype(jnp.bfloat16).astype(jnp.float32)
    summed = jnp.einsum('ihqkt,ikthe->iqhe', rounded, value_tiles.astype(jnp.float32))
    return summed / jnp.transpose(totals, (0, 2, 1))[..., None]

def reference(latents, w_qkv, w_out, modulation, qk_gain, stale_cache, kv_tiles, tile_counts, patch_order):
    patches, patch_rows, model_width = latents.shape
    segments = w_qkv.shape[0]
    inner = w_out.shape[1]
    head_dim = qk_gain.shape[-1]
    heads = inner // head_dim
    tiles_patch = patch_rows // TILE
    group_width = inner // N_TP
    hidden = latents
    outputs = []
    caches = []
    for segment_pos in range(segments):
        cache_now = stale_cache[segment_pos]
        modul = modulation[segment_pos]
        norm_gain = qk_gain[segment_pos]
        tile_table = kv_tiles[segment_pos]
        counts = tile_counts[segment_pos]
        weights = w_qkv[segment_pos].reshape(model_width, 3 * inner)
        out_groups = w_out[segment_pos].reshape(N_TP, group_width, model_width).astype(jnp.float32)
        result = hidden
        for micro_id in range(patches):
            patch_id = patch_order[micro_id]
            inputs_now = hidden[patch_id]
            xf = inputs_now.astype(jnp.float32)
            centred = xf - lax.optimization_barrier(jnp.mean(xf, axis=-1, keepdims=True))
            normed = centred * lax.rsqrt(lax.optimization_barrier(jnp.mean(centred * centred, axis=-1, keepdims=True)) + 1e-06)
            modded = (normed * (1.0 + modul[1]) + modul[0]).astype(jnp.bfloat16)
            projected = jnp.dot(modded, weights, preferred_element_type=jnp.float32)
            projected = projected.reshape(patch_rows, 3, heads, head_dim)
            queries = norm_heads(projected[:, 0], norm_gain[0]).astype(jnp.bfloat16)
            keys_new = norm_heads(projected[:, 1], norm_gain[1]).astype(jnp.bfloat16)
            values_new = projected[:, 2].astype(jnp.bfloat16)
            fresh_kv = jnp.stack([keys_new.reshape(patch_rows, inner), values_new.reshape(patch_rows, inner)])
            cache_now = cache_now.at[:, patch_id].set(fresh_kv)
            tile_pool = cache_now.reshape(2, patches * tiles_patch, TILE, heads, head_dim)
            query_tiles = patch_id * tiles_patch + jnp.arange(tiles_patch, dtype=jnp.int32)
            chosen = tile_table[query_tiles]
            live_mask = jnp.arange(chosen.shape[1], dtype=jnp.int32)[None, :] < counts[query_tiles][:, None]
            attended = tile_attention(queries.reshape(tiles_patch, TILE, heads, head_dim), tile_pool[0][chosen], tile_pool[1][chosen], live_mask)
            attended = attended.reshape(patch_rows, inner).astype(jnp.bfloat16)
            attended_groups = attended.reshape(patch_rows, N_TP, group_width).astype(jnp.float32)
            group_out = jnp.einsum('rgc,gcd->grd', attended_groups, out_groups)
            group_out = lax.optimization_barrier(group_out.astype(jnp.bfloat16)).astype(jnp.float32)
            projected_out = lax.optimization_barrier(jnp.sum(group_out, axis=0))
            mixed_out = (xf + modul[2] * projected_out).astype(jnp.bfloat16)
            result = result.at[patch_id].set(mixed_out)
        hidden = result
        outputs.append(hidden)
        caches.append(cache_now)
    handed = jnp.stack([outputs[-1]] + outputs[:-1])
    return (handed, jnp.stack(caches))
```

```python
import jax
import jax.numpy as jnp
from jax import lax
from jax.experimental import pallas as pl
from jax.experimental.pallas import tpu as pltpu
from jax.sharding import PartitionSpec as P

TILE = 64
EPS = 1e-06
NEAR = (0, 1, -1, 2, -2, 3, -3)
VMEM_BYTES = 48 * 1024 * 1024


def shifted(block, axis, distance):
    devices = range(lax.axis_size(axis))
    route = [((i - distance) % len(devices), i) for i in devices]
    return lax.ppermute(block, axis, route)


def params():
    return pltpu.CompilerParams(vmem_limit_bytes=VMEM_BYTES)


def project_kernel(
    meta,
    x_own,
    x_next,
    x_far_a,
    x_far_b,
    x_prev,
    shift,
    scale,
    gain,
    w_own,
    w_other,
    stale,
    q_out,
    kv_out,
    *rest,
):
    *payloads, xs, acc, stat = rest
    step = pl.program_id(0)
    rows, cols = x_own.shape
    width = cols * 4
    half = rows // 2

    @pl.when(step == 0)
    def _():
        xs[0] = x_own[...]
        xs[1] = x_next[...]
        xs[2, :half] = x_far_a[...]
        xs[2, half:] = x_far_b[...]
        xs[3] = x_prev[...]
        total = jnp.zeros((rows, 1), jnp.float32)
        for part in range(4):
            total += jnp.sum(xs[part].astype(jnp.float32), axis=-1, keepdims=True)
        mean = total / width
        square = jnp.zeros((rows, 1), jnp.float32)
        for part in range(4):
            centred = xs[part].astype(jnp.float32) - mean
            square += jnp.sum(centred * centred, axis=-1, keepdims=True)
        stat[0] = mean
        stat[1] = lax.rsqrt(square / width + EPS)
        acc[...] = jnp.zeros_like(acc)

    normed = (xs[step].astype(jnp.float32) - stat[0]) * stat[1]
    modded = (normed * (1.0 + scale[0]) + shift[0]).astype(jnp.bfloat16)

    @pl.when(meta[1] == 1)
    def _():
        for part in range(3):
            acc[part] += jnp.dot(modded, w_own[part], preferred_element_type=jnp.float32)

    @pl.when(meta[1] == 0)
    def _():
        for part in range(3):
            acc[part] += jnp.dot(modded, w_other[part], preferred_element_type=jnp.float32)

    @pl.when(step == 3)
    def _():
        patches, rows_patch, heads_cols = kv_out.shape[1:]
        head_dim = gain.shape[-1]
        for head in range(heads_cols // head_dim):
            cut = slice(head * head_dim, (head + 1) * head_dim)
            for part in range(2):
                vec = acc[part, :, cut]
                mean_sq = jnp.mean(vec * vec, axis=-1, keepdims=True)
                vec = vec * lax.rsqrt(mean_sq + EPS) * gain[part : part + 1]
                vec = vec.astype(jnp.bfloat16).reshape(patches, rows_patch, head_dim)
                if part == 0:
                    q_out[:, :, cut] = vec
                else:
                    kv_out[0, :, :, cut] = vec
        kv_out[1] = acc[2].astype(jnp.bfloat16).reshape(patches, rows_patch, heads_cols)
        for which, out in enumerate(payloads):
            for patch in range(patches):
                place = 2 + which * patches + patch
                source = meta[place]
                fresh = meta[place + len(payloads) * patches]

                @pl.when(fresh == 1)
                def _():
                    out[:, patch] = kv_out[:, source]

                @pl.when(fresh == 0)
                def _():
                    out[:, patch] = stale[:, source]


def project(meta, blocks, shift, scale, gain, w_own, w_other, stale, count):
    rows, cols = blocks[0].shape
    heads_cols = w_own.shape[-1]
    kv_shape = stale.shape

    def whole(shape):
        return pl.BlockSpec(shape, lambda j, meta: (0,) * len(shape))

    def feature(j, meta):
        return lax.rem(meta[0] + j, 4)

    w_block = (3, cols, heads_cols)
    kv_struct = jax.ShapeDtypeStruct(kv_shape, jnp.bfloat16)
    q_struct = jax.ShapeDtypeStruct(kv_shape[1:], jnp.bfloat16)
    return pl.pallas_call(
        project_kernel,
        grid_spec=pltpu.PrefetchScalarGridSpec(
            num_scalar_prefetch=1,
            grid=(4,),
            in_specs=[whole(b.shape) for b in blocks]
            + [pl.BlockSpec((1, 1, cols), lambda j, meta: (feature(j, meta), 0, 0))] * 2
            + [
                whole(gain.shape),
                pl.BlockSpec(
                    w_block, lambda j, meta: (0, jnp.where(meta[1] == 1, feature(j, meta), 0), 0)
                ),
                pl.BlockSpec(
                    w_block, lambda j, meta: (0, jnp.where(meta[1] == 1, 0, feature(j, meta)), 0)
                ),
                whole(kv_shape),
            ],
            out_specs=[whole(q_struct.shape)] + [whole(kv_shape)] * (1 + count),
            scratch_shapes=[
                pltpu.VMEM((4, rows, cols), jnp.bfloat16),
                pltpu.VMEM((3, rows, heads_cols), jnp.float32),
                pltpu.VMEM((2, rows, 1), jnp.float32),
            ],
        ),
        out_shape=[q_struct] + [kv_struct] * (1 + count),
        compiler_params=params(),
        name="project",
    )(meta, *blocks, shift, scale, gain, w_own, w_other, stale)


def attend_kernel(
    edge, q_own, q_other, own, up1, down1, up2, down2, edge2, up3, down3, far, multiple, *rest
):
    out_own, out_other, qs, kvs = rest
    rows = own.shape[2]
    head_dim = 128
    heads = own.shape[-1] // head_dim
    qs[:rows] = q_own[0]
    qs[rows:] = q_other[0]
    for place, ref in enumerate((own, up1, down1, up2, down2, up3, down3, far)):
        kvs[:, place * rows : (place + 1) * rows] = ref[:, 0]

    @pl.when(edge[0] == 1)
    def _():
        kvs[:, 3 * rows : 4 * rows] = edge2[:, 0]

    @pl.when(edge[1] == 1)
    def _():
        kvs[:, 4 * rows : 5 * rows] = edge2[:, 0]

    times = multiple[0]
    lane = lax.broadcasted_iota(jnp.int32, (2 * rows, head_dim), 1)
    extra = jnp.zeros((2 * rows, head_dim), jnp.float32)
    for head in range(heads):
        cut = slice(head * head_dim, (head + 1) * head_dim)
        scores = lax.dot_general(
            qs[:, cut], kvs[0, :, cut], (((1,), (1,)), ((), ())), preferred_element_type=jnp.float32
        )
        scores = jnp.where(times > 0.0, scores * head_dim ** (-0.5), -1e30)
        peak = jnp.max(scores, axis=-1, keepdims=True)
        weights = jnp.exp(scores - peak) * times
        total = jnp.sum(weights, axis=-1, keepdims=True)
        summed = jnp.dot(
            weights.astype(jnp.bfloat16), kvs[1, :, cut], preferred_element_type=jnp.float32
        )
        out_own[0, :, cut] = summed[:rows]
        out_other[0, :, cut] = summed[rows:]
        extra = jnp.where(lane == head, peak, extra)
        extra = jnp.where(lane == 64 + head, total, extra)
    out_own[0, :, heads * head_dim :] = extra[:rows]
    out_other[0, :, heads * head_dim :] = extra[rows:]


def attend(edge, q_own, q_other, kvs, multiple):
    _, patches, rows, heads_cols = kvs[0].shape
    keys = multiple.shape[-1]
    out_cols = heads_cols + 128
    q_spec = pl.BlockSpec((1, rows, heads_cols), lambda p, edge: (p, 0, 0))
    kv_spec = pl.BlockSpec((2, 1, rows, heads_cols), lambda p, edge: (0, p, 0, 0))
    out_spec = pl.BlockSpec((1, rows, out_cols), lambda p, edge: (p, 0, 0))
    out_struct = jax.ShapeDtypeStruct((patches, rows, out_cols), jnp.float32)
    return pl.pallas_call(
        attend_kernel,
        grid_spec=pltpu.PrefetchScalarGridSpec(
            num_scalar_prefetch=1,
            grid=(patches,),
            in_specs=[q_spec] * 2
            + [kv_spec] * len(kvs)
            + [pl.BlockSpec((1, 1, keys), lambda p, edge: (p, 0, 0))],
            out_specs=[out_spec] * 2,
            scratch_shapes=[
                pltpu.VMEM((2 * rows, heads_cols), jnp.bfloat16),
                pltpu.VMEM((2, keys, heads_cols), jnp.bfloat16),
            ],
        ),
        out_shape=[out_struct] * 2,
        compiler_params=params(),
        name="attend",
    )(edge, q_own, q_other, *kvs, multiple)


def merge_kernel(meta, part_a, part_b, w_own, w_other, att, y_a, y_b):
    head_dim = 128
    heads = att.shape[-1] // head_dim
    half = y_a.shape[0]
    extra_a = part_a[:, heads * head_dim :]
    extra_b = part_b[:, heads * head_dim :]
    for head in range(heads):
        cut = slice(head * head_dim, (head + 1) * head_dim)
        peak_a, total_a = extra_a[:, head : head + 1], extra_a[:, 64 + head : 65 + head]
        peak_b, total_b = extra_b[:, head : head + 1], extra_b[:, 64 + head : 65 + head]
        peak = jnp.maximum(peak_a, peak_b)
        grow_a, grow_b = jnp.exp(peak_a - peak), jnp.exp(peak_b - peak)
        total = total_a * grow_a + total_b * grow_b
        summed = part_a[:, cut] * grow_a + part_b[:, cut] * grow_b
        att[:, cut] = (summed / total).astype(jnp.bfloat16)

    def finish(weight):
        product = jnp.dot(att[...], weight[...], preferred_element_type=jnp.float32)
        y_a[...] = product[:half].astype(jnp.bfloat16)
        y_b[...] = product[half:].astype(jnp.bfloat16)

    @pl.when(meta[1] == 1)
    def _():
        finish(w_own)

    @pl.when(meta[1] == 0)
    def _():
        finish(w_other)


def out_weight_specs(rows, cols, place):
    def chosen(j, meta):
        return (0, jnp.where(meta[1] == 1, lax.rem(meta[0] + place(j), 4), 0))

    def spare(j, meta):
        return (0, jnp.where(meta[1] == 1, 0, lax.rem(meta[0] + place(j), 4)))

    return [pl.BlockSpec((rows, cols), chosen), pl.BlockSpec((rows, cols), spare)]


def merge(meta, part_a, part_b, w_own, w_other):
    rows = part_a.shape[0]
    heads_cols, width = w_own.shape
    cols = width // 4

    def whole(shape):
        return pl.BlockSpec(shape, lambda j, meta: (0,) * len(shape))

    return pl.pallas_call(
        merge_kernel,
        grid_spec=pltpu.PrefetchScalarGridSpec(
            num_scalar_prefetch=1,
            grid=(1,),
            in_specs=[whole(part_a.shape)] * 2
            + out_weight_specs(heads_cols, cols, lambda j: 2),
            out_specs=[whole((rows, heads_cols))] + [whole((rows // 2, cols))] * 2,
        ),
        out_shape=[jax.ShapeDtypeStruct((rows, heads_cols), jnp.bfloat16)]
        + [jax.ShapeDtypeStruct((rows // 2, cols), jnp.bfloat16)] * 2,
        compiler_params=params(),
        name="merge",
    )(meta, part_a, part_b, w_own, w_other)


def spread_kernel(meta, att, from_prev, from_next, w_own, w_other, to_next, to_prev, keep):
    step = pl.program_id(0)
    half = from_prev.shape[0]

    def finish(weight):
        product = jnp.dot(att[...], weight[...], preferred_element_type=jnp.float32)

        @pl.when(step == 0)
        def _():
            to_next[:half] = (product[:half] + from_prev[...].astype(jnp.float32)).astype(
                jnp.bfloat16
            )
            to_next[half:] = product[half:].astype(jnp.bfloat16)

        @pl.when(step == 1)
        def _():
            to_prev[:half] = product[:half].astype(jnp.bfloat16)
            to_prev[half:] = (product[half:] + from_next[...].astype(jnp.float32)).astype(
                jnp.bfloat16
            )

        @pl.when(step == 2)
        def _():
            keep[...] = product

    @pl.when(meta[1] == 1)
    def _():
        finish(w_own)

    @pl.when(meta[1] == 0)
    def _():
        finish(w_other)


def spread(meta, att, from_prev, from_next, w_own, w_other):
    rows, heads_cols = att.shape
    cols = w_own.shape[1] // 4

    def whole(shape):
        return pl.BlockSpec(shape, lambda j, meta: (0,) * len(shape))

    return pl.pallas_call(
        spread_kernel,
        grid_spec=pltpu.PrefetchScalarGridSpec(
            num_scalar_prefetch=1,
            grid=(3,),
            in_specs=[whole(att.shape), whole(from_prev.shape), whole(from_next.shape)]
            + out_weight_specs(
                heads_cols, cols, lambda j: jnp.where(j == 0, 1, jnp.where(j == 1, 3, 0))
            ),
            out_specs=[whole((rows, cols))] * 3,
        ),
        out_shape=[
            jax.ShapeDtypeStruct((rows, cols), jnp.bfloat16),
            jax.ShapeDtypeStruct((rows, cols), jnp.bfloat16),
            jax.ShapeDtypeStruct((rows, cols), jnp.float32),
        ],
        compiler_params=params(),
        name="spread",
    )(meta, att, from_prev, from_next, w_own, w_other)


def local(
    latents, w_qkv, w_out, modulation, qk_gain, stale_cache, kv_tiles, tile_counts, patch_order
):
    core = lax.axis_index("segment")
    seq_size = lax.axis_size("seq")
    seq_pos = lax.axis_index("seq")
    tp_pos = lax.axis_index("tp")
    patches, patch_rows, part_cols = latents.shape
    rows_core = patch_rows // 2
    rows = patches * rows_core
    w_own = jnp.transpose(w_qkv[0], (1, 0, 2))
    wo_own = w_out[0]
    heads_cols = wo_own.shape[0]
    width = wo_own.shape[1]
    head_dim = qk_gain.shape[-1]
    tiles = patches * seq_size

    mine = lax.dynamic_slice_in_dim(latents, core * rows_core, rows_core, 1)
    x_own = mine.reshape(rows, part_cols)

    patch_ids = jnp.arange(patches, dtype=jnp.int32)
    query_tiles = patch_ids * seq_size + seq_pos
    table = lax.dynamic_index_in_dim(
        kv_tiles[0].reshape(patches, seq_size, -1), seq_pos, 1, keepdims=False
    )
    counts = lax.dynamic_index_in_dim(
        tile_counts[0].reshape(patches, seq_size), seq_pos, 1, keepdims=False
    )
    slots = table.shape[1]
    far = tiles // 2 + seq_size // 2
    reach = jnp.array([d % tiles for d in NEAR] + [far], jnp.int32)
    relative = (table - query_tiles[:, None]) % tiles
    live = jnp.arange(slots, dtype=jnp.int32)[None] < counts[:, None]
    hits = (relative[:, :, None] == reach[None, None, :]) & live[:, :, None]
    multiple_own = jnp.sum(hits.astype(jnp.float32), axis=1)

    small_own = jnp.concatenate(
        [modulation[0].reshape(-1), qk_gain[0].reshape(-1), multiple_own.reshape(-1)]
    )
    small_other = shifted(small_own, "segment", 1)
    w_other = shifted(w_own, "segment", 1)
    wo_other = shifted(wo_own, "segment", 1)
    stale_all = stale_cache[0]
    stale_own = lax.dynamic_slice_in_dim(stale_all, core * rows_core, rows_core, 2)
    stale_other = shifted(
        lax.dynamic_slice_in_dim(stale_all, (1 - core) * rows_core, rows_core, 2), "segment", 1
    )

    patch_shift = jnp.stack(
        [
            jnp.where(seq_pos < 1, 1, 0),
            jnp.where(seq_pos >= seq_size - 1, -1, 0),
            jnp.where(seq_pos < 3, 1, 0),
            jnp.where(seq_pos >= seq_size - 3, -1, 0),
            jnp.where(seq_pos < seq_size // 2, patches // 2 + 1, patches // 2),
            jnp.where(seq_pos == 1, 1, jnp.where(seq_pos == seq_size - 2, -1, 0)),
        ]
    ).astype(jnp.int32)
    key_patch = (patch_ids[None] + patch_shift[:, None]) % patches
    turns = jnp.arange(patches, dtype=jnp.int32)
    rank = jnp.sum(jnp.where(patch_order[None] == patch_ids[:, None], turns[None], 0), axis=-1)
    key_rank = jnp.sum(
        jnp.where(patch_order[None, None] == key_patch[..., None], turns[None, None], 0), axis=-1
    )
    fresh = (key_rank <= rank[None]).astype(jnp.int32)
    pairs = patch_shift.shape[0]
    plan = jnp.concatenate([key_patch.reshape(-1), fresh.reshape(-1)])
    edge = jnp.stack([seq_pos == seq_size - 1, seq_pos == 0]).astype(jnp.int32)
    ends = [(1, seq_size - 1), (seq_size - 2, 0)]

    hidden = x_own
    hiddens, caches = [], []
    for section in range(2):
        is_own = core == section
        meta = jnp.concatenate(
            [jnp.stack([tp_pos, is_own.astype(tp_pos.dtype)]).astype(jnp.int32), plan]
        )
        small = jnp.where(is_own, small_own, small_other)
        modul = small[: 3 * width].reshape(3, 4, 1, part_cols)
        gain = small[3 * width : 3 * width + 2 * head_dim].reshape(2, head_dim)
        multiple = small[3 * width + 2 * head_dim :].reshape(patches, -1)
        multiple = jnp.repeat(multiple, rows_core, axis=1)[:, None]
        gate = lax.dynamic_index_in_dim(modul[2], tp_pos, 0, keepdims=False)
        stale = jnp.where(is_own, stale_own, stale_other)

        half = rows // 2
        x_prev = shifted(hidden, "tp", 1)
        x_next = shifted(hidden, "tp", -1)
        far_a = shifted(x_prev[:half], "tp", 1)
        far_b = shifted(x_next[half:], "tp", -1)
        q_own, kv, up1, down1, up3, down3, across, ended = project(
            meta,
            (hidden, x_next, far_a, far_b, x_prev),
            modul[0],
            modul[1],
            gain,
            w_own,
            w_other,
            stale,
            pairs,
        )
        up1 = shifted(up1, "seq", -1)
        down1 = shifted(down1, "seq", 1)
        across = shifted(across, "seq", -(seq_size // 2))
        up3 = shifted(up3, "seq", -3)
        down3 = shifted(down3, "seq", 3)
        up2 = shifted(up1, "seq", -1)
        down2 = shifted(down1, "seq", 1)
        edge2 = lax.ppermute(ended, "seq", ends)
        q_other = shifted(q_own, "segment", 1)
        kv_other = shifted(kv, "segment", 1)
        part_own, part_other = attend(
            edge,
            q_own,
            q_other,
            (kv, up1, down1, up2, down2, edge2, up3, down3, across),
            multiple,
        )
        part_back = shifted(part_other, "segment", 1)
        att, y_a, y_b = merge(
            meta,
            part_own.reshape(rows, -1),
            part_back.reshape(rows, -1),
            wo_own,
            wo_other,
        )
        from_prev = shifted(y_a, "tp", 1)
        from_next = shifted(y_b, "tp", -1)
        to_next, to_prev, keep = spread(meta, att, from_prev, from_next, wo_own, wo_other)
        got_prev = shifted(to_next, "tp", 1)
        got_next = shifted(to_prev, "tp", -1)
        head_sum = keep + got_prev.astype(jnp.float32) + got_next.astype(jnp.float32)
        hidden = (hidden.astype(jnp.float32) + gate * head_sum).astype(jnp.bfloat16)
        hiddens.append((hidden, shifted(hidden, "segment", 1)))
        caches.append((kv, kv_other))

    first = core == 0
    h_shape = (patches, rows_core, part_cols)
    upper = jnp.where(first, hiddens[1][0], hiddens[0][1]).reshape(h_shape)
    lower = jnp.where(first, hiddens[1][1], hiddens[0][0]).reshape(h_shape)
    handed = jnp.concatenate([upper, lower], axis=1)
    cache_upper = jnp.where(first, caches[0][0], caches[1][1])
    cache_lower = jnp.where(first, caches[0][1], caches[1][0])
    new_cache = jnp.concatenate([cache_upper, cache_lower], axis=2)
    return (handed[None], new_cache[None])


def solution(mesh):
    in_specs = (
        P(None, "seq", "tp"),
        P("segment", None, None, "tp"),
        P("segment", "tp", None),
        P("segment", None, None),
        P("segment", None, None),
        P("segment", None, None, "seq", "tp"),
        P("segment", None, None),
        P("segment", None),
        P(),
    )
    out_specs = (P("segment", None, "seq", "tp"), P("segment", None, None, "seq", "tp"))
    return jax.shard_map(local, mesh=mesh, in_specs=in_specs, out_specs=out_specs, check_vma=False)
```

```python
import jax
import jax.numpy as jnp
from jax import lax
from jax.experimental import pallas as pl
from jax.experimental.pallas import tpu as pltpu
from jax.sharding import PartitionSpec as P

EPS = 1e-06
HEAD_DIM = 128
FIRST = (0, 1, -1)
SECOND = (2, -2, 3, -3)
MIB = 1024 * 1024
ON_CHIP = pl.BlockSpec(memory_space=pltpu.VMEM)


def shifted(block, axis, distance):
    devices = range(lax.axis_size(axis))
    route = [((i - distance) % len(devices), i) for i in devices]
    return lax.ppermute(block, axis, route)


def after(values, *gates):
    return lax.optimization_barrier((values, gates))[0]


def params(mib):
    return pltpu.CompilerParams(vmem_limit_bytes=mib * MIB)


def project_kernel(
    meta,
    x_own,
    x_next,
    x_far_a,
    x_far_b,
    x_prev,
    shift,
    scale,
    gain,
    w_own,
    w_other,
    stale,
    q_out,
    kv_out,
    *rest,
):
    *payloads, xs, acc, stat = rest
    step = pl.program_id(0)
    rows, cols = x_own.shape
    width = cols * 4
    half = rows // 2

    @pl.when(step == 0)
    def _():
        xs[0] = x_own[...]
        xs[1] = x_next[...]
        xs[2, :half] = x_far_a[...]
        xs[2, half:] = x_far_b[...]
        xs[3] = x_prev[...]
        total = jnp.zeros((rows, 1), jnp.float32)
        for part in range(4):
            total += jnp.sum(xs[part].astype(jnp.float32), axis=-1, keepdims=True)
        mean = total / width
        square = jnp.zeros((rows, 1), jnp.float32)
        for part in range(4):
            centred = xs[part].astype(jnp.float32) - mean
            square += jnp.sum(centred * centred, axis=-1, keepdims=True)
        stat[0] = mean
        stat[1] = lax.rsqrt(square / width + EPS)
        acc[...] = jnp.zeros_like(acc)

    normed = (xs[step].astype(jnp.float32) - stat[0]) * stat[1]
    modded = (normed * (1.0 + scale[0]) + shift[0]).astype(jnp.bfloat16)

    @pl.when(meta[1] == 1)
    def _():
        for part in range(3):
            acc[part] += jnp.dot(modded, w_own[part], preferred_element_type=jnp.float32)

    @pl.when(meta[1] == 0)
    def _():
        for part in range(3):
            acc[part] += jnp.dot(modded, w_other[part], preferred_element_type=jnp.float32)

    @pl.when(step == 3)
    def _():
        patches, rows_patch, heads_cols = kv_out.shape[1:]
        head_dim = gain.shape[-1]
        for head in range(heads_cols // head_dim):
            cut = slice(head * head_dim, (head + 1) * head_dim)
            for part in range(2):
                vec = acc[part, :, cut]
                mean_sq = jnp.mean(vec * vec, axis=-1, keepdims=True)
                vec = vec * lax.rsqrt(mean_sq + EPS) * gain[part : part + 1]
                vec = vec.astype(jnp.bfloat16).reshape(patches, rows_patch, head_dim)
                if part == 0:
                    q_out[:, :, cut] = vec
                else:
                    kv_out[0, :, :, cut] = vec
        kv_out[1] = acc[2].astype(jnp.bfloat16).reshape(patches, rows_patch, heads_cols)
        for which, out in enumerate(payloads):
            for patch in range(patches):
                place = 2 + which * patches + patch
                source = meta[place]
                fresh = meta[place + len(payloads) * patches]

                @pl.when(fresh == 1)
                def _():
                    out[:, patch] = kv_out[:, source]

                @pl.when(fresh == 0)
                def _():
                    out[:, patch] = stale[:, source]


def project(meta, blocks, shift, scale, gain, w_own, w_other, stale, count):
    rows, cols = blocks[0].shape
    heads_cols = w_own.shape[-1]
    kv_shape = stale.shape

    def whole(shape):
        return pl.BlockSpec(shape, lambda j, meta: (0,) * len(shape))

    def feature(j, meta):
        return lax.rem(meta[0] + j, 4)

    w_block = (3, cols, heads_cols)
    kv_struct = jax.ShapeDtypeStruct(kv_shape, jnp.bfloat16)
    q_struct = jax.ShapeDtypeStruct(kv_shape[1:], jnp.bfloat16)
    return pl.pallas_call(
        project_kernel,
        grid_spec=pltpu.PrefetchScalarGridSpec(
            num_scalar_prefetch=1,
            grid=(4,),
            in_specs=[ON_CHIP] * len(blocks)
            + [pl.BlockSpec((1, 1, cols), lambda j, meta: (feature(j, meta), 0, 0))] * 2
            + [
                whole(gain.shape),
                pl.BlockSpec(
                    w_block, lambda j, meta: (0, jnp.where(meta[1] == 1, feature(j, meta), 0), 0)
                ),
                pl.BlockSpec(
                    w_block, lambda j, meta: (0, jnp.where(meta[1] == 1, 0, feature(j, meta)), 0)
                ),
                ON_CHIP,
            ],
            out_specs=[ON_CHIP] * (2 + count),
            scratch_shapes=[
                pltpu.VMEM((4, rows, cols), jnp.bfloat16),
                pltpu.VMEM((3, rows, heads_cols), jnp.float32),
                pltpu.VMEM((2, rows, 1), jnp.float32),
            ],
        ),
        out_shape=[q_struct] + [kv_struct] * (1 + count),
        compiler_params=params(20),
        name="project",
    )(meta, *blocks, shift, scale, gain, w_own, w_other, stale)


def attend_kernel(meta, q_own, q_other, *rest, count, follows):
    kvs = rest[:count]
    rest = rest[count:]
    if follows:
        ended, multiple, before, out_own, out_other, chosen = rest
    else:
        multiple, out = rest
    rows = q_own.shape[1]
    heads = q_own.shape[-1] // HEAD_DIM
    patches = q_own.shape[0]
    if follows:
        for place in range(2):

            @pl.when(meta[place] == 0)
            def _():
                chosen[place] = kvs[place][...]

            @pl.when(meta[place] == 1)
            def _():
                for patch in range(patches):
                    source = (patch + (1, patches - 1)[place]) % patches
                    fresh = meta[2 + place * patches + patch]

                    @pl.when(fresh == 1)
                    def _():
                        chosen[place, :, patch] = kvs[place][:, source]

                    @pl.when(fresh == 0)
                    def _():
                        chosen[place, :, patch] = ended[:, source]

        kvs = (chosen.at[0], chosen.at[1]) + tuple(kvs[2:])

    lane = lax.broadcasted_iota(jnp.int32, (2 * rows, HEAD_DIM), 1)
    for patch in range(patches):
        times = multiple[patch]
        extra = jnp.zeros((2 * rows, HEAD_DIM), jnp.float32)
        for head in range(heads):
            cut = slice(head * HEAD_DIM, (head + 1) * HEAD_DIM)
            queries = jnp.concatenate([q_own[patch, :, cut], q_other[patch, :, cut]], axis=0)
            keys = jnp.concatenate([kv[0, patch, :, cut] for kv in kvs], axis=0)
            values = jnp.concatenate([kv[1, patch, :, cut] for kv in kvs], axis=0)
            scores = lax.dot_general(
                queries, keys, (((1,), (1,)), ((), ())), preferred_element_type=jnp.float32
            )
            scores = jnp.where(times > 0.0, scores * HEAD_DIM ** (-0.5), -1e30)
            peak = jnp.max(scores, axis=-1, keepdims=True)
            if follows:
                peak_before = before[patch, :, heads * HEAD_DIM + head : heads * HEAD_DIM + head + 1]
                total_before = before[
                    patch, :, heads * HEAD_DIM + 64 + head : heads * HEAD_DIM + 65 + head
                ]
                peak = jnp.maximum(peak, peak_before)
            weights = jnp.exp(scores - peak) * times
            total = jnp.sum(weights, axis=-1, keepdims=True)
            summed = jnp.dot(
                weights.astype(jnp.bfloat16), values, preferred_element_type=jnp.float32
            )
            if follows:
                shrink = jnp.exp(peak_before - peak)
                total += total_before * shrink
                summed += before[patch, :, cut] * shrink
                out_own[patch, :, cut] = summed[:rows]
                out_other[patch, :, cut] = summed[rows:]
            else:
                out[patch, :, cut] = summed
            extra = jnp.where(lane == head, peak, extra)
            extra = jnp.where(lane == 64 + head, total, extra)
        if follows:
            out_own[patch, :, heads * HEAD_DIM :] = extra[:rows]
            out_other[patch, :, heads * HEAD_DIM :] = extra[rows:]
        else:
            out[patch, :, heads * HEAD_DIM :] = extra


def attend(meta, q_own, q_other, kvs, multiple, ended=None, before=None):
    patches, rows, heads_cols = q_own.shape
    follows = before is not None
    cols = heads_cols + HEAD_DIM
    if follows:
        outs = [jax.ShapeDtypeStruct((patches, rows, cols), jnp.float32)] * 2
        extras = [ended, multiple, before]
        scratch = [pltpu.VMEM((2,) + kvs[0].shape, jnp.bfloat16)]
    else:
        scratch = []
        outs = jax.ShapeDtypeStruct((patches, 2 * rows, cols), jnp.float32)
        extras = [multiple]

    def kernel(*refs):
        attend_kernel(*refs, count=len(kvs), follows=follows)

    return pl.pallas_call(
        kernel,
        in_specs=[pl.BlockSpec(memory_space=pltpu.SMEM)]
        + [ON_CHIP] * (2 + len(kvs) + len(extras)),
        out_specs=[ON_CHIP] * 2 if follows else ON_CHIP,
        out_shape=outs,
        scratch_shapes=scratch,
        compiler_params=params(8),
        name="attend_far" if follows else "attend_near",
    )(meta, q_own, q_other, *kvs, *extras)


def merge_kernel(part_a, part_b, att):
    patches, rows, _ = part_a.shape
    heads = att.shape[-1] // HEAD_DIM
    for patch in range(patches):
        extra_a = part_a[patch, :, heads * HEAD_DIM :]
        extra_b = part_b[patch, :, heads * HEAD_DIM :]
        for head in range(heads):
            cut = slice(head * HEAD_DIM, (head + 1) * HEAD_DIM)
            peak_a, total_a = extra_a[:, head : head + 1], extra_a[:, 64 + head : 65 + head]
            peak_b, total_b = extra_b[:, head : head + 1], extra_b[:, 64 + head : 65 + head]
            peak = jnp.maximum(peak_a, peak_b)
            grow_a, grow_b = jnp.exp(peak_a - peak), jnp.exp(peak_b - peak)
            total = total_a * grow_a + total_b * grow_b
            summed = part_a[patch, :, cut] * grow_a + part_b[patch, :, cut] * grow_b
            att[patch * rows : (patch + 1) * rows, cut] = (summed / total).astype(jnp.bfloat16)


def merge(part_a, part_b):
    patches, rows, cols = part_a.shape
    return pl.pallas_call(
        merge_kernel,
        in_specs=[ON_CHIP] * 2,
        out_specs=ON_CHIP,
        out_shape=jax.ShapeDtypeStruct((patches * rows, cols - HEAD_DIM), jnp.bfloat16),
        compiler_params=params(8),
        name="merge",
    )(part_a, part_b)


def output_kernel(att0, att1, att2, att3, weight, hidden, gate, out):
    product = jnp.zeros(out.shape, jnp.float32)
    for place, att in enumerate((att0, att1, att2, att3)):
        product += jnp.dot(att[...], weight[place], preferred_element_type=jnp.float32)
    out[...] = (hidden[...].astype(jnp.float32) + gate[...] * product).astype(out.dtype)


def output(atts, weight, hidden, gate):
    return pl.pallas_call(
        output_kernel,
        in_specs=[ON_CHIP] * 7,
        out_specs=ON_CHIP,
        out_shape=jax.ShapeDtypeStruct(hidden.shape, hidden.dtype),
        compiler_params=params(8),
        name="output",
    )(*atts, weight, hidden, gate)


def local(
    latents, w_qkv, w_out, modulation, qk_gain, stale_cache, kv_tiles, tile_counts, patch_order
):
    core = lax.axis_index("segment")
    seq_size = lax.axis_size("seq")
    seq_pos = lax.axis_index("seq")
    tp_size = lax.axis_size("tp")
    tp_pos = lax.axis_index("tp")
    patches, patch_rows, part_cols = latents.shape
    rows_core = patch_rows // 2
    rows = patches * rows_core
    w_own = jnp.transpose(w_qkv[0], (1, 0, 2))
    heads_cols, width = w_out.shape[1:]
    head_dim = qk_gain.shape[-1]
    tiles = patches * seq_size

    mine = lax.dynamic_slice_in_dim(latents, core * rows_core, rows_core, 1)
    hidden = mine.reshape(rows, part_cols)
    half = rows // 2
    x_prev = shifted(hidden, "tp", 1)
    x_next = shifted(hidden, "tp", -1)
    w_other = shifted(w_own, "segment", 1)
    small_own = jnp.concatenate([modulation[0].reshape(-1), qk_gain[0].reshape(-1)])
    small_other = shifted(small_own, "segment", 1)
    stale_all = stale_cache[0]
    stale_own = lax.dynamic_slice_in_dim(stale_all, core * rows_core, rows_core, 2)
    stale_other = shifted(
        lax.dynamic_slice_in_dim(stale_all, (1 - core) * rows_core, rows_core, 2), "segment", 1
    )
    x_prev, x_next, kv_tiles, tile_counts, patch_order = lax.optimization_barrier(
        (x_prev, x_next, kv_tiles, tile_counts, patch_order)
    )
    far_a = shifted(x_prev[:half], "tp", 1)
    far_b = shifted(x_next[half:], "tp", -1)

    patch_ids = jnp.arange(patches, dtype=jnp.int32)
    patch_shift = jnp.stack(
        [
            jnp.where(seq_pos < 1, 1, 0),
            jnp.where(seq_pos >= seq_size - 1, -1, 0),
            jnp.where(seq_pos < 3, 1, 0),
            jnp.where(seq_pos >= seq_size - 3, -1, 0),
            jnp.where(seq_pos < seq_size // 2, patches // 2 + 1, patches // 2),
            1,
            -1,
        ]
    ).astype(jnp.int32)
    key_patch = (patch_ids[None] + patch_shift[:, None]) % patches
    turns = jnp.arange(patches, dtype=jnp.int32)
    rank = jnp.sum(jnp.where(patch_order[None] == patch_ids[:, None], turns[None], 0), axis=-1)
    key_rank = jnp.sum(
        jnp.where(patch_order[None, None] == key_patch[..., None], turns[None, None], 0), axis=-1
    )
    fresh = (key_rank <= rank[None]).astype(jnp.int32)
    pairs = patch_shift.shape[0] - 2
    plan = jnp.concatenate([key_patch[:pairs].reshape(-1), fresh[:pairs].reshape(-1)])
    edge = jnp.stack([seq_pos == seq_size - 1, seq_pos == 0]).astype(jnp.int32)
    edge = jnp.concatenate([edge, fresh[pairs:].reshape(-1)])
    ends = [(1, seq_size - 1), (seq_size - 2, 0)]

    multiple_own = multiple_other = None
    hiddens, caches = [], []
    for section in range(2):
        is_own = core == section
        meta = jnp.concatenate(
            [jnp.stack([tp_pos, is_own.astype(tp_pos.dtype)]).astype(jnp.int32), plan]
        )
        small = jnp.where(is_own, small_own, small_other)
        modul = small[: 3 * width].reshape(3, tp_size, 1, part_cols)
        gain = small[3 * width :].reshape(2, head_dim)
        gate = lax.dynamic_index_in_dim(modul[2], tp_pos, 0, keepdims=False)
        stale = jnp.where(is_own, stale_own, stale_other)

        if section > 0:
            x_prev = shifted(hidden, "tp", 1)
            x_next = shifted(hidden, "tp", -1)
            far_a = shifted(x_prev[:half], "tp", 1)
            far_b = shifted(x_next[half:], "tp", -1)
            far_a, hidden_other = lax.optimization_barrier((far_a, hiddens[0][1]))
            hiddens[0] = (hidden, hidden_other)
            ended = lax.ppermute(after(stale, hidden), "seq", ends)
        else:
            ended = lax.ppermute(stale, "seq", ends)
        weight = after(w_out[0], far_a, far_b)
        pieces = [
            lax.dynamic_slice_in_dim(
                weight, lax.rem(tp_pos + j, tp_size) * part_cols, part_cols, 1
            )
            for j in range(tp_size)
        ]
        for j in range(1, tp_size):
            route = [
                (section * tp_size + i, section * tp_size + (i + j) % tp_size)
                for i in range(tp_size)
            ]
            pieces[j] = lax.ppermute(pieces[j], ("segment", "tp"), route)
        q_own, kv, up1, down1, up3, down3, across = project(
            meta,
            (hidden, x_next, far_a, far_b, x_prev),
            modul[0],
            modul[1],
            gain,
            w_own,
            w_other,
            stale,
            pairs,
        )
        up1 = shifted(up1, "seq", -1)
        down1 = shifted(down1, "seq", 1)
        q_other = shifted(q_own, "segment", 1)
        if section == 0:
            kv_tiles, tile_counts = after((kv_tiles, tile_counts), q_own)
            multiple_own = count_tiles(kv_tiles[0], tile_counts[0], patches, seq_pos, rows_core)
            multiple_other = shifted(multiple_own, "segment", 1)
        multiple = jnp.where(is_own, multiple_own, multiple_other)
        up1, down1, up3, down3, across, pieces, q_other = lax.optimization_barrier(
            (up1, down1, up3, down3, across, pieces, q_other)
        )
        up2 = shifted(up1, "seq", -1)
        down2 = shifted(down1, "seq", 1)
        up3 = shifted(up3, "seq", -3)
        down3 = shifted(down3, "seq", 3)
        across = shifted(across, "seq", -(seq_size // 2))
        cut = multiple.shape[-1] * len(FIRST) // 8
        before = attend(edge, q_own, q_other, (kv, up1, down1), multiple[..., :cut])
        part_own, part_other = attend(
            edge,
            q_own,
            q_other,
            (up2, down2, up3, down3, across),
            multiple[..., cut:],
            ended,
            before,
        )
        wo_own = jnp.stack(after(pieces, part_other))
        wo_other = shifted(wo_own, "segment", 1)
        kv_other = shifted(after(kv, part_other), "segment", 1)
        part_back = shifted(part_other, "segment", 1)
        att = merge(part_own, part_back)
        atts = [att] + [shifted(att, "tp", j) for j in (1, 2, 3)]
        wo = jnp.where(is_own, wo_own, wo_other)
        hidden = output(atts, wo, hidden, gate)
        hidden, kv_other = lax.optimization_barrier((hidden, kv_other))
        hiddens.append((hidden, shifted(hidden, "segment", 1)))
        caches.append((kv, kv_other))

    first = core == 0
    h_shape = (patches, rows_core, part_cols)
    upper = jnp.where(first, hiddens[1][0], hiddens[0][1]).reshape(h_shape)
    lower = jnp.where(first, hiddens[1][1], hiddens[0][0]).reshape(h_shape)
    handed = jnp.concatenate([upper, lower], axis=1)
    cache_upper = jnp.where(first, caches[0][0], caches[1][1])
    cache_lower = jnp.where(first, caches[0][1], caches[1][0])
    new_cache = jnp.concatenate([cache_upper, cache_lower], axis=2)
    return (handed[None], new_cache[None])


def count_tiles(table, counts, patches, seq_pos, repeat):
    tiles, slots = table.shape
    seq_size = tiles // patches
    table = lax.dynamic_index_in_dim(
        table.reshape(patches, seq_size, slots), seq_pos, 1, keepdims=False
    )
    counts = lax.dynamic_index_in_dim(
        counts.reshape(patches, seq_size), seq_pos, 1, keepdims=False
    )
    query_tiles = jnp.arange(patches, dtype=jnp.int32) * seq_size + seq_pos
    distances = FIRST + SECOND + (tiles // 2 + seq_size // 2,)
    reach = jnp.repeat(jnp.array([d % tiles for d in distances], jnp.int32), repeat)
    relative = (table - query_tiles[:, None]) % tiles
    live = jnp.arange(slots, dtype=jnp.int32)[None] < counts[:, None]
    hits = (relative[:, :, None] == reach[None, None]) & live[:, :, None]
    return jnp.sum(hits.astype(jnp.float32), axis=1)[:, None]


def solution(mesh):
    in_specs = (
        P(None, "seq", "tp"),
        P("segment", None, None, "tp"),
        P("segment", "tp", None),
        P("segment", None, None),
        P("segment", None, None),
        P("segment", None, None, "seq", "tp"),
        P("segment", None, None),
        P("segment", None),
        P(),
    )
    out_specs = (P("segment", None, "seq", "tp"), P("segment", None, None, "seq", "tp"))
    return jax.shard_map(local, mesh=mesh, in_specs=in_specs, out_specs=out_specs, check_vma=False)
```

```python
import jax
import jax.numpy as jnp
from jax import lax
from jax.experimental import pallas as pl
from jax.experimental.pallas import tpu as pltpu
from jax.sharding import PartitionSpec as P

EPS = 1e-06
HEAD_DIM = 128
REACH = 3
MIB = 1024 * 1024
ON_CHIP = pl.BlockSpec(memory_space=pltpu.VMEM)
SCALARS = pl.BlockSpec(memory_space=pltpu.SMEM)


def shifted(block, axis, distance):
    devices = range(lax.axis_size(axis))
    route = [((i - distance) % len(devices), i) for i in devices]
    return lax.ppermute(block, axis, route)


def after(values, *gates):
    return lax.optimization_barrier((values, gates))[0]


def params(mib):
    return pltpu.CompilerParams(vmem_limit_bytes=mib * MIB)


def struct(shape, dtype=jnp.bfloat16):
    return jax.ShapeDtypeStruct(shape, dtype)


def to_work(blocks):
    rounds, size = len(blocks), lax.axis_size("seq")
    share = size // rounds
    out = []
    for r, block in enumerate(blocks):
        route = [
            (s, share * ((s % rounds - r) % rounds) + s // rounds) for s in range(size)
        ]
        out.append(lax.ppermute(block, "seq", route))
    return out


def to_home(blocks):
    rounds, size = len(blocks), lax.axis_size("seq")
    share = size // rounds
    out = []
    for r, block in enumerate(blocks):
        route = [
            (i, rounds * (i % share) + (i // share + r) % rounds) for i in range(size)
        ]
        out.append(lax.ppermute(block, "seq", route))
    return out


def deal_latents_kernel(meta, latents, *outs):
    rounds, rows = len(outs), outs[0].shape[0]
    first = pl.multiple_of(meta[0] * rows, rows)
    for r, out in enumerate(outs):
        patch = lax.rem(meta[1] + rounds - r, rounds)
        out[...] = latents[patch, pl.ds(first, rows)]


def deal_latents(meta, latents):
    patches, rows, cols = latents.shape
    return pl.pallas_call(
        deal_latents_kernel,
        in_specs=[SCALARS, ON_CHIP],
        out_specs=[ON_CHIP] * patches,
        out_shape=[struct((rows // 2, cols))] * patches,
        compiler_params=params(8),
        name="deal_latents",
    )(meta, latents)


def halve_stale_kernel(meta, stale, mine, theirs):
    rows, cols = mine.shape[1], stale.shape[-1]
    for which, out in enumerate((mine, theirs)):
        first = meta[0] if which == 0 else 1 - meta[0]
        first = pl.multiple_of(first * rows, rows)
        for half in range(2):
            out[:, :, half * cols : (half + 1) * cols] = stale[half, :, pl.ds(first, rows)]


def halve_stale(meta, stale):
    _, patches, rows, cols = stale.shape
    out = struct((patches, rows // 2, 2 * cols))
    return pl.pallas_call(
        halve_stale_kernel,
        in_specs=[SCALARS, ON_CHIP],
        out_specs=[ON_CHIP] * 2,
        out_shape=[out] * 2,
        compiler_params=params(8),
        name="halve_stale",
    )(meta, stale)


def deal_stale_kernel(meta, own, other, *outs):
    rounds, rows = len(outs), own.shape[1]
    for r, out in enumerate(outs):
        patch = lax.rem(meta[1] + rounds - r, rounds)
        out[:rows] = own[patch]
        out[rows:] = other[patch]


def deal_stale(meta, own, other):
    patches, rows, cols = own.shape
    return pl.pallas_call(
        deal_stale_kernel,
        in_specs=[SCALARS] + [ON_CHIP] * 2,
        out_specs=[ON_CHIP] * patches,
        out_shape=[struct((2 * rows, cols))] * patches,
        compiler_params=params(8),
        name="deal_stale",
    )(meta, own, other)


def sort_stale_kernel(meta, *refs):
    *blocks, out = refs
    rounds, rows = len(blocks), out.shape[1]
    first = pl.multiple_of((1 - meta[0]) * rows, rows)
    for r, block in enumerate(blocks):
        out[lax.rem(meta[2] + r, rounds)] = block[pl.ds(first, rows)]


def sort_stale(meta, blocks):
    rows, cols = blocks[0].shape
    return pl.pallas_call(
        sort_stale_kernel,
        in_specs=[SCALARS] + [ON_CHIP] * len(blocks),
        out_specs=ON_CHIP,
        out_shape=struct((len(blocks), rows // 2, cols)),
        compiler_params=params(8),
        name="sort_stale",
    )(meta, *blocks)


def deal_results_kernel(meta, for_first, for_second, got, *outs):
    rounds, rows = len(outs), got.shape[1]

    def deal(upper, lower):
        for r, out in enumerate(outs):
            tile = lax.rem(meta[2] + r, rounds)
            out[:rows] = upper[tile]
            out[rows:] = lower[tile]

    @pl.when(meta[0] == 0)
    def _():
        deal(for_first, got)

    @pl.when(meta[0] == 1)
    def _():
        deal(got, for_second)


def deal_results(meta, for_first, for_second, got):
    tiles, rows, cols = got.shape
    return pl.pallas_call(
        deal_results_kernel,
        in_specs=[SCALARS] + [ON_CHIP] * 3,
        out_specs=[ON_CHIP] * tiles,
        out_shape=[struct((2 * rows, cols))] * tiles,
        compiler_params=params(8),
        name="deal_results",
    )(meta, for_first, for_second, got)


def collect_kernel(meta, *refs):
    *blocks, handed, cache = refs
    rounds = len(blocks) // 2
    cols = cache.shape[-1]

    def collect(features, keys):
        for r in range(rounds):
            patch = lax.rem(meta[1] + rounds - r, rounds)
            handed[patch] = features[r][...]
            cache[0, patch] = keys[r][:, :cols]
            cache[1, patch] = keys[r][:, cols:]

    @pl.when(meta[0] == 0)
    def _():
        collect(blocks[rounds:], blocks[:rounds])

    @pl.when(meta[0] == 1)
    def _():
        collect(blocks[:rounds], blocks[rounds:])


def collect(meta, early, late):
    rows, cols = early[0].shape
    rounds = len(early)
    return pl.pallas_call(
        collect_kernel,
        in_specs=[SCALARS] + [ON_CHIP] * (2 * rounds),
        out_specs=[ON_CHIP] * 2,
        out_shape=[struct((rounds, rows, cols)), struct((2, rounds, rows, cols // 2))],
        compiler_params=params(8),
        name="collect",
    )(meta, *early, *late)


def choose(meta, kv, stale, outs):
    tiles = kv.shape[0]
    for place, out in enumerate(outs):
        first = tiles - REACH if place == 1 else 0
        cut = slice(first, first + out.shape[0])

        @pl.when(meta[3 + place] == 1)
        def _():
            out[...] = kv[cut]

        @pl.when(meta[3 + place] == 0)
        def _():
            out[...] = stale[cut]


def choose_kernel(meta, kv, *refs):
    *blocks, lo_out, hi_out, far_out = refs
    rounds, rows, _ = kv.shape
    first = pl.multiple_of((1 - meta[1]) * rows, rows)
    for place, out in enumerate((lo_out, hi_out, far_out)):
        start = rounds - REACH if place == 1 else 0

        @pl.when(meta[3 + place] == 1)
        def _():
            out[...] = kv[start : start + out.shape[0]]

        @pl.when(meta[3 + place] == 0)
        def _():
            for r, block in enumerate(blocks):
                tile = lax.rem(meta[2] + r, rounds) - start

                @pl.when((tile >= 0) & (tile < out.shape[0]))
                def _():
                    out[tile] = block[pl.ds(first, rows)]


def payloads(kv_shape):
    edge = struct((REACH,) + kv_shape[1:])
    return [edge, edge, struct(kv_shape)]


def choose_alone(meta, kv, blocks):
    return pl.pallas_call(
        choose_kernel,
        in_specs=[SCALARS] + [ON_CHIP] * (1 + len(blocks)),
        out_specs=[ON_CHIP] * 3,
        out_shape=payloads(kv.shape),
        compiler_params=params(8),
        name="choose",
    )(meta, kv, *blocks)


def project_kernel(meta, *refs, with_stale):
    blocks = refs[:7]
    shift, scale, gain, w_own, w_other = refs[7:12]
    refs = refs[12:]
    if with_stale:
        stale, x_out, q_out, kv_out, *outs = refs[:-4]
    else:
        x_out, q_out, kv_out = refs[:-4]
    xs, modded, weights, sems = refs[-4:]
    rows, cols = x_out.shape
    tiles, rows_tile, kv_cols = kv_out.shape
    heads_cols = kv_cols // 2
    parts = shift.shape[0]
    width = cols * parts
    features = [lax.rem(meta[0] + j, parts) for j in range(parts)]

    def fetch(j, source):
        first = pl.multiple_of(features[j] * cols, cols)
        return pltpu.make_async_copy(
            source.at[:, pl.ds(first, cols)],
            weights.at[:, j * cols : (j + 1) * cols],
            sems.at[j],
        )

    for chosen, source in enumerate((w_other, w_own)):

        @pl.when(meta[1] == chosen)
        def _():
            for j in range(parts):
                fetch(j, source).start()

    own, next_a, next_b, far_a, far_b, prev_a, prev_b = blocks
    for r in range(tiles):
        tile = lax.rem(meta[2] + r, tiles)
        place = pl.ds(pl.multiple_of(tile * rows_tile, rows_tile), rows_tile)
        here = slice(r * rows_tile, (r + 1) * rows_tile)
        late = r >= tiles // 2
        there = slice((r % (tiles // 2)) * rows_tile, (r % (tiles // 2) + 1) * rows_tile)
        xs[0, place] = own[here]
        xs[1, place] = (next_b if late else next_a)[there]
        xs[2, place] = (far_b if late else far_a)[there]
        xs[3, place] = (prev_b if late else prev_a)[there]
    x_out[...] = xs[0]
    total = jnp.zeros((rows, 1), jnp.float32)
    for j in range(parts):
        total += jnp.sum(xs[j].astype(jnp.float32), axis=-1, keepdims=True)
    mean = total / width
    square = jnp.zeros((rows, 1), jnp.float32)
    for j in range(parts):
        centred = xs[j].astype(jnp.float32) - mean
        square += jnp.sum(centred * centred, axis=-1, keepdims=True)
    spread = lax.rsqrt(square / width + EPS)
    for j in range(parts):
        normed = (xs[j].astype(jnp.float32) - mean) * spread
        modded[:, j * cols : (j + 1) * cols] = (
            normed * (1.0 + scale[features[j]]) + shift[features[j]]
        ).astype(jnp.bfloat16)
    for j in range(parts):
        fetch(j, w_own).wait()

    for part in (1, 2, 0):
        product = jnp.dot(modded[...], weights[part], preferred_element_type=jnp.float32)
        if part == 2:
            kv_out[:, :, heads_cols:] = product.astype(jnp.bfloat16).reshape(
                tiles, rows_tile, heads_cols
            )
            continue
        for head in range(heads_cols // HEAD_DIM):
            cut = slice(head * HEAD_DIM, (head + 1) * HEAD_DIM)
            vec = product[:, cut]
            mean_sq = jnp.mean(vec * vec, axis=-1, keepdims=True)
            vec = vec * lax.rsqrt(mean_sq + EPS) * gain[part : part + 1]
            vec = vec.astype(jnp.bfloat16).reshape(tiles, rows_tile, HEAD_DIM)
            if part == 0:
                q_out[:, :, cut] = vec
            else:
                kv_out[:, :, cut] = vec
    if with_stale:
        choose(meta, kv_out, stale, outs)


def project(meta, blocks, shift, scale, gain, w_own, w_other, stale, kv_shape):
    rows, cols = blocks[0].shape
    tiles, rows_tile, kv_cols = kv_shape
    heads_cols = kv_cols // 2
    parts = shift.shape[0]
    shapes = [struct((rows, cols)), struct((tiles, rows_tile, heads_cols)), struct(kv_shape)]
    extra = []
    if stale is not None:
        shapes += payloads(kv_shape)
        extra = [stale]

    def kernel(*refs):
        project_kernel(*refs, with_stale=stale is not None)

    return pl.pallas_call(
        kernel,
        in_specs=[SCALARS]
        + [ON_CHIP] * (len(blocks) + 3)
        + [pl.BlockSpec(memory_space=pltpu.HBM)] * 2
        + [ON_CHIP] * len(extra),
        out_specs=[ON_CHIP] * len(shapes),
        out_shape=shapes,
        scratch_shapes=[
            pltpu.VMEM((parts, rows, cols), jnp.bfloat16),
            pltpu.VMEM((rows, parts * cols), jnp.bfloat16),
            pltpu.VMEM((3, parts * cols, heads_cols), jnp.bfloat16),
            pltpu.SemaphoreType.DMA((parts,)),
        ],
        compiler_params=params(46),
        name="project",
    )(meta, *blocks, shift, scale, gain, w_own, w_other, *extra)


def soften(queries, keys, values, times, floor):
    scores = lax.dot_general(
        queries, keys, (((1,), (1,)), ((), ())), preferred_element_type=jnp.float32
    )
    scores = jnp.where(times > 0.0, scores * HEAD_DIM ** (-0.5), -1e30)
    peak = jnp.max(scores, axis=-1, keepdims=True)
    if floor is not None:
        peak = jnp.maximum(peak, floor)
    weights = jnp.exp(scores - peak) * times
    total = jnp.sum(weights, axis=-1, keepdims=True)
    summed = jnp.dot(weights.astype(jnp.bfloat16), values, preferred_element_type=jnp.float32)
    return peak, total, summed


def attend_near_kernel(q_own, q_other, below, own, above, multiple, out, window):
    tiles, rows, heads_cols = q_own.shape
    window[: REACH * rows] = below[...].reshape(REACH * rows, 2 * heads_cols)
    window[REACH * rows : (REACH + tiles) * rows] = own[...].reshape(tiles * rows, 2 * heads_cols)
    window[(REACH + tiles) * rows :] = above[...].reshape(REACH * rows, 2 * heads_cols)
    lane = lax.broadcasted_iota(jnp.int32, (2 * rows, HEAD_DIM), 1)
    for tile in range(tiles):
        times = multiple[tile]
        span = slice(tile * rows, tile * rows + times.shape[-1])
        extra = jnp.zeros((2 * rows, HEAD_DIM), jnp.float32)
        for head in range(heads_cols // HEAD_DIM):
            first = head * HEAD_DIM
            cut = slice(first, first + HEAD_DIM)
            queries = jnp.concatenate([q_own[tile, :, cut], q_other[tile, :, cut]], axis=0)
            peak, total, summed = soften(
                queries,
                window[span, cut],
                window[span, heads_cols + first : heads_cols + first + HEAD_DIM],
                times,
                None,
            )
            out[tile, :, cut] = summed
            extra = jnp.where(lane == head, peak, extra)
            extra = jnp.where(lane == 64 + head, total, extra)
        out[tile, :, heads_cols:] = extra


def attend_near(q_own, q_other, below, own, above, multiple):
    tiles, rows, heads_cols = q_own.shape
    return pl.pallas_call(
        attend_near_kernel,
        in_specs=[ON_CHIP] * 6,
        out_specs=ON_CHIP,
        out_shape=struct((tiles, 2 * rows, heads_cols + HEAD_DIM), jnp.float32),
        scratch_shapes=[pltpu.VMEM(((tiles + 2 * REACH) * rows, 2 * heads_cols), jnp.bfloat16)],
        compiler_params=params(8),
        name="attend_near",
    )(q_own, q_other, below, own, above, multiple)


def attend_far_kernel(q_own, q_other, far, multiple, before, out_own, out_other):
    tiles, rows, heads_cols = q_own.shape
    lane = lax.broadcasted_iota(jnp.int32, (2 * rows, HEAD_DIM), 1)
    for tile in range(tiles):
        extra = jnp.zeros((2 * rows, HEAD_DIM), jnp.float32)
        for head in range(heads_cols // HEAD_DIM):
            first = head * HEAD_DIM
            cut = slice(first, first + HEAD_DIM)
            queries = jnp.concatenate([q_own[tile, :, cut], q_other[tile, :, cut]], axis=0)
            peak_before = before[tile, :, heads_cols + head : heads_cols + head + 1]
            total_before = before[tile, :, heads_cols + 64 + head : heads_cols + 65 + head]
            peak, total, summed = soften(
                queries,
                far[tile, :, cut],
                far[tile, :, heads_cols + first : heads_cols + first + HEAD_DIM],
                multiple[tile],
                peak_before,
            )
            shrink = jnp.exp(peak_before - peak)
            total += total_before * shrink
            summed += before[tile, :, cut] * shrink
            out_own[tile, :, cut] = summed[:rows]
            out_other[tile, :, cut] = summed[rows:]
            extra = jnp.where(lane == head, peak, extra)
            extra = jnp.where(lane == 64 + head, total, extra)
        out_own[tile, :, heads_cols:] = extra[:rows]
        out_other[tile, :, heads_cols:] = extra[rows:]


def attend_far(q_own, q_other, far, multiple, before):
    tiles, rows, heads_cols = q_own.shape
    return pl.pallas_call(
        attend_far_kernel,
        in_specs=[ON_CHIP] * 5,
        out_specs=[ON_CHIP] * 2,
        out_shape=[struct((tiles, rows, heads_cols + HEAD_DIM), jnp.float32)] * 2,
        compiler_params=params(8),
        name="attend_far",
    )(q_own, q_other, far, multiple, before)


def merge_kernel(part_a, part_b, att):
    tiles, rows, _ = part_a.shape
    heads_cols = att.shape[-1]
    for tile in range(tiles):
        extra_a = part_a[tile, :, heads_cols:]
        extra_b = part_b[tile, :, heads_cols:]
        for head in range(heads_cols // HEAD_DIM):
            cut = slice(head * HEAD_DIM, (head + 1) * HEAD_DIM)
            peak_a, total_a = extra_a[:, head : head + 1], extra_a[:, 64 + head : 65 + head]
            peak_b, total_b = extra_b[:, head : head + 1], extra_b[:, 64 + head : 65 + head]
            peak = jnp.maximum(peak_a, peak_b)
            grow_a, grow_b = jnp.exp(peak_a - peak), jnp.exp(peak_b - peak)
            total = total_a * grow_a + total_b * grow_b
            summed = part_a[tile, :, cut] * grow_a + part_b[tile, :, cut] * grow_b
            att[tile * rows : (tile + 1) * rows, cut] = (summed / total).astype(jnp.bfloat16)


def merge(part_a, part_b):
    tiles, rows, cols = part_a.shape
    return pl.pallas_call(
        merge_kernel,
        in_specs=[ON_CHIP] * 2,
        out_specs=ON_CHIP,
        out_shape=struct((tiles * rows, cols - HEAD_DIM)),
        compiler_params=params(8),
        name="merge",
    )(part_a, part_b)


def output_kernel(meta, att0, att1, att2, att3, wo_own, wo_other, hidden, gate, out):
    def finish(weight):
        product = jnp.zeros(out.shape, jnp.float32)
        for place, att in enumerate((att0, att1, att2, att3)):
            product += jnp.dot(att[...], weight[place], preferred_element_type=jnp.float32)
        out[...] = (hidden[...].astype(jnp.float32) + gate[...] * product).astype(out.dtype)

    @pl.when(meta[1] == 1)
    def _():
        finish(wo_own)

    @pl.when(meta[1] == 0)
    def _():
        finish(wo_other)


def output(meta, atts, wo_own, wo_other, hidden, gate):
    return pl.pallas_call(
        output_kernel,
        in_specs=[SCALARS] + [ON_CHIP] * 8,
        out_specs=ON_CHIP,
        out_shape=struct(hidden.shape),
        compiler_params=params(8),
        name="output",
    )(meta, *atts, wo_own, wo_other, hidden, gate)


def count_tiles(table, counts, chip, per_chip, repeat):
    tiles, slots = table.shape
    table = lax.dynamic_slice_in_dim(table, chip * per_chip, per_chip, 0)
    counts = lax.dynamic_slice_in_dim(counts, chip * per_chip, per_chip, 0)
    query_tiles = jnp.arange(per_chip, dtype=jnp.int32) + chip * per_chip
    across = tiles // 2 + (tiles // per_chip) // 2
    distances = list(range(-REACH, REACH + 1)) + [across]
    reach = jnp.repeat(jnp.array([d % tiles for d in distances], jnp.int32), repeat)
    relative = (table - query_tiles[:, None]) % tiles
    live = jnp.arange(slots, dtype=jnp.int32)[None] < counts[:, None]
    hits = (relative[:, :, None] == reach[None, None]) & live[:, :, None]
    return jnp.sum(hits.astype(jnp.float32), axis=1)[:, None]


def gather_features(hidden):
    half = hidden.shape[0] // 2
    halves = (hidden[:half], hidden[half:])
    prev_a = shifted(halves[0], "tp", 1)
    next_b = shifted(halves[1], "tp", -1)
    prev_b = shifted(halves[1], "tp", 1)
    next_a = shifted(halves[0], "tp", -1)
    prev_a, next_b = lax.optimization_barrier((prev_a, next_b))
    far_a = shifted(prev_a, "tp", 1)
    far_b = shifted(next_b, "tp", -1)
    return hidden, next_a, next_b, far_a, far_b, prev_a, prev_b


def local(
    latents, w_qkv, w_out, modulation, qk_gain, stale_cache, kv_tiles, tile_counts, patch_order
):
    core = lax.axis_index("segment")
    seq_size = lax.axis_size("seq")
    chip = lax.axis_index("seq")
    tp_size = lax.axis_size("tp")
    tp_pos = lax.axis_index("tp")
    patches, patch_rows, part_cols = latents.shape
    rows_core = patch_rows // 2
    rows = patches * rows_core
    share = seq_size // patches
    w_own = jnp.transpose(w_qkv[0], (1, 0, 2))
    heads_cols, width = w_out.shape[1:]
    head_dim = qk_gain.shape[-1]

    place = jnp.stack([core, lax.rem(chip, patches), chip // share]).astype(jnp.int32)
    x_rounds = to_work(deal_latents(place, latents))
    w_other = shifted(w_own, "segment", 1)
    small_own = jnp.concatenate([modulation[0].reshape(-1), qk_gain[0].reshape(-1)])
    small_other = shifted(small_own, "segment", 1)
    hidden = jnp.concatenate(x_rounds, axis=0)
    blocks = gather_features(hidden)
    stale_own, stale_send = halve_stale(place, stale_cache[0])
    stale_other = shifted(stale_send, "segment", 1)
    stale_rounds = list(deal_stale(place, stale_own, stale_other))
    stale_rounds[:4], w_out = after((stale_rounds[:4], w_out), blocks[2], blocks[5])
    stale_rounds[4:] = after(stale_rounds[4:], blocks)
    stale_rounds = to_work(stale_rounds)

    rows_chip = heads_cols // seq_size
    slab = lax.dynamic_slice_in_dim(w_out[0], chip * rows_chip, rows_chip, 0)
    pieces = [
        lax.dynamic_slice_in_dim(slab, lax.rem(tp_pos + j, tp_size) * part_cols, part_cols, 1)
        for j in range(tp_size)
    ]
    pieces[1:] = [shifted(pieces[j], "tp", j) for j in range(1, tp_size)]
    wo_own = lax.all_gather(jnp.stack(pieces), "seq", axis=1, tiled=True)

    turns = jnp.arange(patches, dtype=jnp.int32)
    asked = jnp.stack([chip, chip - 1, chip + 1, chip - seq_size // 2 - 1]) % seq_size // share
    ranks = jnp.sum(jnp.where(patch_order[None] == asked[:, None], turns[None], 0), axis=-1)
    fresh = (ranks[0] <= ranks[1:]).astype(jnp.int32)

    for section in range(2):
        is_own = core == section
        start = chip // share if section == 0 else jnp.zeros_like(chip)
        meta = jnp.concatenate(
            [jnp.stack([tp_pos, is_own.astype(tp_pos.dtype), start]).astype(jnp.int32), fresh]
        )
        small = jnp.where(is_own, small_own, small_other)
        modul = small[: 3 * width].reshape(3, tp_size, 1, part_cols)
        gain = small[3 * width :].reshape(2, head_dim)
        gate = lax.dynamic_index_in_dim(modul[2], tp_pos, 0, keepdims=False)
        if section > 0:
            blocks = gather_features(hidden)
            early[:4] = after(early[:4], blocks[2], blocks[5])
            early[4:] = after(early[4:], blocks)
            early = to_home(early)
            blocks, early[:4] = lax.optimization_barrier((blocks, early[:4]))
        hidden, q_own, kv, *going = project(
            meta,
            blocks,
            modul[0],
            modul[1],
            gain,
            w_own,
            w_other,
            stale if section > 0 else None,
            stale_own.shape,
        )
        if section == 0:
            going = choose_alone(meta, kv, stale_rounds)
            stale = sort_stale(place, after(stale_rounds, going))
        to_below, to_above, to_far = going
        above = shifted(to_below, "seq", -1)
        below = shifted(to_above, "seq", 1)
        q_other = shifted(q_own, "segment", 1)
        far = shifted(to_far, "seq", -(seq_size // 2) - 1)
        if section == 0:
            kv_tiles, tile_counts = after((kv_tiles, tile_counts), q_own)
            multiple_own = count_tiles(kv_tiles[0], tile_counts[0], chip, patches, rows_core)
            multiple_other = shifted(multiple_own, "segment", 1)
        else:
            above, early = lax.optimization_barrier((above, early))
        multiple = jnp.where(is_own, multiple_own, multiple_other)
        cut = multiple.shape[-1] - rows_core
        before = attend_near(q_own, q_other, below, kv, above, multiple[..., :cut])
        part_own, part_other = attend_far(q_own, q_other, far, multiple[..., cut:], before)
        if section == 0:
            wo_other = shifted(after(wo_own, part_other), "segment", 1)
        part_back = shifted(part_other, "segment", 1)
        att = merge(part_own, part_back)
        atts = [att] + [shifted(att, "tp", j) for j in (1, 2, 3)]
        hidden = output(meta, atts, wo_own, wo_other, hidden, gate)

        features = hidden.reshape(patches, rows_core, part_cols)
        pair = (kv, features) if section == 0 else (features, kv)
        got = shifted(jnp.where(core == 0, pair[1], pair[0]), "segment", 1)
        dealt = list(deal_results(place, *pair, got))
        if section == 0:
            early = dealt
        else:
            late = to_home(dealt)

    handed, new_cache = collect(place, early, late)
    return (handed[None], new_cache[None])


def solution(mesh):
    in_specs = (
        P(None, "seq", "tp"),
        P("segment", None, None, "tp"),
        P("segment", "tp", None),
        P("segment", None, None),
        P("segment", None, None),
        P("segment", None, None, "seq", "tp"),
        P("segment", None, None),
        P("segment", None),
        P(),
    )
    out_specs = (P("segment", None, "seq", "tp"), P("segment", None, None, "seq", "tp"))
    return jax.shard_map(local, mesh=mesh, in_specs=in_specs, out_specs=out_specs, check_vma=False)
```

```python
import jax
import jax.numpy as jnp
from jax import lax
from jax.experimental import pallas as pl
from jax.experimental.pallas import tpu as pltpu
from jax.sharding import PartitionSpec as P

EPS = 1e-06
HEAD_DIM = 128
REACH = 3
MIB = 1024 * 1024
ON_CHIP = pl.BlockSpec(memory_space=pltpu.VMEM)
SCALARS = pl.BlockSpec(memory_space=pltpu.SMEM)


def shifted(block, axis, distance):
    devices = range(lax.axis_size(axis))
    route = [((i - distance) % len(devices), i) for i in devices]
    return lax.ppermute(block, axis, route)


def after(values, *gates):
    return lax.optimization_barrier((values, gates))[0]


def params(mib):
    return pltpu.CompilerParams(vmem_limit_bytes=mib * MIB)


def struct(shape, dtype=jnp.bfloat16):
    return jax.ShapeDtypeStruct(shape, dtype)


def exchanged(tiles):
    group = tiles.shape[0]
    groups = [list(range(i, i + group)) for i in range(0, lax.axis_size("seq"), group)]
    return lax.all_to_all(tiles, "seq", 0, 0, axis_index_groups=groups)


def along_ring(block, distance, per_chip):
    size = lax.axis_size("seq")
    share = size // per_chip
    place = [per_chip * (i % share) + i // share for i in range(size)]
    route = [(place[(i + distance) % size], place[i]) for i in range(size)]
    return lax.ppermute(block, "seq", route)


def collect_kernel(core, early, late, handed, cache):
    cols = cache.shape[-1]

    def collect(features, keys):
        handed[...] = features[...]
        cache[0] = keys[:, :, :cols]
        cache[1] = keys[:, :, cols:]

    @pl.when(core[0] == 0)
    def _():
        collect(late, early)

    @pl.when(core[0] == 1)
    def _():
        collect(early, late)


def collect(core, early, late):
    patches, rows, cols = early.shape
    return pl.pallas_call(
        collect_kernel,
        in_specs=[SCALARS] + [ON_CHIP] * 2,
        out_specs=[ON_CHIP] * 2,
        out_shape=[struct(early.shape), struct((2, patches, rows, cols // 2))],
        compiler_params=params(8),
        name="collect",
    )(core, early, late)


def choose(meta, kv, stale, outs):
    tiles = kv.shape[0]
    for place, out in enumerate(outs):
        first = tiles - REACH if place == 1 else 0
        cut = slice(first, first + out.shape[0])

        @pl.when(meta[2 + place] == 1)
        def _():
            out[...] = kv[cut]

        @pl.when(meta[2 + place] == 0)
        def _():
            out[...] = stale[cut]


def choose_kernel(meta, kv, stale, lo_out, hi_out, far_out):
    choose(meta, kv, stale, (lo_out, hi_out, far_out))


def payloads(kv_shape):
    edge = struct((REACH,) + kv_shape[1:])
    return [edge, edge, struct(kv_shape)]


def choose_alone(meta, kv, stale):
    return pl.pallas_call(
        choose_kernel,
        in_specs=[SCALARS] + [ON_CHIP] * 2,
        out_specs=[ON_CHIP] * 3,
        out_shape=payloads(kv.shape),
        compiler_params=params(8),
        name="choose",
    )(meta, kv, stale)


def project_kernel(meta, *refs, with_stale):
    blocks = refs[:4]
    shift, scale, gain, w_own, w_other = refs[4:9]
    refs = refs[9:]
    if with_stale:
        stale, q_out, kv_out, *outs = refs[:-3]
    else:
        q_out, kv_out = refs[:-3]
    modded, weights, sems = refs[-3:]
    rows, cols = blocks[0].shape
    tiles, rows_tile, kv_cols = kv_out.shape
    heads_cols = kv_cols // 2
    parts = shift.shape[0]
    width = cols * parts
    features = [lax.rem(meta[0] + j, parts) for j in range(parts)]

    def fetch(j, source):
        first = pl.multiple_of(features[j] * cols, cols)
        return pltpu.make_async_copy(
            source.at[:, pl.ds(first, cols)],
            weights.at[:, j * cols : (j + 1) * cols],
            sems.at[j],
        )

    for chosen, source in enumerate((w_other, w_own)):

        @pl.when(meta[1] == chosen)
        def _():
            for j in range(parts):
                fetch(j, source).start()

    total = jnp.zeros((rows, 1), jnp.float32)
    for j in range(parts):
        total += jnp.sum(blocks[j][...].astype(jnp.float32), axis=-1, keepdims=True)
    mean = total / width
    square = jnp.zeros((rows, 1), jnp.float32)
    for j in range(parts):
        centred = blocks[j][...].astype(jnp.float32) - mean
        square += jnp.sum(centred * centred, axis=-1, keepdims=True)
    spread = lax.rsqrt(square / width + EPS)
    for j in range(parts):
        normed = (blocks[j][...].astype(jnp.float32) - mean) * spread
        modded[:, j * cols : (j + 1) * cols] = (
            normed * (1.0 + scale[features[j]]) + shift[features[j]]
        ).astype(jnp.bfloat16)
    for j in range(parts):
        fetch(j, w_own).wait()

    for part in (1, 2, 0):
        product = jnp.dot(modded[...], weights[part], preferred_element_type=jnp.float32)
        if part == 2:
            kv_out[:, :, heads_cols:] = product.astype(jnp.bfloat16).reshape(
                tiles, rows_tile, heads_cols
            )
            continue
        for head in range(heads_cols // HEAD_DIM):
            cut = slice(head * HEAD_DIM, (head + 1) * HEAD_DIM)
            vec = product[:, cut]
            mean_sq = jnp.mean(vec * vec, axis=-1, keepdims=True)
            vec = vec * lax.rsqrt(mean_sq + EPS) * gain[part : part + 1]
            vec = vec.astype(jnp.bfloat16).reshape(tiles, rows_tile, HEAD_DIM)
            if part == 0:
                q_out[:, :, cut] = vec
            else:
                kv_out[:, :, cut] = vec
    if with_stale:
        choose(meta, kv_out, stale, outs)


def project(meta, blocks, shift, scale, gain, w_own, w_other, stale, kv_shape):
    rows, cols = blocks[0].shape
    tiles, rows_tile, kv_cols = kv_shape
    heads_cols = kv_cols // 2
    parts = shift.shape[0]
    shapes = [struct((tiles, rows_tile, heads_cols)), struct(kv_shape)]
    extra = []
    if stale is not None:
        shapes += payloads(kv_shape)
        extra = [stale]

    def kernel(*refs):
        project_kernel(*refs, with_stale=stale is not None)

    return pl.pallas_call(
        kernel,
        in_specs=[SCALARS]
        + [ON_CHIP] * (len(blocks) + 3)
        + [pl.BlockSpec(memory_space=pltpu.HBM)] * 2
        + [ON_CHIP] * len(extra),
        out_specs=[ON_CHIP] * len(shapes),
        out_shape=shapes,
        scratch_shapes=[
            pltpu.VMEM((rows, parts * cols), jnp.bfloat16),
            pltpu.VMEM((3, parts * cols, heads_cols), jnp.bfloat16),
            pltpu.SemaphoreType.DMA((parts,)),
        ],
        compiler_params=params(46),
        name="project",
    )(meta, *blocks, shift, scale, gain, w_own, w_other, *extra)


def soften(queries, keys, values, times, floor):
    scores = lax.dot_general(
        queries, keys, (((1,), (1,)), ((), ())), preferred_element_type=jnp.float32
    )
    scores = jnp.where(times > 0.0, scores * HEAD_DIM ** (-0.5), -1e30)
    peak = jnp.max(scores, axis=-1, keepdims=True)
    if floor is not None:
        peak = jnp.maximum(peak, floor)
    weights = jnp.exp(scores - peak) * times
    total = jnp.sum(weights, axis=-1, keepdims=True)
    summed = jnp.dot(weights.astype(jnp.bfloat16), values, preferred_element_type=jnp.float32)
    return peak, total, summed


def attend_near_kernel(q_own, q_other, below, own, above, multiple, out, window):
    tiles, rows, heads_cols = q_own.shape
    window[: REACH * rows] = below[...].reshape(REACH * rows, 2 * heads_cols)
    window[REACH * rows : (REACH + tiles) * rows] = own[...].reshape(tiles * rows, 2 * heads_cols)
    window[(REACH + tiles) * rows :] = above[...].reshape(REACH * rows, 2 * heads_cols)
    lane = lax.broadcasted_iota(jnp.int32, (2 * rows, HEAD_DIM), 1)
    for tile in range(tiles):
        times = multiple[tile]
        span = slice(tile * rows, tile * rows + times.shape[-1])
        extra = jnp.zeros((2 * rows, HEAD_DIM), jnp.float32)
        for head in range(heads_cols // HEAD_DIM):
            first = head * HEAD_DIM
            cut = slice(first, first + HEAD_DIM)
            queries = jnp.concatenate([q_own[tile, :, cut], q_other[tile, :, cut]], axis=0)
            peak, total, summed = soften(
                queries,
                window[span, cut],
                window[span, heads_cols + first : heads_cols + first + HEAD_DIM],
                times,
                None,
            )
            out[tile, :, cut] = summed
            extra = jnp.where(lane == head, peak, extra)
            extra = jnp.where(lane == 64 + head, total, extra)
        out[tile, :, heads_cols:] = extra


def attend_near(q_own, q_other, below, own, above, multiple):
    tiles, rows, heads_cols = q_own.shape
    return pl.pallas_call(
        attend_near_kernel,
        in_specs=[ON_CHIP] * 6,
        out_specs=ON_CHIP,
        out_shape=struct((tiles, 2 * rows, heads_cols + HEAD_DIM), jnp.float32),
        scratch_shapes=[pltpu.VMEM(((tiles + 2 * REACH) * rows, 2 * heads_cols), jnp.bfloat16)],
        compiler_params=params(8),
        name="attend_near",
    )(q_own, q_other, below, own, above, multiple)


def attend_far_kernel(q_own, q_other, far, multiple, before, out_own, out_other):
    tiles, rows, heads_cols = q_own.shape
    lane = lax.broadcasted_iota(jnp.int32, (2 * rows, HEAD_DIM), 1)
    for tile in range(tiles):
        extra = jnp.zeros((2 * rows, HEAD_DIM), jnp.float32)
        for head in range(heads_cols // HEAD_DIM):
            first = head * HEAD_DIM
            cut = slice(first, first + HEAD_DIM)
            queries = jnp.concatenate([q_own[tile, :, cut], q_other[tile, :, cut]], axis=0)
            peak_before = before[tile, :, heads_cols + head : heads_cols + head + 1]
            total_before = before[tile, :, heads_cols + 64 + head : heads_cols + 65 + head]
            peak, total, summed = soften(
                queries,
                far[tile, :, cut],
                far[tile, :, heads_cols + first : heads_cols + first + HEAD_DIM],
                multiple[tile],
                peak_before,
            )
            shrink = jnp.exp(peak_before - peak)
            total += total_before * shrink
            summed += before[tile, :, cut] * shrink
            out_own[tile, :, cut] = summed[:rows]
            out_other[tile, :, cut] = summed[rows:]
            extra = jnp.where(lane == head, peak, extra)
            extra = jnp.where(lane == 64 + head, total, extra)
        out_own[tile, :, heads_cols:] = extra[:rows]
        out_other[tile, :, heads_cols:] = extra[rows:]


def attend_far(q_own, q_other, far, multiple, before):
    tiles, rows, heads_cols = q_own.shape
    return pl.pallas_call(
        attend_far_kernel,
        in_specs=[ON_CHIP] * 5,
        out_specs=[ON_CHIP] * 2,
        out_shape=[struct((tiles, rows, heads_cols + HEAD_DIM), jnp.float32)] * 2,
        compiler_params=params(8),
        name="attend_far",
    )(q_own, q_other, far, multiple, before)


def merge_kernel(part_a, part_b, att):
    tiles, rows, _ = part_a.shape
    heads_cols = att.shape[-1]
    for tile in range(tiles):
        extra_a = part_a[tile, :, heads_cols:]
        extra_b = part_b[tile, :, heads_cols:]
        for head in range(heads_cols // HEAD_DIM):
            cut = slice(head * HEAD_DIM, (head + 1) * HEAD_DIM)
            peak_a, total_a = extra_a[:, head : head + 1], extra_a[:, 64 + head : 65 + head]
            peak_b, total_b = extra_b[:, head : head + 1], extra_b[:, 64 + head : 65 + head]
            peak = jnp.maximum(peak_a, peak_b)
            grow_a, grow_b = jnp.exp(peak_a - peak), jnp.exp(peak_b - peak)
            total = total_a * grow_a + total_b * grow_b
            summed = part_a[tile, :, cut] * grow_a + part_b[tile, :, cut] * grow_b
            att[tile * rows : (tile + 1) * rows, cut] = (summed / total).astype(jnp.bfloat16)


def merge(part_a, part_b):
    tiles, rows, cols = part_a.shape
    return pl.pallas_call(
        merge_kernel,
        in_specs=[ON_CHIP] * 2,
        out_specs=ON_CHIP,
        out_shape=struct((tiles * rows, cols - HEAD_DIM)),
        compiler_params=params(8),
        name="merge",
    )(part_a, part_b)


def output_kernel(meta, att0, att1, att2, att3, wo_own, wo_other, hidden, gate, out):
    def finish(weight):
        product = jnp.zeros(out.shape, jnp.float32)
        for place, att in enumerate((att0, att1, att2, att3)):
            product += jnp.dot(att[...], weight[place], preferred_element_type=jnp.float32)
        out[...] = (hidden[...].astype(jnp.float32) + gate[...] * product).astype(out.dtype)

    @pl.when(meta[1] == 1)
    def _():
        finish(wo_own)

    @pl.when(meta[1] == 0)
    def _():
        finish(wo_other)


def output(meta, atts, wo_own, wo_other, hidden, gate):
    return pl.pallas_call(
        output_kernel,
        in_specs=[SCALARS] + [ON_CHIP] * 8,
        out_specs=ON_CHIP,
        out_shape=struct(hidden.shape),
        compiler_params=params(8),
        name="output",
    )(meta, *atts, wo_own, wo_other, hidden, gate)


def count_tiles(table, counts, chip, per_chip, repeat):
    tiles, slots = table.shape
    table = lax.dynamic_slice_in_dim(table, chip * per_chip, per_chip, 0)
    counts = lax.dynamic_slice_in_dim(counts, chip * per_chip, per_chip, 0)
    query_tiles = jnp.arange(per_chip, dtype=jnp.int32) + chip * per_chip
    across = tiles // 2 + (tiles // per_chip) // 2
    distances = list(range(-REACH, REACH + 1)) + [across]
    reach = jnp.repeat(jnp.array([d % tiles for d in distances], jnp.int32), repeat)
    relative = (table - query_tiles[:, None]) % tiles
    live = jnp.arange(slots, dtype=jnp.int32)[None] < counts[:, None]
    hits = (relative[:, :, None] == reach[None, None]) & live[:, :, None]
    return jnp.sum(hits.astype(jnp.float32), axis=1)[:, None]


def gather_features(hidden):
    across = shifted(hidden, "tp", 2)
    return hidden, shifted(hidden, "tp", -1), across, shifted(hidden, "tp", 1)


def local(
    latents, w_qkv, w_out, modulation, qk_gain, stale_cache, kv_tiles, tile_counts, patch_order
):
    core = lax.axis_index("segment")
    seq_size = lax.axis_size("seq")
    seq_pos = lax.axis_index("seq")
    tp_size = lax.axis_size("tp")
    tp_pos = lax.axis_index("tp")
    patches, patch_rows, part_cols = latents.shape
    rows_core = patch_rows // 2
    rows = patches * rows_core
    share = seq_size // patches
    chip = share * lax.rem(seq_pos, patches) + seq_pos // patches
    w_own = jnp.transpose(w_qkv[0], (1, 0, 2))
    heads_cols, width = w_out.shape[1:]
    head_dim = qk_gain.shape[-1]

    mine = lax.dynamic_slice_in_dim(latents, core * rows_core, rows_core, 1)
    hidden = exchanged(mine).reshape(rows, part_cols)
    w_other = shifted(w_own, "segment", 1)
    small_own = jnp.concatenate([modulation[0].reshape(-1), qk_gain[0].reshape(-1)])
    small_other = shifted(small_own, "segment", 1)
    stale, w_out = after((stale_cache[0], w_out), hidden)
    stale = exchanged(jnp.concatenate([stale[0], stale[1]], axis=-1))
    stale_own = lax.dynamic_slice_in_dim(stale, core * rows_core, rows_core, 1)
    stale_other = shifted(
        lax.dynamic_slice_in_dim(stale, (1 - core) * rows_core, rows_core, 1), "segment", 1
    )

    rows_chip = heads_cols // seq_size
    slab = lax.dynamic_slice_in_dim(w_out[0], seq_pos * rows_chip, rows_chip, 0)
    pieces = [
        lax.dynamic_slice_in_dim(slab, lax.rem(tp_pos + j, tp_size) * part_cols, part_cols, 1)
        for j in range(tp_size)
    ]
    pieces[1:] = [shifted(pieces[j], "tp", j) for j in range(1, tp_size)]
    wo_own = lax.all_gather(jnp.stack(pieces), "seq", axis=1, tiled=True)

    turns = jnp.arange(patches, dtype=jnp.int32)
    asked = jnp.stack([chip, chip - 1, chip + 1, chip - seq_size // 2 - 1]) % seq_size // share
    ranks = jnp.sum(jnp.where(patch_order[None] == asked[:, None], turns[None], 0), axis=-1)
    fresh = (ranks[0] <= ranks[1:]).astype(jnp.int32)

    for section in range(2):
        is_own = core == section
        meta = jnp.concatenate(
            [jnp.stack([tp_pos, is_own.astype(tp_pos.dtype)]).astype(jnp.int32), fresh]
        )
        small = jnp.where(is_own, small_own, small_other)
        modul = small[: 3 * width].reshape(3, tp_size, 1, part_cols)
        gain = small[3 * width :].reshape(2, head_dim)
        gate = lax.dynamic_index_in_dim(modul[2], tp_pos, 0, keepdims=False)
        stale = jnp.where(is_own, stale_own, stale_other)

        blocks = gather_features(hidden)
        if section > 0:
            early = exchanged(early)
            blocks, early = lax.optimization_barrier((blocks, early))
        q_own, kv, *going = project(
            meta,
            blocks,
            modul[0],
            modul[1],
            gain,
            w_own,
            w_other,
            stale if section > 0 else None,
            stale.shape,
        )
        if section == 0:
            going = choose_alone(meta, kv, stale)
        to_below, to_above, to_far = going
        far = along_ring(to_far, seq_size // 2 + 1, patches)
        above = along_ring(to_below, 1, patches)
        below = along_ring(to_above, -1, patches)
        q_other = shifted(q_own, "segment", 1)
        if section == 0:
            kv_tiles, tile_counts = after((kv_tiles, tile_counts), q_own)
            multiple_own = count_tiles(kv_tiles[0], tile_counts[0], chip, patches, rows_core)
            multiple_other = shifted(multiple_own, "segment", 1)
        multiple = jnp.where(is_own, multiple_own, multiple_other)
        cut = multiple.shape[-1] - rows_core
        before = attend_near(q_own, q_other, below, kv, above, multiple[..., :cut])
        part_own, part_other = attend_far(q_own, q_other, far, multiple[..., cut:], before)
        if section == 0:
            wo_other = shifted(after(wo_own, part_other), "segment", 1)
        part_back = shifted(part_other, "segment", 1)
        att = merge(part_own, part_back)
        atts = [att] + [shifted(att, "tp", j) for j in (1, 2, 3)]
        hidden = output(meta, atts, wo_own, wo_other, hidden, gate)

        features = hidden.reshape(patches, rows_core, part_cols)
        pair = (kv, features) if section == 0 else (features, kv)
        got = shifted(jnp.where(core == 0, pair[1], pair[0]), "segment", 1)
        own = jnp.where(core == 0, pair[0], pair[1])
        halves = [jnp.where(core == place, own, got) for place in range(2)]
        if section == 0:
            early = jnp.concatenate(halves, axis=1)
        else:
            late = exchanged(jnp.concatenate(halves, axis=1))

    handed, new_cache = collect(core.astype(jnp.int32)[None], early, late)
    return (handed[None], new_cache[None])


def solution(mesh):
    in_specs = (
        P(None, "seq", "tp"),
        P("segment", None, None, "tp"),
        P("segment", "tp", None),
        P("segment", None, None),
        P("segment", None, None),
        P("segment", None, None, "seq", "tp"),
        P("segment", None, None),
        P("segment", None),
        P(),
    )
    out_specs = (P("segment", None, "seq", "tp"), P("segment", None, None, "seq", "tp"))
    return jax.shard_map(local, mesh=mesh, in_specs=in_specs, out_specs=out_specs, check_vma=False)
```

```python
import jax
import jax.numpy as jnp
from jax import lax
from jax.experimental import pallas as pl
from jax.experimental.pallas import tpu as pltpu
from jax.sharding import PartitionSpec as P

EPS = 1e-06
HEAD_DIM = 128
REACH = 3
MIB = 1024 * 1024
ON_CHIP = pl.BlockSpec(memory_space=pltpu.VMEM)
SCALARS = pl.BlockSpec(memory_space=pltpu.SMEM)
ANYWHERE = pl.BlockSpec(memory_space=pl.ANY)


def shifted(block, axis, distance):
    devices = range(lax.axis_size(axis))
    route = [((i - distance) % len(devices), i) for i in devices]
    return lax.ppermute(block, axis, route)


def after(values, *gates):
    return lax.optimization_barrier((values, gates))[0]


def params(mib):
    return pltpu.CompilerParams(vmem_limit_bytes=mib * MIB)


def struct(shape, dtype=jnp.bfloat16):
    return jax.ShapeDtypeStruct(shape, dtype)


def exchanged(tiles):
    group = tiles.shape[0]
    groups = [list(range(i, i + group)) for i in range(0, lax.axis_size("seq"), group)]
    return lax.all_to_all(tiles, "seq", 0, 0, axis_index_groups=groups)


def along_ring(block, distance, per_chip):
    size = lax.axis_size("seq")
    share = size // per_chip
    place = [per_chip * (i % share) + i // share for i in range(size)]
    route = [(place[(i + distance) % size], place[i]) for i in range(size)]
    return lax.ppermute(block, "seq", route)


def collect_kernel(core, early, late, handed, cache):
    cols = cache.shape[-1]

    def collect(features, keys):
        handed[...] = features[...]
        cache[0] = keys[:, :, :cols]
        cache[1] = keys[:, :, cols:]

    @pl.when(core[0] == 0)
    def _():
        collect(late, early)

    @pl.when(core[0] == 1)
    def _():
        collect(early, late)


def collect(core, early, late):
    patches, rows, cols = early.shape
    return pl.pallas_call(
        collect_kernel,
        in_specs=[SCALARS] + [ON_CHIP] * 2,
        out_specs=[ON_CHIP] * 2,
        out_shape=[struct(early.shape), struct((2, patches, rows, cols // 2))],
        compiler_params=params(8),
        name="collect",
    )(core, early, late)


def choose(meta, kv, stale, outs):
    tiles, rows, _ = kv.shape
    old = pl.ds(pl.multiple_of((1 - meta[1]) * rows, rows), rows)
    for place, out in enumerate(outs):
        first = tiles - REACH if place == 1 else 0
        cut = slice(first, first + out.shape[0])

        @pl.when(meta[2 + place] == 1)
        def _():
            out[...] = kv[cut]

        @pl.when(meta[2 + place] == 0)
        def _():
            out[...] = stale[cut, old]


def choose_kernel(meta, kv, stale, lo_out, hi_out, far_out):
    choose(meta, kv, stale, (lo_out, hi_out, far_out))


def payloads(kv_shape):
    edge = struct((REACH,) + kv_shape[1:])
    return [edge, edge, struct(kv_shape)]


def choose_alone(meta, kv, stale):
    return pl.pallas_call(
        choose_kernel,
        in_specs=[SCALARS] + [ON_CHIP] * 2,
        out_specs=[ON_CHIP] * 3,
        out_shape=payloads(kv.shape),
        compiler_params=params(8),
        name="choose",
    )(meta, kv, stale)


def project_kernel(meta, *refs, with_stale):
    blocks = refs[:4]
    shift, scale, gain, w_own, w_other = refs[4:9]
    refs = refs[9:]
    if with_stale:
        stale, q_out, kv_out, *outs = refs[:-4]
    else:
        q_out, kv_out = refs[:-4]
    xs, modded, weights, sems = refs[-4:]
    _, rows, cols = xs.shape
    tiles, rows_tile, kv_cols = kv_out.shape
    heads_cols = kv_cols // 2
    parts = shift.shape[0]
    width = cols * parts
    features = [lax.rem(meta[0] + j, parts) for j in range(parts)]

    def fetch(j, source):
        first = pl.multiple_of(features[j] * cols, cols)
        return pltpu.make_async_copy(
            source.at[:, pl.ds(first, cols)],
            weights.at[:, j * cols : (j + 1) * cols],
            sems.at[j],
        )

    arriving = [
        pltpu.make_async_copy(blocks[j], xs.at[j], sems.at[parts + j]) for j in range(parts)
    ]
    for copy in arriving:
        copy.start()
    for chosen, source in enumerate((w_other, w_own)):

        @pl.when(meta[1] == chosen)
        def _():
            for j in range(parts):
                fetch(j, source).start()

    for copy in arriving:
        copy.wait()
    total = jnp.zeros((rows, 1), jnp.float32)
    for j in range(parts):
        total += jnp.sum(xs[j].astype(jnp.float32), axis=-1, keepdims=True)
    mean = total / width
    square = jnp.zeros((rows, 1), jnp.float32)
    for j in range(parts):
        centred = xs[j].astype(jnp.float32) - mean
        square += jnp.sum(centred * centred, axis=-1, keepdims=True)
    spread = lax.rsqrt(square / width + EPS)
    for j in range(parts):
        normed = (xs[j].astype(jnp.float32) - mean) * spread
        modded[:, j * cols : (j + 1) * cols] = (
            normed * (1.0 + scale[features[j]]) + shift[features[j]]
        ).astype(jnp.bfloat16)
    for j in range(parts):
        fetch(j, w_own).wait()

    for part in (1, 2, 0):
        product = jnp.dot(modded[...], weights[part], preferred_element_type=jnp.float32)
        if part == 2:
            kv_out[:, :, heads_cols:] = product.astype(jnp.bfloat16).reshape(
                tiles, rows_tile, heads_cols
            )
            continue
        for head in range(heads_cols // HEAD_DIM):
            cut = slice(head * HEAD_DIM, (head + 1) * HEAD_DIM)
            vec = product[:, cut]
            mean_sq = jnp.mean(vec * vec, axis=-1, keepdims=True)
            vec = vec * lax.rsqrt(mean_sq + EPS) * gain[part : part + 1]
            vec = vec.astype(jnp.bfloat16).reshape(tiles, rows_tile, HEAD_DIM)
            if part == 0:
                q_out[:, :, cut] = vec
            else:
                kv_out[:, :, cut] = vec
    if with_stale:
        choose(meta, kv_out, stale, outs)


def project(meta, blocks, shift, scale, gain, w_own, w_other, stale, kv_shape):
    rows, cols = blocks[0].shape
    tiles, rows_tile, kv_cols = kv_shape
    heads_cols = kv_cols // 2
    parts = shift.shape[0]
    shapes = [struct((tiles, rows_tile, heads_cols)), struct(kv_shape)]
    extra = []
    if stale is not None:
        shapes += payloads(kv_shape)
        extra = [stale]

    def kernel(*refs):
        project_kernel(*refs, with_stale=stale is not None)

    return pl.pallas_call(
        kernel,
        in_specs=[SCALARS]
        + [ANYWHERE] * len(blocks)
        + [ON_CHIP] * 3
        + [ANYWHERE] * 2
        + [ON_CHIP] * len(extra),
        out_specs=[ON_CHIP] * len(shapes),
        out_shape=shapes,
        scratch_shapes=[
            pltpu.VMEM((parts, rows, cols), jnp.bfloat16),
            pltpu.VMEM((rows, parts * cols), jnp.bfloat16),
            pltpu.VMEM((3, parts * cols, heads_cols), jnp.bfloat16),
            pltpu.SemaphoreType.DMA((2 * parts,)),
        ],
        compiler_params=params(16),
        name="project",
    )(meta, *blocks, shift, scale, gain, w_own, w_other, *extra)


def soften(queries, keys, values, times, floor):
    scores = lax.dot_general(
        queries, keys, (((1,), (1,)), ((), ())), preferred_element_type=jnp.float32
    )
    scores = jnp.where(times > 0.0, scores * HEAD_DIM ** (-0.5), -1e30)
    peak = jnp.max(scores, axis=-1, keepdims=True)
    if floor is not None:
        peak = jnp.maximum(peak, floor)
    weights = jnp.exp(scores - peak) * times
    total = jnp.sum(weights, axis=-1, keepdims=True)
    summed = jnp.dot(weights.astype(jnp.bfloat16), values, preferred_element_type=jnp.float32)
    return peak, total, summed


def attend_own_kernel(q_own, q_other, own, multiple, out):
    tiles, rows, heads_cols = q_own.shape
    lane = lax.broadcasted_iota(jnp.int32, (2 * rows, HEAD_DIM), 1)
    for tile in range(tiles):
        first, last = max(0, tile - REACH), min(tiles, tile + REACH + 1)
        count = (last - first) * rows
        extra = jnp.zeros((2 * rows, HEAD_DIM), jnp.float32)
        for head in range(heads_cols // HEAD_DIM):
            start = head * HEAD_DIM
            cut = slice(start, start + HEAD_DIM)
            second = slice(heads_cols + start, heads_cols + start + HEAD_DIM)
            queries = jnp.concatenate([q_own[tile, :, cut], q_other[tile, :, cut]], axis=0)
            peak, total, summed = soften(
                queries,
                own[first:last, :, cut].reshape(count, HEAD_DIM),
                own[first:last, :, second].reshape(count, HEAD_DIM),
                multiple[tile, :, :count],
                None,
            )
            out[tile, :, cut] = summed
            extra = jnp.where(lane == head, peak, extra)
            extra = jnp.where(lane == 64 + head, total, extra)
        out[tile, :, heads_cols:] = extra


def attend_own(q_own, q_other, own, multiple):
    tiles, rows, heads_cols = q_own.shape
    return pl.pallas_call(
        attend_own_kernel,
        in_specs=[ON_CHIP] * 4,
        out_specs=ON_CHIP,
        out_shape=struct((tiles, 2 * rows, heads_cols + HEAD_DIM), jnp.float32),
        compiler_params=params(8),
        name="attend_own",
    )(q_own, q_other, own, multiple)


def attend_rest_kernel(q_own, q_other, below, above, far, multiple, before, out_own, out_other):
    tiles, rows, heads_cols = q_own.shape
    lane = lax.broadcasted_iota(jnp.int32, (2 * rows, HEAD_DIM), 1)
    for tile in range(tiles):
        pieces = [below[place] for place in range(tile, REACH)]
        pieces += [above[place] for place in range(tile + REACH + 1 - tiles)]
        pieces += [far[tile]]
        keys_values = jnp.concatenate(pieces, axis=0)
        extra = jnp.zeros((2 * rows, HEAD_DIM), jnp.float32)
        for head in range(heads_cols // HEAD_DIM):
            start = head * HEAD_DIM
            cut = slice(start, start + HEAD_DIM)
            second = slice(heads_cols + start, heads_cols + start + HEAD_DIM)
            queries = jnp.concatenate([q_own[tile, :, cut], q_other[tile, :, cut]], axis=0)
            peak_before = before[tile, :, heads_cols + head : heads_cols + head + 1]
            total_before = before[tile, :, heads_cols + 64 + head : heads_cols + 65 + head]
            peak, total, summed = soften(
                queries,
                keys_values[:, cut],
                keys_values[:, second],
                multiple[tile, :, : keys_values.shape[0]],
                peak_before,
            )
            shrink = jnp.exp(peak_before - peak)
            total += total_before * shrink
            summed += before[tile, :, cut] * shrink
            out_own[tile, :, cut] = summed[:rows]
            out_other[tile, :, cut] = summed[rows:]
            extra = jnp.where(lane == head, peak, extra)
            extra = jnp.where(lane == 64 + head, total, extra)
        out_own[tile, :, heads_cols:] = extra[:rows]
        out_other[tile, :, heads_cols:] = extra[rows:]


def attend_rest(q_own, q_other, below, above, far, multiple, before):
    tiles, rows, heads_cols = q_own.shape
    return pl.pallas_call(
        attend_rest_kernel,
        in_specs=[ON_CHIP] * 7,
        out_specs=[ON_CHIP] * 2,
        out_shape=[struct((tiles, rows, heads_cols + HEAD_DIM), jnp.float32)] * 2,
        compiler_params=params(8),
        name="attend_rest",
    )(q_own, q_other, below, above, far, multiple, before)


def spread_kernel(
    meta, part_a, part_b, wo_own, wo_other, keep, to_next, to_across, to_prev, att, weights, sems
):
    tiles, rows, _ = part_a.shape
    parts, heads_cols, cols = weights.shape

    def fetch(j, source):
        first = pl.multiple_of(lax.rem(meta[0] + j, parts) * cols, cols)
        return pltpu.make_async_copy(
            source.at[:, pl.ds(first, cols)], weights.at[j], sems.at[j]
        )

    for chosen, source in enumerate((wo_other, wo_own)):

        @pl.when(meta[1] == chosen)
        def _():
            for j in range(parts):
                fetch(j, source).start()

    for tile in range(tiles):
        extra_a = part_a[tile, :, heads_cols:]
        extra_b = part_b[tile, :, heads_cols:]
        for head in range(heads_cols // HEAD_DIM):
            cut = slice(head * HEAD_DIM, (head + 1) * HEAD_DIM)
            peak_a, total_a = extra_a[:, head : head + 1], extra_a[:, 64 + head : 65 + head]
            peak_b, total_b = extra_b[:, head : head + 1], extra_b[:, 64 + head : 65 + head]
            peak = jnp.maximum(peak_a, peak_b)
            grow_a, grow_b = jnp.exp(peak_a - peak), jnp.exp(peak_b - peak)
            total = total_a * grow_a + total_b * grow_b
            summed = part_a[tile, :, cut] * grow_a + part_b[tile, :, cut] * grow_b
            att[tile * rows : (tile + 1) * rows, cut] = (summed / total).astype(jnp.bfloat16)
    for j in range(parts):
        fetch(j, wo_own).wait()
    for j, out in enumerate((keep, to_next, to_across, to_prev)):
        product = jnp.dot(att[...], weights[j], preferred_element_type=jnp.float32)
        out[...] = product.astype(out.dtype)


def spread(meta, part_a, part_b, wo_own, wo_other, parts):
    tiles, rows, _ = part_a.shape
    heads_cols, width = wo_own.shape
    shape = (tiles * rows, width // parts)
    return pl.pallas_call(
        spread_kernel,
        in_specs=[SCALARS] + [ON_CHIP] * 2 + [ANYWHERE] * 2,
        out_specs=[ON_CHIP] * 4,
        out_shape=[struct(shape, jnp.float32)] + [struct(shape)] * 3,
        scratch_shapes=[
            pltpu.VMEM((tiles * rows, heads_cols), jnp.bfloat16),
            pltpu.VMEM((parts, heads_cols, width // parts), jnp.bfloat16),
            pltpu.SemaphoreType.DMA((parts,)),
        ],
        compiler_params=params(12),
        name="spread",
    )(meta, part_a, part_b, wo_own, wo_other)


def finish_kernel(hidden, gate, keep, from_prev, from_across, from_next, out):
    total = keep[...]
    for part in (from_prev, from_across, from_next):
        total += part[...].astype(jnp.float32)
    out[...] = (hidden[...].astype(jnp.float32) + gate[...] * total).astype(out.dtype)


def finish(hidden, gate, *parts):
    return pl.pallas_call(
        finish_kernel,
        in_specs=[ON_CHIP] * (2 + len(parts)),
        out_specs=ON_CHIP,
        out_shape=struct(hidden.shape),
        compiler_params=params(8),
        name="finish",
    )(hidden, gate, *parts)


def count_tiles(table, counts, chip, per_chip, repeat):
    tiles, slots = table.shape
    table = lax.dynamic_slice_in_dim(table, chip * per_chip, per_chip, 0)
    counts = lax.dynamic_slice_in_dim(counts, chip * per_chip, per_chip, 0)
    query_tiles = jnp.arange(per_chip, dtype=jnp.int32) + chip * per_chip
    across = tiles // 2 + (tiles // per_chip) // 2
    rows = []
    for tile in range(per_chip):
        first, last = max(0, tile - REACH), min(per_chip, tile + REACH + 1)
        own = [place - tile for place in range(first, last)]
        rest = [place - REACH - tile for place in range(tile, REACH)]
        rest += [per_chip + place - tile for place in range(tile + REACH + 1 - per_chip)]
        rest += [across]
        own = [d % tiles for d in own] + [-1] * (256 // repeat - len(own))
        rest = [d % tiles for d in rest] + [-1] * (128 // repeat - len(rest))
        rows.append([d for d in own + rest for _ in range(repeat)])
    reach = jnp.array(rows, jnp.int32)
    relative = (table - query_tiles[:, None]) % tiles
    live = jnp.arange(slots, dtype=jnp.int32)[None] < counts[:, None]
    hits = (relative[:, :, None] == reach[:, None]) & live[:, :, None]
    return jnp.sum(hits.astype(jnp.float32), axis=1)[:, None]


def gather_features(hidden):
    across = shifted(hidden, "tp", 2)
    return hidden, shifted(hidden, "tp", -1), across, shifted(hidden, "tp", 1)


def local(
    latents, w_qkv, w_out, modulation, qk_gain, stale_cache, kv_tiles, tile_counts, patch_order
):
    core = lax.axis_index("segment")
    seq_size = lax.axis_size("seq")
    seq_pos = lax.axis_index("seq")
    tp_size = lax.axis_size("tp")
    tp_pos = lax.axis_index("tp")
    patches, patch_rows, part_cols = latents.shape
    rows_core = patch_rows // 2
    rows = patches * rows_core
    share = seq_size // patches
    chip = share * lax.rem(seq_pos, patches) + seq_pos // patches
    w_own = jnp.transpose(w_qkv[0], (1, 0, 2))
    heads_cols, width = w_out.shape[1:]
    head_dim = qk_gain.shape[-1]

    mine = lax.dynamic_slice_in_dim(latents, core * rows_core, rows_core, 1)
    hidden = exchanged(mine).reshape(rows, part_cols)
    w_other = shifted(w_own, "segment", 1)
    small_own = jnp.concatenate([modulation[0].reshape(-1), qk_gain[0].reshape(-1)])
    small_other = shifted(small_own, "segment", 1)
    stale = after(stale_cache[0], mine)
    stale = jnp.concatenate([stale[0], stale[1]], axis=-1)
    stale_own = lax.dynamic_slice_in_dim(stale, core * rows_core, rows_core, 1)
    stale_other = shifted(
        lax.dynamic_slice_in_dim(stale, (1 - core) * rows_core, rows_core, 1), "segment", 1
    )
    stale = jnp.concatenate([stale_own, stale_other], axis=1)
    wo_own = after(w_out[0], hidden)
    wo_other = shifted(wo_own, "segment", 1)

    turns = jnp.arange(patches, dtype=jnp.int32)
    asked = jnp.stack([chip, chip - 1, chip + 1, chip - seq_size // 2 - 1]) % seq_size // share
    ranks = jnp.sum(jnp.where(patch_order[None] == asked[:, None], turns[None], 0), axis=-1)
    fresh = (ranks[0] <= ranks[1:]).astype(jnp.int32)

    for section in range(2):
        is_own = core == section
        meta = jnp.concatenate(
            [jnp.stack([tp_pos, is_own.astype(tp_pos.dtype)]).astype(jnp.int32), fresh]
        )
        small = jnp.where(is_own, small_own, small_other)
        modul = small[: 3 * width].reshape(3, tp_size, 1, part_cols)
        gain = small[3 * width :].reshape(2, head_dim)
        gate = lax.dynamic_index_in_dim(modul[2], tp_pos, 0, keepdims=False)

        blocks = gather_features(hidden)
        if section == 0:
            stale = exchanged(after(stale, blocks[1], blocks[3]))
        else:
            early = exchanged(after(early, blocks[1], blocks[3]))
        q_own, kv, *going = project(
            meta,
            blocks,
            modul[0],
            modul[1],
            gain,
            w_own,
            w_other,
            stale if section > 0 else None,
            stale_own.shape,
        )
        if section == 0:
            going = choose_alone(meta, kv, stale)
        to_below, to_above, to_far = going
        far = along_ring(to_far, seq_size // 2 + 1, patches)
        above = along_ring(to_below, 1, patches)
        below = along_ring(to_above, -1, patches)
        q_other = shifted(q_own, "segment", 1)
        if section == 0:
            kv_tiles, tile_counts = after((kv_tiles, tile_counts), q_own)
            multiple_own = count_tiles(kv_tiles[0], tile_counts[0], chip, patches, rows_core)
            multiple_other = shifted(multiple_own, "segment", 1)
        else:
            above, early = lax.optimization_barrier((above, early))
        multiple = jnp.where(is_own, multiple_own, multiple_other)
        before = attend_own(q_own, q_other, kv, multiple[..., :256])
        part_own, part_other = attend_rest(
            q_own, q_other, below, above, far, multiple[..., 256:], before
        )
        part_back = shifted(part_other, "segment", 1)
        keep, to_next, to_across, to_prev = spread(
            meta, part_own, part_back, wo_own, wo_other, tp_size
        )
        from_across = shifted(to_across, "tp", 2)
        from_prev = shifted(to_next, "tp", 1)
        from_next = shifted(to_prev, "tp", -1)
        hidden = finish(hidden, gate, keep, from_prev, from_across, from_next)

        features = hidden.reshape(patches, rows_core, part_cols)
        pair = (kv, features) if section == 0 else (features, kv)
        got = shifted(jnp.where(core == 0, pair[1], pair[0]), "segment", 1)
        own = jnp.where(core == 0, pair[0], pair[1])
        halves = [jnp.where(core == place, own, got) for place in range(2)]
        if section == 0:
            early = jnp.concatenate(halves, axis=1)
        else:
            late = exchanged(jnp.concatenate(halves, axis=1))

    handed, new_cache = collect(core.astype(jnp.int32)[None], early, late)
    return (handed[None], new_cache[None])


def solution(mesh):
    in_specs = (
        P(None, "seq", "tp"),
        P("segment", None, None, "tp"),
        P("segment", "tp", None),
        P("segment", None, None),
        P("segment", None, None),
        P("segment", None, None, "seq", "tp"),
        P("segment", None, None),
        P("segment", None),
        P(),
    )
    out_specs = (P("segment", None, "seq", "tp"), P("segment", None, None, "seq", "tp"))
    return jax.shard_map(local, mesh=mesh, in_specs=in_specs, out_specs=out_specs, check_vma=False)
```

```python
import jax
import jax.numpy as jnp
from jax import lax
from jax.experimental import pallas as pl
from jax.experimental.pallas import tpu as pltpu
from jax.sharding import PartitionSpec as P

EPS = 1e-06
HEAD_DIM = 128
REACH = 3
MIB = 1024 * 1024
ON_CHIP = pl.BlockSpec(memory_space=pltpu.VMEM)
SCALARS = pl.BlockSpec(memory_space=pltpu.SMEM)
ANYWHERE = pl.BlockSpec(memory_space=pl.ANY)


def shifted(block, axis, distance):
    devices = range(lax.axis_size(axis))
    route = [((i - distance) % len(devices), i) for i in devices]
    return lax.ppermute(block, axis, route)


def after(values, *gates):
    return lax.optimization_barrier((values, gates))[0]


def params(mib):
    return pltpu.CompilerParams(vmem_limit_bytes=mib * MIB)


def struct(shape, dtype=jnp.bfloat16):
    return jax.ShapeDtypeStruct(shape, dtype)


def exchanged(tiles):
    group = tiles.shape[0]
    groups = [list(range(i, i + group)) for i in range(0, lax.axis_size("seq"), group)]
    return lax.all_to_all(tiles, "seq", 0, 0, axis_index_groups=groups)


def along_ring(block, distance, per_chip):
    size = lax.axis_size("seq")
    share = size // per_chip
    place = [per_chip * (i % share) + i // share for i in range(size)]
    route = [(place[(i + distance) % size], place[i]) for i in range(size)]
    return lax.ppermute(block, "seq", route)


def collect_kernel(core, early, late, handed, cache):
    cols = cache.shape[-1]

    def collect(features, keys):
        handed[...] = features[...]
        cache[0] = keys[:, :, :cols]
        cache[1] = keys[:, :, cols:]

    @pl.when(core[0] == 0)
    def _():
        collect(late, early)

    @pl.when(core[0] == 1)
    def _():
        collect(early, late)


def collect(core, early, late):
    patches, rows, cols = early.shape
    return pl.pallas_call(
        collect_kernel,
        in_specs=[SCALARS] + [ON_CHIP] * 2,
        out_specs=[ON_CHIP] * 2,
        out_shape=[struct(early.shape), struct((2, patches, rows, cols // 2))],
        compiler_params=params(8),
        name="collect",
    )(core, early, late)


def choose(meta, kv, stale, outs):
    tiles, rows, _ = kv.shape
    old = pl.ds(pl.multiple_of((1 - meta[1]) * rows, rows), rows)
    for place, out in enumerate(outs):
        first = tiles - REACH if place == 1 else 0
        cut = slice(first, first + out.shape[0])

        @pl.when(meta[2 + place] == 1)
        def _():
            out[...] = kv[cut]

        @pl.when(meta[2 + place] == 0)
        def _():
            out[...] = stale[cut, old]


def choose_kernel(meta, kv, stale, lo_out, hi_out, far_out):
    choose(meta, kv, stale, (lo_out, hi_out, far_out))


def payloads(kv_shape):
    edge = struct((REACH,) + kv_shape[1:])
    return [edge, edge, struct(kv_shape)]


def choose_alone(meta, kv, stale):
    return pl.pallas_call(
        choose_kernel,
        in_specs=[SCALARS] + [ON_CHIP] * 2,
        out_specs=[ON_CHIP] * 3,
        out_shape=payloads(kv.shape),
        compiler_params=params(8),
        name="choose",
    )(meta, kv, stale)


def project_kernel(meta, *refs, with_stale):
    blocks = refs[:4]
    shift, scale, gain, w_own, w_other = refs[4:9]
    refs = refs[9:]
    if with_stale:
        stale, q_out, kv_out, *outs = refs[:-4]
    else:
        q_out, kv_out = refs[:-4]
    xs, modded, weights, sems = refs[-4:]
    _, rows, cols = xs.shape
    tiles, rows_tile, kv_cols = kv_out.shape
    heads_cols = kv_cols // 2
    parts = shift.shape[0]
    width = cols * parts
    features = [lax.rem(meta[0] + j, parts) for j in (2, 1, 3, 0)]

    def fetch(j, source):
        first = pl.multiple_of(features[j] * cols, cols)
        return pltpu.make_async_copy(
            source.at[:, pl.ds(first, cols)],
            weights.at[:, j * cols : (j + 1) * cols],
            sems.at[j],
        )

    arriving = [
        pltpu.make_async_copy(blocks[j], xs.at[j], sems.at[parts + j]) for j in range(parts)
    ]
    for copy in arriving:
        copy.start()
    for chosen, source in enumerate((w_other, w_own)):

        @pl.when(meta[1] == chosen)
        def _():
            for j in range(parts):
                fetch(j, source).start()

    for copy in arriving:
        copy.wait()
    total = jnp.zeros((rows, 1), jnp.float32)
    for j in range(parts):
        total += jnp.sum(xs[j].astype(jnp.float32), axis=-1, keepdims=True)
    mean = total / width
    square = jnp.zeros((rows, 1), jnp.float32)
    for j in range(parts):
        centred = xs[j].astype(jnp.float32) - mean
        square += jnp.sum(centred * centred, axis=-1, keepdims=True)
    spread = lax.rsqrt(square / width + EPS)
    for j in range(parts):
        normed = (xs[j].astype(jnp.float32) - mean) * spread
        modded[:, j * cols : (j + 1) * cols] = (
            normed * (1.0 + scale[features[j]]) + shift[features[j]]
        ).astype(jnp.bfloat16)
    for j in range(parts):
        fetch(j, w_own).wait()

    for part in (1, 2, 0):
        product = jnp.dot(modded[...], weights[part], preferred_element_type=jnp.float32)
        if part == 2:
            kv_out[:, :, heads_cols:] = product.astype(jnp.bfloat16).reshape(
                tiles, rows_tile, heads_cols
            )
            continue
        for head in range(heads_cols // HEAD_DIM):
            cut = slice(head * HEAD_DIM, (head + 1) * HEAD_DIM)
            vec = product[:, cut]
            mean_sq = jnp.mean(vec * vec, axis=-1, keepdims=True)
            vec = vec * lax.rsqrt(mean_sq + EPS) * gain[part : part + 1]
            vec = vec.astype(jnp.bfloat16).reshape(tiles, rows_tile, HEAD_DIM)
            if part == 0:
                q_out[:, :, cut] = vec
            else:
                kv_out[:, :, cut] = vec
    if with_stale:
        choose(meta, kv_out, stale, outs)


def project(meta, blocks, shift, scale, gain, w_own, w_other, stale, kv_shape):
    rows, cols = blocks[0].shape
    tiles, rows_tile, kv_cols = kv_shape
    heads_cols = kv_cols // 2
    parts = shift.shape[0]
    shapes = [struct((tiles, rows_tile, heads_cols)), struct(kv_shape)]
    extra = []
    if stale is not None:
        shapes += payloads(kv_shape)
        extra = [stale]

    def kernel(*refs):
        project_kernel(*refs, with_stale=stale is not None)

    return pl.pallas_call(
        kernel,
        in_specs=[SCALARS]
        + [ANYWHERE] * len(blocks)
        + [ON_CHIP] * 3
        + [ANYWHERE] * 2
        + [ON_CHIP] * len(extra),
        out_specs=[ON_CHIP] * len(shapes),
        out_shape=shapes,
        scratch_shapes=[
            pltpu.VMEM((parts, rows, cols), jnp.bfloat16),
            pltpu.VMEM((rows, parts * cols), jnp.bfloat16),
            pltpu.VMEM((3, parts * cols, heads_cols), jnp.bfloat16),
            pltpu.SemaphoreType.DMA((2 * parts,)),
        ],
        compiler_params=params(56),
        name="project",
    )(meta, *blocks, shift, scale, gain, w_own, w_other, *extra)


def soften(queries, keys, values, times, floors):
    scores = [
        lax.dot_general(q, k, (((1,), (1,)), ((), ())), preferred_element_type=jnp.float32)
        for q, k in zip(queries, keys)
    ]
    scores = [
        jnp.where(count > 0.0, each * HEAD_DIM ** (-0.5), -1e30)
        for each, count in zip(scores, times)
    ]
    peaks = [jnp.max(each, axis=-1, keepdims=True) for each in scores]
    if floors is not None:
        peaks = [jnp.maximum(peak, floor) for peak, floor in zip(peaks, floors)]
    weights = [
        jnp.exp(each - peak) * count for each, peak, count in zip(scores, peaks, times)
    ]
    totals = [jnp.sum(each, axis=-1, keepdims=True) for each in weights]
    summed = [
        jnp.dot(each.astype(jnp.bfloat16), v, preferred_element_type=jnp.float32)
        for each, v in zip(weights, values)
    ]
    return peaks, totals, summed


def head_cuts(heads_cols):
    return [slice(first, first + HEAD_DIM) for first in range(0, heads_cols, HEAD_DIM)]


def packed(peaks, totals):
    lane = lax.broadcasted_iota(jnp.int32, (peaks[0].shape[0], HEAD_DIM), 1)
    out = jnp.zeros((peaks[0].shape[0], HEAD_DIM), jnp.float32)
    for head, (peak, total) in enumerate(zip(peaks, totals)):
        out = jnp.where(lane == head, peak, out)
        out = jnp.where(lane == 64 + head, total, out)
    return out


def attend_own_kernel(q_own, q_other, own, multiple, out):
    tiles, rows, heads_cols = q_own.shape
    cuts = head_cuts(heads_cols)
    for tile in range(tiles):
        first, last = max(0, tile - REACH), min(tiles, tile + REACH + 1)
        count = (last - first) * rows
        both = own[first:last].reshape(count, 2 * heads_cols)
        queries = jnp.concatenate([q_own[tile], q_other[tile]], axis=0)
        peaks, totals, summed = soften(
            [queries[:, cut] for cut in cuts],
            [both[:, cut] for cut in cuts],
            [both[:, heads_cols + cut.start : heads_cols + cut.stop] for cut in cuts],
            [multiple[tile, :, :count]] * len(cuts),
            None,
        )
        for cut, each in zip(cuts, summed):
            out[tile, :, cut] = each
        out[tile, :, heads_cols:] = packed(peaks, totals)


def attend_own(q_own, q_other, own, multiple):
    tiles, rows, heads_cols = q_own.shape
    return pl.pallas_call(
        attend_own_kernel,
        in_specs=[ON_CHIP] * 4,
        out_specs=ON_CHIP,
        out_shape=struct((tiles, 2 * rows, heads_cols + HEAD_DIM), jnp.float32),
        compiler_params=params(8),
        name="attend_own",
    )(q_own, q_other, own, multiple)


def attend_rest_kernel(q_own, q_other, below, above, far, multiple, before, out_own, out_other):
    tiles, rows, heads_cols = q_own.shape
    cuts = head_cuts(heads_cols)
    heads = len(cuts)
    for pair in range(0, tiles, 2):
        queries, keys, values, times, floors, earlier = [], [], [], [], [], []
        for tile in (pair, pair + 1):
            pieces = [below[place] for place in range(tile, REACH)]
            pieces += [above[place] for place in range(tile + REACH + 1 - tiles)]
            pieces += [far[tile]]
            both = jnp.concatenate(pieces, axis=0)
            asked = jnp.concatenate([q_own[tile], q_other[tile]], axis=0)
            extra = before[tile, :, heads_cols:]
            queries += [asked[:, cut] for cut in cuts]
            keys += [both[:, cut] for cut in cuts]
            values += [both[:, heads_cols + cut.start : heads_cols + cut.stop] for cut in cuts]
            times += [multiple[tile, :, : both.shape[0]]] * heads
            floors += [extra[:, head : head + 1] for head in range(heads)]
            earlier += [extra[:, 64 + head : 65 + head] for head in range(heads)]
        peaks, totals, summed = soften(queries, keys, values, times, floors)
        shrink = [jnp.exp(floor - peak) for floor, peak in zip(floors, peaks)]
        totals = [total + old * less for total, old, less in zip(totals, earlier, shrink)]
        for place, tile in enumerate((pair, pair + 1)):
            here = slice(place * heads, (place + 1) * heads)
            for cut, each, less in zip(cuts, summed[here], shrink[here]):
                result = each + before[tile, :, cut] * less
                out_own[tile, :, cut] = result[:rows]
                out_other[tile, :, cut] = result[rows:]
            extra = packed(peaks[here], totals[here])
            out_own[tile, :, heads_cols:] = extra[:rows]
            out_other[tile, :, heads_cols:] = extra[rows:]


def attend_rest(q_own, q_other, below, above, far, multiple, before):
    tiles, rows, heads_cols = q_own.shape
    return pl.pallas_call(
        attend_rest_kernel,
        in_specs=[ON_CHIP] * 7,
        out_specs=[ON_CHIP] * 2,
        out_shape=[struct((tiles, rows, heads_cols + HEAD_DIM), jnp.float32)] * 2,
        compiler_params=params(8),
        name="attend_rest",
    )(q_own, q_other, below, above, far, multiple, before)


def spread_kernel(
    meta, part_a, part_b, wo_own, wo_other, keep, to_next, to_across, to_prev, att, weights, sems
):
    tiles, rows, _ = part_a.shape
    parts, heads_cols, cols = weights.shape

    def fetch(j, source):
        first = pl.multiple_of(lax.rem(meta[0] + j, parts) * cols, cols)
        return pltpu.make_async_copy(
            source.at[:, pl.ds(first, cols)], weights.at[j], sems.at[j]
        )

    for chosen, source in enumerate((wo_other, wo_own)):

        @pl.when(meta[1] == chosen)
        def _():
            for j in range(parts):
                fetch(j, source).start()

    extra_a = part_a[:, :, heads_cols:].reshape(tiles * rows, HEAD_DIM)
    extra_b = part_b[:, :, heads_cols:].reshape(tiles * rows, HEAD_DIM)
    for head, cut in enumerate(head_cuts(heads_cols)):
        peak_a, total_a = extra_a[:, head : head + 1], extra_a[:, 64 + head : 65 + head]
        peak_b, total_b = extra_b[:, head : head + 1], extra_b[:, 64 + head : 65 + head]
        peak = jnp.maximum(peak_a, peak_b)
        grow_a, grow_b = jnp.exp(peak_a - peak), jnp.exp(peak_b - peak)
        total = total_a * grow_a + total_b * grow_b
        summed_a = part_a[:, :, cut].reshape(tiles * rows, HEAD_DIM)
        summed_b = part_b[:, :, cut].reshape(tiles * rows, HEAD_DIM)
        att[:, cut] = (summed_a * (grow_a / total) + summed_b * (grow_b / total)).astype(
            jnp.bfloat16
        )
    for j in range(parts):
        fetch(j, wo_own).wait()
    for j, out in enumerate((keep, to_next, to_across, to_prev)):
        product = jnp.dot(att[...], weights[j], preferred_element_type=jnp.float32)
        out[...] = product.astype(out.dtype)


def spread(meta, part_a, part_b, wo_own, wo_other, parts):
    tiles, rows, _ = part_a.shape
    heads_cols, width = wo_own.shape
    shape = (tiles * rows, width // parts)
    return pl.pallas_call(
        spread_kernel,
        in_specs=[SCALARS] + [ON_CHIP] * 2 + [ANYWHERE] * 2,
        out_specs=[ON_CHIP] * 4,
        out_shape=[struct(shape, jnp.float32)] + [struct(shape)] * 3,
        scratch_shapes=[
            pltpu.VMEM((tiles * rows, heads_cols), jnp.bfloat16),
            pltpu.VMEM((parts, heads_cols, width // parts), jnp.bfloat16),
            pltpu.SemaphoreType.DMA((parts,)),
        ],
        compiler_params=params(12),
        name="spread",
    )(meta, part_a, part_b, wo_own, wo_other)


def finish_kernel(meta, from_across, from_prev, from_next, keep, hidden, gates, out):
    total = keep[...]
    for part in (from_prev, from_across, from_next):
        total += part[...].astype(jnp.float32)
    gate = gates[meta[0]]
    out[...] = (hidden[...].astype(jnp.float32) + gate * total).astype(out.dtype)


def finish(meta, from_across, from_prev, from_next, keep, hidden, gates):
    return pl.pallas_call(
        finish_kernel,
        in_specs=[SCALARS] + [ON_CHIP] * 6,
        out_specs=ON_CHIP,
        out_shape=struct(hidden.shape),
        compiler_params=params(8),
        name="finish",
    )(meta, from_across, from_prev, from_next, keep, hidden, gates)


def count_tiles(table, counts, chip, per_chip, repeat):
    tiles, slots = table.shape
    table = lax.dynamic_slice_in_dim(table, chip * per_chip, per_chip, 0)
    counts = lax.dynamic_slice_in_dim(counts, chip * per_chip, per_chip, 0)
    query_tiles = jnp.arange(per_chip, dtype=jnp.int32) + chip * per_chip
    across = tiles // 2 + (tiles // per_chip) // 2
    rows = []
    for tile in range(per_chip):
        first, last = max(0, tile - REACH), min(per_chip, tile + REACH + 1)
        own = [place - tile for place in range(first, last)]
        rest = [place - REACH - tile for place in range(tile, REACH)]
        rest += [per_chip + place - tile for place in range(tile + REACH + 1 - per_chip)]
        rest += [across]
        own = [d % tiles for d in own] + [-1] * (256 // repeat - len(own))
        rest = [d % tiles for d in rest] + [-1] * (128 // repeat - len(rest))
        rows.append([d for d in own + rest for _ in range(repeat)])
    reach = jnp.array(rows, jnp.int32)
    relative = (table - query_tiles[:, None]) % tiles
    live = jnp.arange(slots, dtype=jnp.int32)[None] < counts[:, None]
    hits = (relative[:, :, None] == reach[:, None]) & live[:, :, None]
    return jnp.sum(hits.astype(jnp.float32), axis=1)[:, None]


def gather_features(hidden):
    across = shifted(hidden, "tp", 2)
    return across, shifted(hidden, "tp", -1), shifted(hidden, "tp", 1), hidden


def local(
    latents, w_qkv, w_out, modulation, qk_gain, stale_cache, kv_tiles, tile_counts, patch_order
):
    core = lax.axis_index("segment")
    seq_size = lax.axis_size("seq")
    seq_pos = lax.axis_index("seq")
    tp_size = lax.axis_size("tp")
    tp_pos = lax.axis_index("tp")
    patches, patch_rows, part_cols = latents.shape
    rows_core = patch_rows // 2
    rows = patches * rows_core
    share = seq_size // patches
    chip = share * lax.rem(seq_pos, patches) + seq_pos // patches
    w_own = jnp.transpose(w_qkv[0], (1, 0, 2))
    heads_cols, width = w_out.shape[1:]
    head_dim = qk_gain.shape[-1]

    mine = lax.dynamic_slice_in_dim(latents, core * rows_core, rows_core, 1)
    hidden = exchanged(mine).reshape(rows, part_cols)
    w_other = shifted(w_own, "segment", 1)
    small_own = jnp.concatenate([modulation[0].reshape(-1), qk_gain[0].reshape(-1)])
    small_other = shifted(small_own, "segment", 1)
    stale = after(stale_cache[0], mine)
    stale = jnp.concatenate([stale[0], stale[1]], axis=-1)
    stale_own = lax.dynamic_slice_in_dim(stale, core * rows_core, rows_core, 1)
    stale_other = shifted(
        lax.dynamic_slice_in_dim(stale, (1 - core) * rows_core, rows_core, 1), "segment", 1
    )
    stale = jnp.concatenate([stale_own, stale_other], axis=1)
    turns = jnp.arange(patches, dtype=jnp.int32)
    asked = jnp.stack([chip, chip - 1, chip + 1, chip - seq_size // 2 - 1]) % seq_size // share
    ranks = jnp.sum(jnp.where(patch_order[None] == asked[:, None], turns[None], 0), axis=-1)
    fresh = (ranks[0] <= ranks[1:]).astype(jnp.int32)
    multiple_own = count_tiles(kv_tiles[0], tile_counts[0], chip, patches, rows_core)
    multiple_other = shifted(multiple_own, "segment", 1)
    given = []
    for section in range(2):
        is_own = core == section
        meta = jnp.concatenate(
            [jnp.stack([tp_pos, is_own.astype(tp_pos.dtype)]).astype(jnp.int32), fresh]
        )
        small = jnp.where(is_own, small_own, small_other)
        modul = small[: 3 * width].reshape(3, tp_size, 1, part_cols)
        gain = small[3 * width :].reshape(2, head_dim)
        multiple = jnp.where(is_own, multiple_own, multiple_other)
        given.append(
            (meta, modul[0], modul[1], modul[2], gain, multiple[..., :256], multiple[..., 256:])
        )
    hidden, given, stale, w_out = lax.optimization_barrier((hidden, given, stale, w_out))
    wo_own = w_out[0]
    wo_other = shifted(wo_own, "segment", 1)

    for section in range(2):
        meta, shift, scale, gates, gain, times_own, times_rest = given[section]
        blocks = gather_features(hidden)
        if section == 0:
            stale = exchanged(after(stale, blocks[1], blocks[2]))
        else:
            early = exchanged(after(early, blocks[1], blocks[2]))
        q_own, kv, *going = project(
            meta,
            blocks,
            shift,
            scale,
            gain,
            w_own,
            w_other,
            stale if section > 0 else None,
            stale_own.shape,
        )
        if section == 0:
            going = choose_alone(meta, kv, stale)
        to_below, to_above, to_far = going
        far = along_ring(to_far, seq_size // 2 + 1, patches)
        above = along_ring(to_below, 1, patches)
        below = along_ring(to_above, -1, patches)
        q_other = shifted(q_own, "segment", 1)
        if section > 0:
            above, early = lax.optimization_barrier((above, early))
        before = attend_own(q_own, q_other, kv, times_own)
        part_own, part_other = attend_rest(
            q_own, q_other, below, above, far, times_rest, before
        )
        part_back = shifted(part_other, "segment", 1)
        keep, to_next, to_across, to_prev = spread(
            meta, part_own, part_back, wo_own, wo_other, tp_size
        )
        from_across = shifted(to_across, "tp", 2)
        from_prev = shifted(to_next, "tp", 1)
        from_next = shifted(to_prev, "tp", -1)
        hidden = finish(meta, from_across, from_prev, from_next, keep, hidden, gates)

        features = hidden.reshape(patches, rows_core, part_cols)
        pair = (kv, features) if section == 0 else (features, kv)
        got = shifted(jnp.where(core == 0, pair[1], pair[0]), "segment", 1)
        own = jnp.where(core == 0, pair[0], pair[1])
        halves = [jnp.where(core == place, own, got) for place in range(2)]
        if section == 0:
            early = jnp.concatenate(halves, axis=1)
        else:
            late = exchanged(jnp.concatenate(halves, axis=1))

    handed, new_cache = collect(core.astype(jnp.int32)[None], early, late)
    return (handed[None], new_cache[None])


def solution(mesh):
    in_specs = (
        P(None, "seq", "tp"),
        P("segment", None, None, "tp"),
        P("segment", "tp", None),
        P("segment", None, None),
        P("segment", None, None),
        P("segment", None, None, "seq", "tp"),
        P("segment", None, None),
        P("segment", None),
        P(),
    )
    out_specs = (P("segment", None, "seq", "tp"), P("segment", None, None, "seq", "tp"))
    return jax.shard_map(local, mesh=mesh, in_specs=in_specs, out_specs=out_specs, check_vma=False)
```

```python
import jax
import jax.numpy as jnp
from jax import lax
from jax.experimental import pallas as pl
from jax.experimental.pallas import tpu as pltpu
from jax.sharding import PartitionSpec as P

EPS = 1e-06
HEAD_DIM = 128
REACH = 3
MIB = 1024 * 1024
ON_CHIP = pl.BlockSpec(memory_space=pltpu.VMEM)
SCALARS = pl.BlockSpec(memory_space=pltpu.SMEM)
ANYWHERE = pl.BlockSpec(memory_space=pl.ANY)


def shifted(block, axis, distance):
    devices = range(lax.axis_size(axis))
    route = [((i - distance) % len(devices), i) for i in devices]
    return lax.ppermute(block, axis, route)


def after(values, *gates):
    return lax.optimization_barrier((values, gates))[0]


def params(mib):
    return pltpu.CompilerParams(vmem_limit_bytes=mib * MIB)


def struct(shape, dtype=jnp.bfloat16):
    return jax.ShapeDtypeStruct(shape, dtype)


def exchanged(tiles):
    group = tiles.shape[0]
    groups = [list(range(i, i + group)) for i in range(0, lax.axis_size("seq"), group)]
    return lax.all_to_all(tiles, "seq", 0, 0, axis_index_groups=groups)


def along_ring(block, distance, per_chip):
    size = lax.axis_size("seq")
    share = size // per_chip
    place = [per_chip * (i % share) + i // share for i in range(size)]
    route = [(place[(i + distance) % size], place[i]) for i in range(size)]
    return lax.ppermute(block, "seq", route)


def collect_kernel(core, early, own, got, handed, cache):
    patches, rows, _ = own.shape
    cols = cache.shape[-1]

    @pl.when(core[0] == 0)
    def _():
        handed[:, :rows] = own[...]
        handed[:, rows:] = got[...]
        cache[0] = early[:, : 2 * rows, :cols]
        cache[1] = early[:, : 2 * rows, cols:]

    @pl.when(core[0] == 1)
    def _():
        handed[...] = early[:, : 2 * rows]
        for half in range(2):
            cut = slice(half * cols, (half + 1) * cols)
            cache[half, :, :rows] = got[:, :, cut]
            cache[half, :, rows:] = own[:, :, cut]


def collect(core, early, own, got):
    patches, rows, cols = own.shape
    return pl.pallas_call(
        collect_kernel,
        in_specs=[SCALARS] + [ON_CHIP] * 3,
        out_specs=[ON_CHIP] * 2,
        out_shape=[
            struct((patches, 2 * rows, cols)),
            struct((2, patches, 2 * rows, cols // 2)),
        ],
        compiler_params=params(8),
        name="collect",
    )(core, early, own, got)


def choose(meta, kv, stale, outs):
    tiles = kv.shape[0]
    for place, out in enumerate(outs):
        first = tiles - REACH if place == 1 else 0
        cut = slice(first, first + out.shape[0])

        @pl.when(meta[2 + place] == 1)
        def _():
            out[...] = kv[cut]

        @pl.when(meta[2 + place] == 0)
        def _():
            out[...] = stale[cut]


def payloads(kv_shape):
    edge = struct((REACH,) + kv_shape[1:])
    return [edge, edge, struct(kv_shape)]


def project_kernel(meta, *refs):
    blocks = refs[:4]
    shift, scale, gain, w_own, w_other = refs[4:9]
    refs = refs[9:]
    stale, q_out, kv_out, *outs = refs[:-4]
    xs, modded, weights, sems = refs[-4:]
    _, rows, cols = xs.shape
    tiles, rows_tile, kv_cols = kv_out.shape
    heads_cols = kv_cols // 2
    parts = shift.shape[0]
    width = cols * parts
    features = [lax.rem(meta[0] + j, parts) for j in (2, 1, 3, 0)]

    def fetch(j, source):
        first = pl.multiple_of(features[j] * cols, cols)
        return pltpu.make_async_copy(
            source.at[:, pl.ds(first, cols)],
            weights.at[:, j * cols : (j + 1) * cols],
            sems.at[j],
        )

    arriving = [
        pltpu.make_async_copy(blocks[j], xs.at[j], sems.at[parts + j]) for j in range(parts)
    ]
    for copy in arriving:
        copy.start()
    for chosen, source in enumerate((w_other, w_own)):

        @pl.when(meta[1] == chosen)
        def _():
            for j in range(parts):
                fetch(j, source).start()

    for copy in arriving:
        copy.wait()
    total = jnp.zeros((rows, 1), jnp.float32)
    for j in range(parts):
        total += jnp.sum(xs[j].astype(jnp.float32), axis=-1, keepdims=True)
    mean = total / width
    square = jnp.zeros((rows, 1), jnp.float32)
    for j in range(parts):
        centred = xs[j].astype(jnp.float32) - mean
        square += jnp.sum(centred * centred, axis=-1, keepdims=True)
    spread = lax.rsqrt(square / width + EPS)
    for j in range(parts):
        normed = (xs[j].astype(jnp.float32) - mean) * spread
        modded[:, j * cols : (j + 1) * cols] = (
            normed * (1.0 + scale[features[j]]) + shift[features[j]]
        ).astype(jnp.bfloat16)
    for j in range(parts):
        fetch(j, w_own).wait()

    for part in (1, 2, 0):
        product = jnp.dot(modded[...], weights[part], preferred_element_type=jnp.float32)
        if part == 2:
            kv_out[:, :, heads_cols:] = product.astype(jnp.bfloat16).reshape(
                tiles, rows_tile, heads_cols
            )
            continue
        for head in range(heads_cols // HEAD_DIM):
            cut = slice(head * HEAD_DIM, (head + 1) * HEAD_DIM)
            vec = product[:, cut]
            mean_sq = jnp.mean(vec * vec, axis=-1, keepdims=True)
            vec = vec * lax.rsqrt(mean_sq + EPS) * gain[part : part + 1]
            vec = vec.astype(jnp.bfloat16).reshape(tiles, rows_tile, HEAD_DIM)
            if part == 0:
                q_out[:, :, cut] = vec
            else:
                kv_out[:, :, cut] = vec
    choose(meta, kv_out, stale, outs)


def project(meta, blocks, shift, scale, gain, w_own, w_other, stale):
    rows, cols = blocks[0].shape
    tiles, rows_tile, kv_cols = stale.shape
    heads_cols = kv_cols // 2
    parts = shift.shape[0]
    shapes = [struct((tiles, rows_tile, heads_cols)), struct(stale.shape)]
    shapes += payloads(stale.shape)
    return pl.pallas_call(
        project_kernel,
        in_specs=[SCALARS]
        + [ANYWHERE] * len(blocks)
        + [ON_CHIP] * 3
        + [ANYWHERE] * 2
        + [ON_CHIP],
        out_specs=[ON_CHIP] * len(shapes),
        out_shape=shapes,
        scratch_shapes=[
            pltpu.VMEM((parts, rows, cols), jnp.bfloat16),
            pltpu.VMEM((rows, parts * cols), jnp.bfloat16),
            pltpu.VMEM((3, parts * cols, heads_cols), jnp.bfloat16),
            pltpu.SemaphoreType.DMA((2 * parts,)),
        ],
        compiler_params=params(52),
        name="project",
    )(meta, *blocks, shift, scale, gain, w_own, w_other, stale)


def soften(queries, keys, values, times, floors):
    scores = [
        lax.dot_general(q, k, (((1,), (1,)), ((), ())), preferred_element_type=jnp.float32)
        for q, k in zip(queries, keys)
    ]
    scores = [
        jnp.where(count > 0.0, each * HEAD_DIM ** (-0.5), -1e30)
        for each, count in zip(scores, times)
    ]
    peaks = [jnp.max(each, axis=-1, keepdims=True) for each in scores]
    if floors is not None:
        peaks = [jnp.maximum(peak, floor) for peak, floor in zip(peaks, floors)]
    weights = [
        jnp.exp(each - peak) * count for each, peak, count in zip(scores, peaks, times)
    ]
    totals = [jnp.sum(each, axis=-1, keepdims=True) for each in weights]
    summed = [
        jnp.dot(each.astype(jnp.bfloat16), v, preferred_element_type=jnp.float32)
        for each, v in zip(weights, values)
    ]
    return peaks, totals, summed


def head_cuts(heads_cols):
    return [slice(first, first + HEAD_DIM) for first in range(0, heads_cols, HEAD_DIM)]


def packed(peaks, totals):
    lane = lax.broadcasted_iota(jnp.int32, (peaks[0].shape[0], HEAD_DIM), 1)
    out = jnp.zeros((peaks[0].shape[0], HEAD_DIM), jnp.float32)
    for head, (peak, total) in enumerate(zip(peaks, totals)):
        out = jnp.where(lane == head, peak, out)
        out = jnp.where(lane == 64 + head, total, out)
    return out


def attend_own_kernel(q_own, q_other, own, multiple, out):
    tiles, rows, heads_cols = q_own.shape
    cuts = head_cuts(heads_cols)
    for tile in range(tiles):
        first, last = max(0, tile - REACH), min(tiles, tile + REACH + 1)
        count = (last - first) * rows
        both = own[first:last].reshape(count, 2 * heads_cols)
        queries = jnp.concatenate([q_own[tile], q_other[tile]], axis=0)
        peaks, totals, summed = soften(
            [queries[:, cut] for cut in cuts],
            [both[:, cut] for cut in cuts],
            [both[:, heads_cols + cut.start : heads_cols + cut.stop] for cut in cuts],
            [multiple[tile, :, :count]] * len(cuts),
            None,
        )
        for cut, each in zip(cuts, summed):
            out[tile, :, cut] = each
        out[tile, :, heads_cols:] = packed(peaks, totals)


def attend_own(q_own, q_other, own, multiple):
    tiles, rows, heads_cols = q_own.shape
    return pl.pallas_call(
        attend_own_kernel,
        in_specs=[ON_CHIP] * 4,
        out_specs=ON_CHIP,
        out_shape=struct((tiles, 2 * rows, heads_cols + HEAD_DIM), jnp.float32),
        compiler_params=params(8),
        name="attend_own",
    )(q_own, q_other, own, multiple)


def attend_rest_kernel(q_own, q_other, below, above, far, multiple, before, out_own, out_other):
    tiles, rows, heads_cols = q_own.shape
    cuts = head_cuts(heads_cols)
    heads = len(cuts)
    for pair in range(0, tiles, 2):
        queries, keys, values, times, floors, earlier = [], [], [], [], [], []
        for tile in (pair, pair + 1):
            pieces = [below[place] for place in range(tile, REACH)]
            pieces += [above[place] for place in range(tile + REACH + 1 - tiles)]
            pieces += [far[tile]]
            both = jnp.concatenate(pieces, axis=0)
            asked = jnp.concatenate([q_own[tile], q_other[tile]], axis=0)
            extra = before[tile, :, heads_cols:]
            queries += [asked[:, cut] for cut in cuts]
            keys += [both[:, cut] for cut in cuts]
            values += [both[:, heads_cols + cut.start : heads_cols + cut.stop] for cut in cuts]
            times += [multiple[tile, :, : both.shape[0]]] * heads
            floors += [extra[:, head : head + 1] for head in range(heads)]
            earlier += [extra[:, 64 + head : 65 + head] for head in range(heads)]
        peaks, totals, summed = soften(queries, keys, values, times, floors)
        shrink = [jnp.exp(floor - peak) for floor, peak in zip(floors, peaks)]
        totals = [total + old * less for total, old, less in zip(totals, earlier, shrink)]
        for place, tile in enumerate((pair, pair + 1)):
            here = slice(place * heads, (place + 1) * heads)
            for cut, each, less in zip(cuts, summed[here], shrink[here]):
                result = each + before[tile, :, cut] * less
                out_own[tile, :, cut] = result[:rows]
                out_other[tile, :, cut] = result[rows:]
            extra = packed(peaks[here], totals[here])
            out_own[tile, :, heads_cols:] = extra[:rows]
            out_other[tile, :, heads_cols:] = extra[rows:]


def attend_rest(q_own, q_other, below, above, far, multiple, before):
    tiles, rows, heads_cols = q_own.shape
    return pl.pallas_call(
        attend_rest_kernel,
        in_specs=[ON_CHIP] * 7,
        out_specs=[ON_CHIP] * 2,
        out_shape=[struct((tiles, rows, heads_cols + HEAD_DIM), jnp.float32)] * 2,
        compiler_params=params(8),
        name="attend_rest",
    )(q_own, q_other, below, above, far, multiple, before)


def spread_kernel(
    meta, part_a, part_b, wo_own, wo_other, keep, to_next, to_across, to_prev, att, weights, sems
):
    tiles, rows, _ = part_a.shape
    parts, heads_cols, cols = weights.shape

    def fetch(j, source):
        first = pl.multiple_of(lax.rem(meta[0] + j, parts) * cols, cols)
        return pltpu.make_async_copy(
            source.at[:, pl.ds(first, cols)], weights.at[j], sems.at[j]
        )

    for chosen, source in enumerate((wo_other, wo_own)):

        @pl.when(meta[1] == chosen)
        def _():
            for j in range(parts):
                fetch(j, source).start()

    extra_a = part_a[:, :, heads_cols:].reshape(tiles * rows, HEAD_DIM)
    extra_b = part_b[:, :, heads_cols:].reshape(tiles * rows, HEAD_DIM)
    for head, cut in enumerate(head_cuts(heads_cols)):
        peak_a, total_a = extra_a[:, head : head + 1], extra_a[:, 64 + head : 65 + head]
        peak_b, total_b = extra_b[:, head : head + 1], extra_b[:, 64 + head : 65 + head]
        peak = jnp.maximum(peak_a, peak_b)
        grow_a, grow_b = jnp.exp(peak_a - peak), jnp.exp(peak_b - peak)
        total = total_a * grow_a + total_b * grow_b
        summed_a = part_a[:, :, cut].reshape(tiles * rows, HEAD_DIM)
        summed_b = part_b[:, :, cut].reshape(tiles * rows, HEAD_DIM)
        att[:, cut] = (summed_a * (grow_a / total) + summed_b * (grow_b / total)).astype(
            jnp.bfloat16
        )
    for j in range(parts):
        fetch(j, wo_own).wait()
    for j, out in enumerate((keep, to_next, to_across, to_prev)):
        product = jnp.dot(att[...], weights[j], preferred_element_type=jnp.float32)
        out[...] = product.astype(out.dtype)


def spread(meta, part_a, part_b, wo_own, wo_other, parts):
    tiles, rows, _ = part_a.shape
    heads_cols, width = wo_own.shape
    shape = (tiles * rows, width // parts)
    return pl.pallas_call(
        spread_kernel,
        in_specs=[SCALARS] + [ON_CHIP] * 2 + [ANYWHERE] * 2,
        out_specs=[ON_CHIP] * 4,
        out_shape=[struct(shape, jnp.float32)] + [struct(shape)] * 3,
        scratch_shapes=[
            pltpu.VMEM((tiles * rows, heads_cols), jnp.bfloat16),
            pltpu.VMEM((parts, heads_cols, width // parts), jnp.bfloat16),
            pltpu.SemaphoreType.DMA((parts,)),
        ],
        compiler_params=params(12),
        name="spread",
    )(meta, part_a, part_b, wo_own, wo_other)


def finish_kernel(meta, from_across, from_prev, from_next, keep, hidden, gates, out):
    total = keep[...]
    for part in (from_prev, from_across, from_next):
        total += part[...].astype(jnp.float32)
    gate = gates[meta[0]]
    out[...] = (hidden[...].astype(jnp.float32) + gate * total).astype(out.dtype)


def finish(meta, from_across, from_prev, from_next, keep, hidden, gates):
    return pl.pallas_call(
        finish_kernel,
        in_specs=[SCALARS] + [ON_CHIP] * 6,
        out_specs=ON_CHIP,
        out_shape=struct(hidden.shape),
        compiler_params=params(8),
        name="finish",
    )(meta, from_across, from_prev, from_next, keep, hidden, gates)


def count_tiles(table, counts, chip, per_chip, repeat):
    tiles, slots = table.shape
    table = lax.dynamic_slice_in_dim(table, chip * per_chip, per_chip, 0)
    counts = lax.dynamic_slice_in_dim(counts, chip * per_chip, per_chip, 0)
    query_tiles = jnp.arange(per_chip, dtype=jnp.int32) + chip * per_chip
    across = tiles // 2 + (tiles // per_chip) // 2
    rows = []
    for tile in range(per_chip):
        first, last = max(0, tile - REACH), min(per_chip, tile + REACH + 1)
        own = [place - tile for place in range(first, last)]
        rest = [place - REACH - tile for place in range(tile, REACH)]
        rest += [per_chip + place - tile for place in range(tile + REACH + 1 - per_chip)]
        rest += [across]
        own = [d % tiles for d in own] + [-1] * (256 // repeat - len(own))
        rest = [d % tiles for d in rest] + [-1] * (128 // repeat - len(rest))
        rows.append([d for d in own + rest for _ in range(repeat)])
    reach = jnp.array(rows, jnp.int32)
    relative = (table - query_tiles[:, None]) % tiles
    live = jnp.arange(slots, dtype=jnp.int32)[None] < counts[:, None]
    hits = (relative[:, :, None] == reach[:, None]) & live[:, :, None]
    return jnp.sum(hits.astype(jnp.float32), axis=1)[:, None]


def gather_features(hidden):
    across = shifted(hidden, "tp", 2)
    return across, shifted(hidden, "tp", -1), shifted(hidden, "tp", 1), hidden


def local(
    latents, w_qkv, w_out, modulation, qk_gain, stale_cache, kv_tiles, tile_counts, patch_order
):
    core = lax.axis_index("segment")
    seq_size = lax.axis_size("seq")
    seq_pos = lax.axis_index("seq")
    tp_size = lax.axis_size("tp")
    tp_pos = lax.axis_index("tp")
    patches, patch_rows, part_cols = latents.shape
    rows_core = patch_rows // 2
    rows = patches * rows_core
    share = seq_size // patches
    chip = share * lax.rem(seq_pos, patches) + seq_pos // patches
    w_own = jnp.transpose(w_qkv[0], (1, 0, 2))
    heads_cols, width = w_out.shape[1:]
    head_dim = qk_gain.shape[-1]

    mine = lax.dynamic_slice_in_dim(latents, core * rows_core, rows_core, 1)
    hidden = exchanged(mine).reshape(rows, part_cols)
    w_other = shifted(w_own, "segment", 1)
    small_own = jnp.concatenate([modulation[0].reshape(-1), qk_gain[0].reshape(-1)])
    small_other = shifted(small_own, "segment", 1)
    stale_all, kv_tiles, tile_counts = after((stale_cache[0], kv_tiles, tile_counts), mine)
    stale_all = exchanged(jnp.concatenate([stale_all[0], stale_all[1]], axis=-1))
    kv_tiles, tile_counts = after((kv_tiles, tile_counts), small_other)
    turns = jnp.arange(patches, dtype=jnp.int32)
    asked = jnp.stack([chip, chip - 1, chip + 1, chip - seq_size // 2 - 1]) % seq_size // share
    ranks = jnp.sum(jnp.where(patch_order[None] == asked[:, None], turns[None], 0), axis=-1)
    fresh = (ranks[0] <= ranks[1:]).astype(jnp.int32)
    multiple_own = count_tiles(kv_tiles[0], tile_counts[0], chip, patches, rows_core)
    multiple_other = shifted(multiple_own, "segment", 1)
    given = []
    for section in range(2):
        is_own = core == section
        meta = jnp.concatenate(
            [jnp.stack([tp_pos, is_own.astype(tp_pos.dtype)]).astype(jnp.int32), fresh]
        )
        small = jnp.where(is_own, small_own, small_other)
        modul = small[: 3 * width].reshape(3, tp_size, 1, part_cols)
        gain = small[3 * width :].reshape(2, head_dim)
        multiple = jnp.where(is_own, multiple_own, multiple_other)
        given.append(
            (meta, modul[0], modul[1], modul[2], gain, multiple[..., :256], multiple[..., 256:])
        )
    hidden, given, stale_all, w_out = lax.optimization_barrier(
        (hidden, given, stale_all, w_out)
    )
    stale_own = lax.dynamic_slice_in_dim(stale_all, core * rows_core, rows_core, 1)
    stale_other = shifted(
        lax.dynamic_slice_in_dim(stale_all, (1 - core) * rows_core, rows_core, 1), "segment", 1
    )
    wo_own = w_out[0]
    wo_other = shifted(wo_own, "segment", 1)

    for section in range(2):
        meta, shift, scale, gates, gain, times_own, times_rest = given[section]
        blocks = gather_features(hidden)
        stale = jnp.where(core == section, stale_own, stale_other)
        q_own, kv, to_below, to_above, to_far = project(
            meta,
            blocks,
            shift,
            scale,
            gain,
            w_own,
            w_other,
            stale,
        )
        far = along_ring(to_far, seq_size // 2 + 1, patches)
        above = along_ring(to_below, 1, patches)
        below = along_ring(to_above, -1, patches)
        q_other = shifted(q_own, "segment", 1)
        before = attend_own(q_own, q_other, kv, times_own)
        part_own, part_other = attend_rest(
            q_own, q_other, below, above, far, times_rest, before
        )
        part_back = shifted(part_other, "segment", 1)
        keep, to_next, to_across, to_prev = spread(
            meta, part_own, part_back, wo_own, wo_other, tp_size
        )
        from_across = shifted(to_across, "tp", 2)
        from_prev = shifted(to_next, "tp", 1)
        from_next = shifted(to_prev, "tp", -1)
        if section > 0:
            early = jnp.concatenate([early, kv], axis=1)
            early = exchanged(after(early, from_prev))
        hidden = finish(meta, from_across, from_prev, from_next, keep, hidden, gates)
        features = hidden.reshape(patches, rows_core, part_cols)
        if section == 0:
            got = shifted(jnp.where(core == 0, features, kv), "segment", 1)
            own = jnp.where(core == 0, kv, features)
            halves = [jnp.where(core == place, own, got) for place in range(2)]
            early = jnp.concatenate(halves, axis=1)
        else:
            features = exchanged(features)

    keys = early[:, patch_rows:]
    got = shifted(jnp.where(core == 0, keys, features), "segment", 1)
    own = jnp.where(core == 0, features, keys)
    handed, new_cache = collect(core.astype(jnp.int32)[None], early, own, got)
    return (handed[None], new_cache[None])


def solution(mesh):
    in_specs = (
        P(None, "seq", "tp"),
        P("segment", None, None, "tp"),
        P("segment", "tp", None),
        P("segment", None, None),
        P("segment", None, None),
        P("segment", None, None, "seq", "tp"),
        P("segment", None, None),
        P("segment", None),
        P(),
    )
    out_specs = (P("segment", None, "seq", "tp"), P("segment", None, None, "seq", "tp"))
    return jax.shard_map(local, mesh=mesh, in_specs=in_specs, out_specs=out_specs, check_vma=False)
```

```python
import jax
import jax.numpy as jnp
from jax import lax
from jax.experimental import pallas as pl
from jax.experimental.pallas import tpu as pltpu
from jax.sharding import PartitionSpec as P

EPS = 1e-06
HEAD_DIM = 128
REACH = 3
MIB = 1024 * 1024
ON_CHIP = pl.BlockSpec(memory_space=pltpu.VMEM)
SCALARS = pl.BlockSpec(memory_space=pltpu.SMEM)
ANYWHERE = pl.BlockSpec(memory_space=pl.ANY)


def shifted(block, axis, distance):
    devices = range(lax.axis_size(axis))
    route = [((i - distance) % len(devices), i) for i in devices]
    return lax.ppermute(block, axis, route)


def after(values, *gates):
    return lax.optimization_barrier((values, gates))[0]


def params(mib):
    return pltpu.CompilerParams(vmem_limit_bytes=mib * MIB)


def struct(shape, dtype=jnp.bfloat16):
    return jax.ShapeDtypeStruct(shape, dtype)


def exchanged(tiles):
    group = tiles.shape[0]
    groups = [list(range(i, i + group)) for i in range(0, lax.axis_size("seq"), group)]
    return lax.all_to_all(tiles, "seq", 0, 0, axis_index_groups=groups)


def along_ring(block, distance, per_chip):
    size = lax.axis_size("seq")
    share = size // per_chip
    place = [per_chip * (i % share) + i // share for i in range(size)]
    route = [(place[(i + distance) % size], place[i]) for i in range(size)]
    return lax.ppermute(block, "seq", route)


def pack_kernel(core, latents, stale, out, sems):
    rows, cols = latents.shape[1] // 2, stale.shape[-1]
    first = pl.multiple_of(core[0] * rows, rows)
    copies = [
        pltpu.make_async_copy(latents.at[:, pl.ds(first, rows)], out.at[:, :rows], sems.at[0])
    ]
    for half in range(2):
        there = out.at[:, rows:, half * cols : (half + 1) * cols]
        copies.append(pltpu.make_async_copy(stale.at[half], there, sems.at[1 + half]))
    for copy in copies:
        copy.start()
    for copy in copies:
        copy.wait()


def pack(core, latents, stale):
    patches, rows, cols = latents.shape
    return pl.pallas_call(
        pack_kernel,
        in_specs=[SCALARS] + [ANYWHERE] * 2,
        out_specs=ON_CHIP,
        out_shape=struct((patches, rows // 2 + rows, cols)),
        scratch_shapes=[pltpu.SemaphoreType.DMA((3,))],
        compiler_params=params(8),
        name="pack",
    )(core, latents, stale)


def collect_kernel(core, keys0, features1, keys1, features2, got1, got2, handed, cache):
    rows, cols = keys0.shape[1], cache.shape[-1]

    def collect(features, keys):
        for half in range(2):
            here = slice(half * rows, (half + 1) * rows)
            handed[:, here] = features[half][...]
            for which in range(2):
                cache[which, :, here] = keys[half][:, :, which * cols : (which + 1) * cols]

    @pl.when(core[0] == 0)
    def _():
        collect((features2, got2), (keys0, got1))

    @pl.when(core[0] == 1)
    def _():
        collect((got1, features1), (got2, keys1))


def collect(core, *halves):
    patches, rows, cols = halves[0].shape
    return pl.pallas_call(
        collect_kernel,
        in_specs=[SCALARS] + [ON_CHIP] * 6,
        out_specs=[ON_CHIP] * 2,
        out_shape=[
            struct((patches, 2 * rows, cols)),
            struct((2, patches, 2 * rows, cols // 2)),
        ],
        compiler_params=params(8),
        name="collect",
    )(core, *halves)


def choose(meta, kv, stale, outs):
    tiles = kv.shape[0]
    for place, out in enumerate(outs):
        first = tiles - REACH if place == 1 else 0
        cut = slice(first, first + out.shape[0])

        @pl.when(meta[2 + place] == 1)
        def _():
            out[...] = kv[cut]

        @pl.when(meta[2 + place] == 0)
        def _():
            out[...] = stale[cut]


def payloads(kv_shape):
    edge = struct((REACH,) + kv_shape[1:])
    return [edge, edge, struct(kv_shape)]


def project_kernel(meta, *refs):
    blocks = refs[:4]
    shift, scale, gain, w_own, w_other = refs[4:9]
    refs = refs[9:]
    stale, q_out, kv_out, *outs = refs[:-4]
    xs, modded, weights, sems = refs[-4:]
    _, rows, cols = xs.shape
    tiles, rows_tile, kv_cols = kv_out.shape
    heads_cols = kv_cols // 2
    parts = shift.shape[0]
    width = cols * parts
    features = [lax.rem(meta[0] + j, parts) for j in (2, 1, 3, 0)]

    def fetch(j, source):
        first = pl.multiple_of(features[j] * cols, cols)
        return pltpu.make_async_copy(
            source.at[:, pl.ds(first, cols)],
            weights.at[:, j * cols : (j + 1) * cols],
            sems.at[j],
        )

    arriving = [
        pltpu.make_async_copy(blocks[j], xs.at[j], sems.at[parts + j]) for j in range(parts)
    ]
    for copy in arriving:
        copy.start()
    for chosen, source in enumerate((w_other, w_own)):

        @pl.when(meta[1] == chosen)
        def _():
            for j in range(parts):
                fetch(j, source).start()

    for copy in arriving:
        copy.wait()
    total = jnp.zeros((rows, 1), jnp.float32)
    for j in range(parts):
        total += jnp.sum(xs[j].astype(jnp.float32), axis=-1, keepdims=True)
    mean = total / width
    square = jnp.zeros((rows, 1), jnp.float32)
    for j in range(parts):
        centred = xs[j].astype(jnp.float32) - mean
        square += jnp.sum(centred * centred, axis=-1, keepdims=True)
    spread = lax.rsqrt(square / width + EPS)
    for j in range(parts):
        normed = (xs[j].astype(jnp.float32) - mean) * spread
        modded[:, j * cols : (j + 1) * cols] = (
            normed * (1.0 + scale[features[j]]) + shift[features[j]]
        ).astype(jnp.bfloat16)
    for j in range(parts):
        fetch(j, w_own).wait()

    for part in (1, 2, 0):
        product = jnp.dot(modded[...], weights[part], preferred_element_type=jnp.float32)
        if part == 2:
            kv_out[:, :, heads_cols:] = product.astype(jnp.bfloat16).reshape(
                tiles, rows_tile, heads_cols
            )
            continue
        for head in range(heads_cols // HEAD_DIM):
            cut = slice(head * HEAD_DIM, (head + 1) * HEAD_DIM)
            vec = product[:, cut]
            mean_sq = jnp.mean(vec * vec, axis=-1, keepdims=True)
            vec = vec * lax.rsqrt(mean_sq + EPS) * gain[part : part + 1]
            vec = vec.astype(jnp.bfloat16).reshape(tiles, rows_tile, HEAD_DIM)
            if part == 0:
                q_out[:, :, cut] = vec
            else:
                kv_out[:, :, cut] = vec
    choose(meta, kv_out, stale, outs)


def project(meta, blocks, shift, scale, gain, w_own, w_other, stale):
    rows, cols = blocks[0].shape
    tiles, rows_tile, kv_cols = stale.shape
    heads_cols = kv_cols // 2
    parts = shift.shape[0]
    shapes = [struct((tiles, rows_tile, heads_cols)), struct(stale.shape)]
    shapes += payloads(stale.shape)
    return pl.pallas_call(
        project_kernel,
        in_specs=[SCALARS]
        + [ANYWHERE] * len(blocks)
        + [ON_CHIP] * 3
        + [ANYWHERE] * 2
        + [ON_CHIP],
        out_specs=[ON_CHIP] * len(shapes),
        out_shape=shapes,
        scratch_shapes=[
            pltpu.VMEM((parts, rows, cols), jnp.bfloat16),
            pltpu.VMEM((rows, parts * cols), jnp.bfloat16),
            pltpu.VMEM((3, parts * cols, heads_cols), jnp.bfloat16),
            pltpu.SemaphoreType.DMA((2 * parts,)),
        ],
        compiler_params=params(52),
        name="project",
    )(meta, *blocks, shift, scale, gain, w_own, w_other, stale)


def soften(queries, keys, values, times, floors):
    scores = [
        lax.dot_general(q, k, (((1,), (1,)), ((), ())), preferred_element_type=jnp.float32)
        for q, k in zip(queries, keys)
    ]
    scores = [
        jnp.where(count > 0.0, each * HEAD_DIM ** (-0.5), -1e30)
        for each, count in zip(scores, times)
    ]
    peaks = [jnp.max(each, axis=-1, keepdims=True) for each in scores]
    if floors is not None:
        peaks = [jnp.maximum(peak, floor) for peak, floor in zip(peaks, floors)]
    weights = [
        jnp.exp(each - peak) * count for each, peak, count in zip(scores, peaks, times)
    ]
    totals = [jnp.sum(each, axis=-1, keepdims=True) for each in weights]
    summed = [
        jnp.dot(each.astype(jnp.bfloat16), v, preferred_element_type=jnp.float32)
        for each, v in zip(weights, values)
    ]
    return peaks, totals, summed


def head_cuts(heads_cols):
    return [slice(first, first + HEAD_DIM) for first in range(0, heads_cols, HEAD_DIM)]


def packed(peaks, totals):
    lane = lax.broadcasted_iota(jnp.int32, (peaks[0].shape[0], HEAD_DIM), 1)
    out = jnp.zeros((peaks[0].shape[0], HEAD_DIM), jnp.float32)
    for head, (peak, total) in enumerate(zip(peaks, totals)):
        out = jnp.where(lane == head, peak, out)
        out = jnp.where(lane == 64 + head, total, out)
    return out


def attend_own_kernel(q_own, q_other, own, multiple, out):
    tiles, rows, heads_cols = q_own.shape
    cuts = head_cuts(heads_cols)
    for tile in range(tiles):
        first, last = max(0, tile - REACH), min(tiles, tile + REACH + 1)
        count = (last - first) * rows
        both = own[first:last].reshape(count, 2 * heads_cols)
        queries = jnp.concatenate([q_own[tile], q_other[tile]], axis=0)
        peaks, totals, summed = soften(
            [queries[:, cut] for cut in cuts],
            [both[:, cut] for cut in cuts],
            [both[:, heads_cols + cut.start : heads_cols + cut.stop] for cut in cuts],
            [multiple[tile, :, :count]] * len(cuts),
            None,
        )
        for cut, each in zip(cuts, summed):
            out[tile, :, cut] = each
        out[tile, :, heads_cols:] = packed(peaks, totals)


def attend_own(q_own, q_other, own, multiple):
    tiles, rows, heads_cols = q_own.shape
    return pl.pallas_call(
        attend_own_kernel,
        in_specs=[ON_CHIP] * 4,
        out_specs=ON_CHIP,
        out_shape=struct((tiles, 2 * rows, heads_cols + HEAD_DIM), jnp.float32),
        compiler_params=params(8),
        name="attend_own",
    )(q_own, q_other, own, multiple)


def attend_rest_kernel(q_own, q_other, below, above, far, multiple, before, out_own, out_other):
    tiles, rows, heads_cols = q_own.shape
    cuts = head_cuts(heads_cols)
    heads = len(cuts)
    for pair in range(0, tiles, 2):
        queries, keys, values, times, floors, earlier = [], [], [], [], [], []
        for tile in (pair, pair + 1):
            pieces = [below[place] for place in range(tile, REACH)]
            pieces += [above[place] for place in range(tile + REACH + 1 - tiles)]
            pieces += [far[tile]]
            both = jnp.concatenate(pieces, axis=0)
            asked = jnp.concatenate([q_own[tile], q_other[tile]], axis=0)
            extra = before[tile, :, heads_cols:]
            queries += [asked[:, cut] for cut in cuts]
            keys += [both[:, cut] for cut in cuts]
            values += [both[:, heads_cols + cut.start : heads_cols + cut.stop] for cut in cuts]
            times += [multiple[tile, :, : both.shape[0]]] * heads
            floors += [extra[:, head : head + 1] for head in range(heads)]
            earlier += [extra[:, 64 + head : 65 + head] for head in range(heads)]
        peaks, totals, summed = soften(queries, keys, values, times, floors)
        shrink = [jnp.exp(floor - peak) for floor, peak in zip(floors, peaks)]
        totals = [total + old * less for total, old, less in zip(totals, earlier, shrink)]
        for place, tile in enumerate((pair, pair + 1)):
            here = slice(place * heads, (place + 1) * heads)
            for cut, each, less in zip(cuts, summed[here], shrink[here]):
                result = each + before[tile, :, cut] * less
                out_own[tile, :, cut] = result[:rows]
                out_other[tile, :, cut] = result[rows:]
            extra = packed(peaks[here], totals[here])
            out_own[tile, :, heads_cols:] = extra[:rows]
            out_other[tile, :, heads_cols:] = extra[rows:]


def attend_rest(q_own, q_other, below, above, far, multiple, before):
    tiles, rows, heads_cols = q_own.shape
    return pl.pallas_call(
        attend_rest_kernel,
        in_specs=[ON_CHIP] * 7,
        out_specs=[ON_CHIP] * 2,
        out_shape=[struct((tiles, rows, heads_cols + HEAD_DIM), jnp.float32)] * 2,
        compiler_params=params(8),
        name="attend_rest",
    )(q_own, q_other, below, above, far, multiple, before)


def spread_kernel(
    meta, part_a, part_b, wo_own, wo_other, keep, to_next, to_across, to_prev, att, weights, sems
):
    tiles, rows, _ = part_a.shape
    parts, heads_cols, cols = weights.shape

    def fetch(j, source):
        first = pl.multiple_of(lax.rem(meta[0] + j, parts) * cols, cols)
        return pltpu.make_async_copy(
            source.at[:, pl.ds(first, cols)], weights.at[j], sems.at[j]
        )

    for chosen, source in enumerate((wo_other, wo_own)):

        @pl.when(meta[1] == chosen)
        def _():
            for j in range(parts):
                fetch(j, source).start()

    extra_a = part_a[:, :, heads_cols:].reshape(tiles * rows, HEAD_DIM)
    extra_b = part_b[:, :, heads_cols:].reshape(tiles * rows, HEAD_DIM)
    for head, cut in enumerate(head_cuts(heads_cols)):
        peak_a, total_a = extra_a[:, head : head + 1], extra_a[:, 64 + head : 65 + head]
        peak_b, total_b = extra_b[:, head : head + 1], extra_b[:, 64 + head : 65 + head]
        peak = jnp.maximum(peak_a, peak_b)
        grow_a, grow_b = jnp.exp(peak_a - peak), jnp.exp(peak_b - peak)
        total = total_a * grow_a + total_b * grow_b
        summed_a = part_a[:, :, cut].reshape(tiles * rows, HEAD_DIM)
        summed_b = part_b[:, :, cut].reshape(tiles * rows, HEAD_DIM)
        att[:, cut] = (summed_a * (grow_a / total) + summed_b * (grow_b / total)).astype(
            jnp.bfloat16
        )
    for j in range(parts):
        fetch(j, wo_own).wait()
    for j, out in enumerate((keep, to_next, to_across, to_prev)):
        product = jnp.dot(att[...], weights[j], preferred_element_type=jnp.float32)
        out[...] = product.astype(out.dtype)


def spread(meta, part_a, part_b, wo_own, wo_other, parts):
    tiles, rows, _ = part_a.shape
    heads_cols, width = wo_own.shape
    shape = (tiles * rows, width // parts)
    return pl.pallas_call(
        spread_kernel,
        in_specs=[SCALARS] + [ON_CHIP] * 2 + [ANYWHERE] * 2,
        out_specs=[ON_CHIP] * 4,
        out_shape=[struct(shape, jnp.float32)] + [struct(shape)] * 3,
        scratch_shapes=[
            pltpu.VMEM((tiles * rows, heads_cols), jnp.bfloat16),
            pltpu.VMEM((parts, heads_cols, width // parts), jnp.bfloat16),
            pltpu.SemaphoreType.DMA((parts,)),
        ],
        compiler_params=params(12),
        name="spread",
    )(meta, part_a, part_b, wo_own, wo_other)


def finish_kernel(meta, from_across, from_prev, from_next, keep, hidden, gates, out):
    total = keep[...]
    for part in (from_prev, from_across, from_next):
        total += part[...].astype(jnp.float32)
    gate = gates[meta[0]]
    out[...] = (hidden[...].astype(jnp.float32) + gate * total).astype(out.dtype)


def finish(meta, from_across, from_prev, from_next, keep, hidden, gates):
    return pl.pallas_call(
        finish_kernel,
        in_specs=[SCALARS] + [ON_CHIP] * 6,
        out_specs=ON_CHIP,
        out_shape=struct(hidden.shape),
        compiler_params=params(8),
        name="finish",
    )(meta, from_across, from_prev, from_next, keep, hidden, gates)


def count_tiles(table, counts, chip, per_chip, repeat):
    tiles, slots = table.shape
    table = lax.dynamic_slice_in_dim(table, chip * per_chip, per_chip, 0)
    counts = lax.dynamic_slice_in_dim(counts, chip * per_chip, per_chip, 0)
    query_tiles = jnp.arange(per_chip, dtype=jnp.int32) + chip * per_chip
    across = tiles // 2 + (tiles // per_chip) // 2
    rows = []
    for tile in range(per_chip):
        first, last = max(0, tile - REACH), min(per_chip, tile + REACH + 1)
        own = [place - tile for place in range(first, last)]
        rest = [place - REACH - tile for place in range(tile, REACH)]
        rest += [per_chip + place - tile for place in range(tile + REACH + 1 - per_chip)]
        rest += [across]
        own = [d % tiles for d in own] + [-1] * (256 // repeat - len(own))
        rest = [d % tiles for d in rest] + [-1] * (128 // repeat - len(rest))
        rows.append([d for d in own + rest for _ in range(repeat)])
    reach = jnp.array(rows, jnp.int32)
    relative = (table - query_tiles[:, None]) % tiles
    live = jnp.arange(slots, dtype=jnp.int32)[None] < counts[:, None]
    hits = (relative[:, :, None] == reach[:, None]) & live[:, :, None]
    return jnp.sum(hits.astype(jnp.float32), axis=1)[:, None]


def gather_features(hidden):
    across = shifted(hidden, "tp", 2)
    return across, shifted(hidden, "tp", -1), shifted(hidden, "tp", 1), hidden


def local(
    latents, w_qkv, w_out, modulation, qk_gain, stale_cache, kv_tiles, tile_counts, patch_order
):
    core = lax.axis_index("segment")
    seq_size = lax.axis_size("seq")
    seq_pos = lax.axis_index("seq")
    tp_size = lax.axis_size("tp")
    tp_pos = lax.axis_index("tp")
    patches, patch_rows, part_cols = latents.shape
    rows_core = patch_rows // 2
    rows = patches * rows_core
    share = seq_size // patches
    chip = share * lax.rem(seq_pos, patches) + seq_pos // patches
    w_own = jnp.transpose(w_qkv[0], (1, 0, 2))
    heads_cols, width = w_out.shape[1:]
    head_dim = qk_gain.shape[-1]

    core_scalar = core.astype(jnp.int32)[None]
    arrived = exchanged(pack(core_scalar, latents, stale_cache[0]))
    hidden = arrived[:, :rows_core].reshape(rows, part_cols)
    stale_all = arrived[:, rows_core:]
    w_other = shifted(w_own, "segment", 1)
    small_own = jnp.concatenate([modulation[0].reshape(-1), qk_gain[0].reshape(-1)])
    small_other = shifted(small_own, "segment", 1)
    kv_tiles, tile_counts = after((kv_tiles, tile_counts), small_other)
    turns = jnp.arange(patches, dtype=jnp.int32)
    asked = jnp.stack([chip, chip - 1, chip + 1, chip - seq_size // 2 - 1]) % seq_size // share
    ranks = jnp.sum(jnp.where(patch_order[None] == asked[:, None], turns[None], 0), axis=-1)
    fresh = (ranks[0] <= ranks[1:]).astype(jnp.int32)
    multiple_own = count_tiles(kv_tiles[0], tile_counts[0], chip, patches, rows_core)
    multiple_other = shifted(multiple_own, "segment", 1)
    given = []
    for section in range(2):
        is_own = core == section
        meta = jnp.concatenate(
            [jnp.stack([tp_pos, is_own.astype(tp_pos.dtype)]).astype(jnp.int32), fresh]
        )
        small = jnp.where(is_own, small_own, small_other)
        modul = small[: 3 * width].reshape(3, tp_size, 1, part_cols)
        gain = small[3 * width :].reshape(2, head_dim)
        multiple = jnp.where(is_own, multiple_own, multiple_other)
        given.append(
            (meta, modul[0], modul[1], modul[2], gain, multiple[..., :256], multiple[..., 256:])
        )
    hidden, given, stale_all, w_out = lax.optimization_barrier(
        (hidden, given, stale_all, w_out)
    )
    stale_own = lax.dynamic_slice_in_dim(stale_all, core * rows_core, rows_core, 1)
    stale_other = shifted(
        lax.dynamic_slice_in_dim(stale_all, (1 - core) * rows_core, rows_core, 1), "segment", 1
    )
    wo_own = w_out[0]
    wo_other = shifted(wo_own, "segment", 1)

    home = []
    for section in range(2):
        meta, shift, scale, gates, gain, times_own, times_rest = given[section]
        blocks = gather_features(hidden)
        stale = jnp.where(core == section, stale_own, stale_other)
        q_own, kv, to_below, to_above, to_far = project(
            meta,
            blocks,
            shift,
            scale,
            gain,
            w_own,
            w_other,
            stale,
        )
        far = along_ring(to_far, seq_size // 2 + 1, patches)
        above = along_ring(to_below, 1, patches)
        below = along_ring(to_above, -1, patches)
        q_other = shifted(q_own, "segment", 1)
        before = attend_own(q_own, q_other, kv, times_own)
        part_own, part_other = attend_rest(
            q_own, q_other, below, above, far, times_rest, before
        )
        part_back = shifted(part_other, "segment", 1)
        keep, to_next, to_across, to_prev = spread(
            meta, part_own, part_back, wo_own, wo_other, tp_size
        )
        from_across = shifted(to_across, "tp", 2)
        from_prev = shifted(to_next, "tp", 1)
        from_next = shifted(to_prev, "tp", -1)
        tiled = hidden.reshape(patches, rows_core, part_cols)
        leaving = kv if section == 0 else jnp.concatenate([tiled, kv], axis=1)
        leaving = exchanged(after(leaving, from_across))
        from_prev, from_next, leaving = lax.optimization_barrier((from_prev, from_next, leaving))
        home.append(leaving)
        hidden = finish(meta, from_across, from_prev, from_next, keep, hidden, gates)

    keys0, features1, keys1 = home[0], home[1][:, :rows_core], home[1][:, rows_core:]
    features2 = exchanged(hidden.reshape(patches, rows_core, part_cols))
    got1 = shifted(jnp.where(core == 0, features1, keys0), "segment", 1)
    got2 = shifted(jnp.where(core == 0, keys1, features2), "segment", 1)
    handed, new_cache = collect(core_scalar, keys0, features1, keys1, features2, got1, got2)
    return (handed[None], new_cache[None])


def solution(mesh):
    in_specs = (
        P(None, "seq", "tp"),
        P("segment", None, None, "tp"),
        P("segment", "tp", None),
        P("segment", None, None),
        P("segment", None, None),
        P("segment", None, None, "seq", "tp"),
        P("segment", None, None),
        P("segment", None),
        P(),
    )
    out_specs = (P("segment", None, "seq", "tp"), P("segment", None, None, "seq", "tp"))
    return jax.shard_map(local, mesh=mesh, in_specs=in_specs, out_specs=out_specs, check_vma=False)
```

```python
import jax
import jax.numpy as jnp
from jax import lax
from jax.experimental import pallas as pl
from jax.experimental.pallas import tpu as pltpu
from jax.sharding import PartitionSpec as P

EPS = 1e-06
HEAD_DIM = 128
REACH = 3
MIB = 1024 * 1024
ON_CHIP = pl.BlockSpec(memory_space=pltpu.VMEM)
SCALARS = pl.BlockSpec(memory_space=pltpu.SMEM)
ANYWHERE = pl.BlockSpec(memory_space=pl.ANY)


def shifted(block, axis, distance):
    devices = range(lax.axis_size(axis))
    route = [((i - distance) % len(devices), i) for i in devices]
    return lax.ppermute(block, axis, route)


def after(values, *gates):
    return lax.optimization_barrier((values, gates))[0]


def params(mib):
    return pltpu.CompilerParams(vmem_limit_bytes=mib * MIB)


def struct(shape, dtype=jnp.bfloat16):
    return jax.ShapeDtypeStruct(shape, dtype)


def exchanged(tiles):
    group = tiles.shape[0]
    groups = [list(range(i, i + group)) for i in range(0, lax.axis_size("seq"), group)]
    return lax.all_to_all(tiles, "seq", 0, 0, axis_index_groups=groups)


def along_ring(block, distance, per_chip):
    size = lax.axis_size("seq")
    share = size // per_chip
    place = [per_chip * (i % share) + i // share for i in range(size)]
    route = [(place[(i + distance) % size], place[i]) for i in range(size)]
    return lax.ppermute(block, "seq", route)


def halve_kernel(core, stale, mine, theirs, sems):
    rows, cols = mine.shape[1], stale.shape[-1]
    copies = []
    for place, out in enumerate((mine, theirs)):
        first = core[0] if place == 0 else 1 - core[0]
        first = pl.multiple_of(first * rows, rows)
        for half in range(2):
            copies.append(
                pltpu.make_async_copy(
                    stale.at[half, :, pl.ds(first, rows)],
                    out.at[:, :, half * cols : (half + 1) * cols],
                    sems.at[2 * place + half],
                )
            )
    for copy in copies:
        copy.start()
    for copy in copies:
        copy.wait()


def halve(core, stale):
    _, patches, rows, cols = stale.shape
    return pl.pallas_call(
        halve_kernel,
        in_specs=[SCALARS, ANYWHERE],
        out_specs=[ON_CHIP] * 2,
        out_shape=[struct((patches, rows // 2, 2 * cols))] * 2,
        scratch_shapes=[pltpu.SemaphoreType.DMA((4,))],
        compiler_params=params(8),
        name="halve",
    )(core, stale)


def join_kernel(upper, lower, out, sems):
    rows = upper.shape[1]
    copies = [
        pltpu.make_async_copy(upper, out.at[:, :rows], sems.at[0]),
        pltpu.make_async_copy(lower, out.at[:, rows:], sems.at[1]),
    ]
    for copy in copies:
        copy.start()
    for copy in copies:
        copy.wait()


def join(upper, lower):
    tiles, rows, cols = upper.shape
    return pl.pallas_call(
        join_kernel,
        in_specs=[ANYWHERE] * 2,
        out_specs=ON_CHIP,
        out_shape=struct((tiles, 2 * rows, cols)),
        scratch_shapes=[pltpu.SemaphoreType.DMA((2,))],
        compiler_params=params(8),
        name="join",
    )(upper, lower)


def collect_kernel(core, early, late, got1, got2, handed, cache):
    rows, cols = got1.shape[1], cache.shape[-1]
    upper, lower = slice(0, rows), slice(rows, 2 * rows)

    def collect(features, keys):
        for half in range(2):
            here = slice(half * rows, (half + 1) * rows)
            ref, there = features[half]
            handed[:, here] = ref[:, there]
            ref, there = keys[half]
            for which in range(2):
                cache[which, :, here] = ref[:, there, which * cols : (which + 1) * cols]

    @pl.when(core[0] == 0)
    def _():
        collect(((late, lower), (got2, upper)), ((early, upper), (got1, upper)))

    @pl.when(core[0] == 1)
    def _():
        collect(((got1, upper), (early, lower)), ((got2, upper), (late, upper)))


def collect(core, early, late, got1, got2):
    patches, rows, cols = got1.shape
    return pl.pallas_call(
        collect_kernel,
        in_specs=[SCALARS] + [ON_CHIP] * 4,
        out_specs=[ON_CHIP] * 2,
        out_shape=[
            struct((patches, 2 * rows, cols)),
            struct((2, patches, 2 * rows, cols // 2)),
        ],
        compiler_params=params(8),
        name="collect",
    )(core, early, late, got1, got2)


def choose(meta, kv, stale, outs):
    tiles, rows, _ = kv.shape
    old = pl.ds(pl.multiple_of((1 - meta[1]) * rows, rows), rows)
    for place, out in enumerate(outs):
        first = tiles - REACH if place == 1 else 0
        cut = slice(first, first + out.shape[0])

        @pl.when(meta[2 + place] == 1)
        def _():
            out[...] = kv[cut]

        @pl.when(meta[2 + place] == 0)
        def _():
            out[...] = stale[cut, old]


def choose_kernel(meta, kv, stale, lo_out, hi_out, far_out):
    choose(meta, kv, stale, (lo_out, hi_out, far_out))


def payloads(kv_shape):
    edge = struct((REACH,) + kv_shape[1:])
    return [edge, edge, struct(kv_shape)]


def choose_alone(meta, kv, stale):
    return pl.pallas_call(
        choose_kernel,
        in_specs=[SCALARS] + [ON_CHIP] * 2,
        out_specs=[ON_CHIP] * 3,
        out_shape=payloads(kv.shape),
        compiler_params=params(8),
        name="choose",
    )(meta, kv, stale)


def project_kernel(meta, *refs, with_stale):
    blocks = refs[:4]
    shift, scale, gain, w_own, w_other = refs[4:9]
    refs = refs[9:]
    if with_stale:
        stale, q_out, kv_out, *outs = refs[:-4]
    else:
        q_out, kv_out = refs[:-4]
    xs, modded, weights, sems = refs[-4:]
    _, rows, cols = xs.shape
    tiles, rows_tile, kv_cols = kv_out.shape
    heads_cols = kv_cols // 2
    parts = shift.shape[0]
    width = cols * parts
    features = [lax.rem(meta[0] + j, parts) for j in (2, 1, 3, 0)]

    def fetch(j, source):
        first = pl.multiple_of(features[j] * cols, cols)
        return pltpu.make_async_copy(
            source.at[:, pl.ds(first, cols)],
            weights.at[:, j * cols : (j + 1) * cols],
            sems.at[j],
        )

    arriving = [
        pltpu.make_async_copy(blocks[j], xs.at[j], sems.at[parts + j]) for j in range(parts)
    ]
    for copy in arriving:
        copy.start()
    for chosen, source in enumerate((w_other, w_own)):

        @pl.when(meta[1] == chosen)
        def _():
            for j in range(parts):
                fetch(j, source).start()

    for copy in arriving:
        copy.wait()
    total = jnp.zeros((rows, 1), jnp.float32)
    for j in range(parts):
        total += jnp.sum(xs[j].astype(jnp.float32), axis=-1, keepdims=True)
    mean = total / width
    square = jnp.zeros((rows, 1), jnp.float32)
    for j in range(parts):
        centred = xs[j].astype(jnp.float32) - mean
        square += jnp.sum(centred * centred, axis=-1, keepdims=True)
    spread = lax.rsqrt(square / width + EPS)
    for j in range(parts):
        normed = (xs[j].astype(jnp.float32) - mean) * spread
        modded[:, j * cols : (j + 1) * cols] = (
            normed * (1.0 + scale[features[j]]) + shift[features[j]]
        ).astype(jnp.bfloat16)
    for j in range(parts):
        fetch(j, w_own).wait()

    for part in (1, 2, 0):
        product = jnp.dot(modded[...], weights[part], preferred_element_type=jnp.float32)
        if part == 2:
            kv_out[:, :, heads_cols:] = product.astype(jnp.bfloat16).reshape(
                tiles, rows_tile, heads_cols
            )
            continue
        for head in range(heads_cols // HEAD_DIM):
            cut = slice(head * HEAD_DIM, (head + 1) * HEAD_DIM)
            vec = product[:, cut]
            mean_sq = jnp.mean(vec * vec, axis=-1, keepdims=True)
            vec = vec * lax.rsqrt(mean_sq + EPS) * gain[part : part + 1]
            vec = vec.astype(jnp.bfloat16).reshape(tiles, rows_tile, HEAD_DIM)
            if part == 0:
                q_out[:, :, cut] = vec
            else:
                kv_out[:, :, cut] = vec
    if with_stale:
        choose(meta, kv_out, stale, outs)


def project(meta, blocks, shift, scale, gain, w_own, w_other, stale, kv_shape):
    rows, cols = blocks[0].shape
    tiles, rows_tile, kv_cols = kv_shape
    heads_cols = kv_cols // 2
    parts = shift.shape[0]
    shapes = [struct((tiles, rows_tile, heads_cols)), struct(kv_shape)]
    extra = []
    if stale is not None:
        shapes += payloads(kv_shape)
        extra = [stale]

    def kernel(*refs):
        project_kernel(*refs, with_stale=stale is not None)

    return pl.pallas_call(
        kernel,
        in_specs=[SCALARS]
        + [ANYWHERE] * len(blocks)
        + [ON_CHIP] * 3
        + [ANYWHERE] * 2
        + [ON_CHIP] * len(extra),
        out_specs=[ON_CHIP] * len(shapes),
        out_shape=shapes,
        scratch_shapes=[
            pltpu.VMEM((parts, rows, cols), jnp.bfloat16),
            pltpu.VMEM((rows, parts * cols), jnp.bfloat16),
            pltpu.VMEM((3, parts * cols, heads_cols), jnp.bfloat16),
            pltpu.SemaphoreType.DMA((2 * parts,)),
        ],
        compiler_params=params(52),
        name="project",
    )(meta, *blocks, shift, scale, gain, w_own, w_other, *extra)


def soften(queries, keys, values, times, floors):
    scores = [
        lax.dot_general(q, k, (((1,), (1,)), ((), ())), preferred_element_type=jnp.float32)
        for q, k in zip(queries, keys)
    ]
    scores = [
        jnp.where(count > 0.0, each * HEAD_DIM ** (-0.5), -1e30)
        for each, count in zip(scores, times)
    ]
    peaks = [jnp.max(each, axis=-1, keepdims=True) for each in scores]
    if floors is not None:
        peaks = [jnp.maximum(peak, floor) for peak, floor in zip(peaks, floors)]
    weights = [
        jnp.exp(each - peak) * count for each, peak, count in zip(scores, peaks, times)
    ]
    totals = [jnp.sum(each, axis=-1, keepdims=True) for each in weights]
    summed = [
        jnp.dot(each.astype(jnp.bfloat16), v, preferred_element_type=jnp.float32)
        for each, v in zip(weights, values)
    ]
    return peaks, totals, summed


def head_cuts(heads_cols):
    return [slice(first, first + HEAD_DIM) for first in range(0, heads_cols, HEAD_DIM)]


def packed(peaks, totals):
    lane = lax.broadcasted_iota(jnp.int32, (peaks[0].shape[0], HEAD_DIM), 1)
    out = jnp.zeros((peaks[0].shape[0], HEAD_DIM), jnp.float32)
    for head, (peak, total) in enumerate(zip(peaks, totals)):
        out = jnp.where(lane == head, peak, out)
        out = jnp.where(lane == 64 + head, total, out)
    return out


def attend_own_kernel(q_own, q_other, own, multiple, out):
    tiles, rows, heads_cols = q_own.shape
    cuts = head_cuts(heads_cols)
    for tile in range(tiles):
        first, last = max(0, tile - REACH), min(tiles, tile + REACH + 1)
        count = (last - first) * rows
        both = own[first:last].reshape(count, 2 * heads_cols)
        queries = jnp.concatenate([q_own[tile], q_other[tile]], axis=0)
        peaks, totals, summed = soften(
            [queries[:, cut] for cut in cuts],
            [both[:, cut] for cut in cuts],
            [both[:, heads_cols + cut.start : heads_cols + cut.stop] for cut in cuts],
            [multiple[tile, :, :count]] * len(cuts),
            None,
        )
        for cut, each in zip(cuts, summed):
            out[tile, :, cut] = each
        out[tile, :, heads_cols:] = packed(peaks, totals)


def attend_own(q_own, q_other, own, multiple):
    tiles, rows, heads_cols = q_own.shape
    return pl.pallas_call(
        attend_own_kernel,
        in_specs=[ON_CHIP] * 4,
        out_specs=ON_CHIP,
        out_shape=struct((tiles, 2 * rows, heads_cols + HEAD_DIM), jnp.float32),
        compiler_params=params(8),
        name="attend_own",
    )(q_own, q_other, own, multiple)


def attend_rest_kernel(q_own, q_other, below, above, far, multiple, before, out_own, out_other):
    tiles, rows, heads_cols = q_own.shape
    cuts = head_cuts(heads_cols)
    heads = len(cuts)
    for pair in range(0, tiles, 2):
        queries, keys, values, times, floors, earlier = [], [], [], [], [], []
        for tile in (pair, pair + 1):
            pieces = [below[place] for place in range(tile, REACH)]
            pieces += [above[place] for place in range(tile + REACH + 1 - tiles)]
            pieces += [far[tile]]
            both = jnp.concatenate(pieces, axis=0)
            asked = jnp.concatenate([q_own[tile], q_other[tile]], axis=0)
            extra = before[tile, :, heads_cols:]
            queries += [asked[:, cut] for cut in cuts]
            keys += [both[:, cut] for cut in cuts]
            values += [both[:, heads_cols + cut.start : heads_cols + cut.stop] for cut in cuts]
            times += [multiple[tile, :, : both.shape[0]]] * heads
            floors += [extra[:, head : head + 1] for head in range(heads)]
            earlier += [extra[:, 64 + head : 65 + head] for head in range(heads)]
        peaks, totals, summed = soften(queries, keys, values, times, floors)
        shrink = [jnp.exp(floor - peak) for floor, peak in zip(floors, peaks)]
        totals = [total + old * less for total, old, less in zip(totals, earlier, shrink)]
        for place, tile in enumerate((pair, pair + 1)):
            here = slice(place * heads, (place + 1) * heads)
            for cut, each, less in zip(cuts, summed[here], shrink[here]):
                result = each + before[tile, :, cut] * less
                out_own[tile, :, cut] = result[:rows]
                out_other[tile, :, cut] = result[rows:]
            extra = packed(peaks[here], totals[here])
            out_own[tile, :, heads_cols:] = extra[:rows]
            out_other[tile, :, heads_cols:] = extra[rows:]


def attend_rest(q_own, q_other, below, above, far, multiple, before):
    tiles, rows, heads_cols = q_own.shape
    return pl.pallas_call(
        attend_rest_kernel,
        in_specs=[ON_CHIP] * 7,
        out_specs=[ON_CHIP] * 2,
        out_shape=[struct((tiles, rows, heads_cols + HEAD_DIM), jnp.float32)] * 2,
        compiler_params=params(8),
        name="attend_rest",
    )(q_own, q_other, below, above, far, multiple, before)


def merge_kernel(part_a, part_b, att):
    tiles, rows, _ = part_a.shape
    heads_cols = att.shape[-1]
    extra_a = part_a[:, :, heads_cols:].reshape(tiles * rows, HEAD_DIM)
    extra_b = part_b[:, :, heads_cols:].reshape(tiles * rows, HEAD_DIM)
    for head, cut in enumerate(head_cuts(heads_cols)):
        peak_a, total_a = extra_a[:, head : head + 1], extra_a[:, 64 + head : 65 + head]
        peak_b, total_b = extra_b[:, head : head + 1], extra_b[:, 64 + head : 65 + head]
        peak = jnp.maximum(peak_a, peak_b)
        grow_a, grow_b = jnp.exp(peak_a - peak), jnp.exp(peak_b - peak)
        total = total_a * grow_a + total_b * grow_b
        summed_a = part_a[:, :, cut].reshape(tiles * rows, HEAD_DIM)
        summed_b = part_b[:, :, cut].reshape(tiles * rows, HEAD_DIM)
        att[:, cut] = (summed_a * (grow_a / total) + summed_b * (grow_b / total)).astype(
            jnp.bfloat16
        )


def merge(part_a, part_b):
    tiles, rows, cols = part_a.shape
    return pl.pallas_call(
        merge_kernel,
        in_specs=[ON_CHIP] * 2,
        out_specs=ON_CHIP,
        out_shape=struct((tiles * rows, cols - HEAD_DIM)),
        compiler_params=params(8),
        name="merge",
    )(part_a, part_b)


def output_kernel(meta, *refs):
    *refs, out, weights, sems = refs
    parts = weights.shape[0]
    atts, refs = refs[:parts], refs[parts:]
    own, other, (hidden, gates) = refs[:parts], refs[parts : 2 * parts], refs[2 * parts :]

    def fetch(j, sources):
        return pltpu.make_async_copy(sources[j], weights.at[j], sems.at[j])

    for chosen, sources in enumerate((other, own)):

        @pl.when(meta[1] == chosen)
        def _():
            for j in range(parts):
                fetch(j, sources).start()

    product = jnp.zeros(out.shape, jnp.float32)
    for j in range(parts):
        fetch(j, own).wait()
        product += jnp.dot(atts[j][...], weights[j], preferred_element_type=jnp.float32)
    out[...] = (hidden[...].astype(jnp.float32) + gates[meta[0]] * product).astype(out.dtype)


def output(meta, atts, own, other, hidden, gates):
    parts = len(atts)
    return pl.pallas_call(
        output_kernel,
        in_specs=[SCALARS] + [ON_CHIP] * parts + [ANYWHERE] * (2 * parts) + [ON_CHIP] * 2,
        out_specs=ON_CHIP,
        out_shape=struct(hidden.shape),
        scratch_shapes=[
            pltpu.VMEM((parts,) + own[0].shape, jnp.bfloat16),
            pltpu.SemaphoreType.DMA((parts,)),
        ],
        compiler_params=params(12),
        name="output",
    )(meta, *atts, *own, *other, hidden, gates)


def count_tiles(table, counts, chip, per_chip, repeat):
    tiles, slots = table.shape
    table = lax.dynamic_slice_in_dim(table, chip * per_chip, per_chip, 0)
    counts = lax.dynamic_slice_in_dim(counts, chip * per_chip, per_chip, 0)
    query_tiles = jnp.arange(per_chip, dtype=jnp.int32) + chip * per_chip
    across = tiles // 2 + (tiles // per_chip) // 2
    rows = []
    for tile in range(per_chip):
        first, last = max(0, tile - REACH), min(per_chip, tile + REACH + 1)
        own = [place - tile for place in range(first, last)]
        rest = [place - REACH - tile for place in range(tile, REACH)]
        rest += [per_chip + place - tile for place in range(tile + REACH + 1 - per_chip)]
        rest += [across]
        own = [d % tiles for d in own] + [-1] * (256 // repeat - len(own))
        rest = [d % tiles for d in rest] + [-1] * (128 // repeat - len(rest))
        rows.append([d for d in own + rest for _ in range(repeat)])
    reach = jnp.array(rows, jnp.int32)
    relative = (table - query_tiles[:, None]) % tiles
    live = jnp.arange(slots, dtype=jnp.int32)[None] < counts[:, None]
    hits = (relative[:, :, None] == reach[:, None]) & live[:, :, None]
    return jnp.sum(hits.astype(jnp.float32), axis=1)[:, None]


def gather_features(hidden):
    across = shifted(hidden, "tp", 2)
    return across, shifted(hidden, "tp", -1), shifted(hidden, "tp", 1), hidden


def local(
    latents, w_qkv, w_out, modulation, qk_gain, stale_cache, kv_tiles, tile_counts, patch_order
):
    core = lax.axis_index("segment")
    seq_size = lax.axis_size("seq")
    seq_pos = lax.axis_index("seq")
    tp_size = lax.axis_size("tp")
    tp_pos = lax.axis_index("tp")
    patches, patch_rows, part_cols = latents.shape
    rows_core = patch_rows // 2
    rows = patches * rows_core
    share = seq_size // patches
    chip = share * lax.rem(seq_pos, patches) + seq_pos // patches
    w_own = jnp.transpose(w_qkv[0], (1, 0, 2))
    heads_cols, width = w_out.shape[1:]
    head_dim = qk_gain.shape[-1]

    core_scalar = core.astype(jnp.int32)[None]
    mine = lax.dynamic_slice_in_dim(latents, core * rows_core, rows_core, 1)
    hidden = exchanged(mine).reshape(rows, part_cols)
    stale, stale_send = halve(core_scalar, after(stale_cache[0], mine))
    stale = join(stale, shifted(stale_send, "segment", 1))
    hidden, stale = lax.optimization_barrier((hidden, stale))
    w_other = shifted(w_own, "segment", 1)
    small_own = jnp.concatenate([modulation[0].reshape(-1), qk_gain[0].reshape(-1)])
    small_other = shifted(small_own, "segment", 1)
    kv_tiles, tile_counts = after((kv_tiles, tile_counts), small_other)
    turns = jnp.arange(patches, dtype=jnp.int32)
    asked = jnp.stack([chip, chip - 1, chip + 1, chip - seq_size // 2 - 1]) % seq_size // share
    ranks = jnp.sum(jnp.where(patch_order[None] == asked[:, None], turns[None], 0), axis=-1)
    fresh = (ranks[0] <= ranks[1:]).astype(jnp.int32)
    multiple_own = count_tiles(kv_tiles[0], tile_counts[0], chip, patches, rows_core)
    multiple_other = shifted(multiple_own, "segment", 1)
    given = []
    for section in range(2):
        is_own = core == section
        meta = jnp.concatenate(
            [jnp.stack([tp_pos, is_own.astype(tp_pos.dtype)]).astype(jnp.int32), fresh]
        )
        small = jnp.where(is_own, small_own, small_other)
        modul = small[: 3 * width].reshape(3, tp_size, 1, part_cols)
        gain = small[3 * width :].reshape(2, head_dim)
        multiple = jnp.where(is_own, multiple_own, multiple_other)
        given.append(
            (meta, modul[0], modul[1], modul[2], gain, multiple[..., :256], multiple[..., 256:])
        )
    slices = [
        lax.dynamic_slice_in_dim(
            w_out[0], lax.rem(tp_pos + j, tp_size) * part_cols, part_cols, 1
        )
        for j in range(tp_size)
    ]

    for section in range(2):
        blocks = gather_features(hidden)
        if section == 0:
            stale = exchanged(after(stale, blocks[0]))
            blocks, given, slices = lax.optimization_barrier((blocks, given, slices))
        else:
            early = join(kv, hidden.reshape(kv.shape))
            early = exchanged(after(early, blocks[0]))
            blocks, early = lax.optimization_barrier((blocks, early))
        meta, shift, scale, gates, gain, times_own, times_rest = given[section]
        q_own, kv, *going = project(
            meta,
            blocks,
            shift,
            scale,
            gain,
            w_own,
            w_other,
            stale if section > 0 else None,
            (patches, rows_core, 2 * heads_cols),
        )
        if section == 0:
            going = choose_alone(meta, kv, stale)
        to_below, to_above, to_far = going
        far = along_ring(to_far, seq_size // 2 + 1, patches)
        above = along_ring(to_below, 1, patches)
        below = along_ring(to_above, -1, patches)
        q_other = shifted(q_own, "segment", 1)
        if section == 0:
            slices = after(slices, q_other)
            wo_own = slices[:1] + [shifted(slices[j], "tp", j) for j in range(1, tp_size)]
        before = attend_own(q_own, q_other, kv, times_own)
        part_own, part_other = attend_rest(
            q_own, q_other, below, above, far, times_rest, before
        )
        part_back = shifted(part_other, "segment", 1)
        att = merge(part_own, part_back)
        across = shifted(att, "tp", 2)
        atts = [att, shifted(att, "tp", 1), across, shifted(att, "tp", 3)]
        if section == 0:
            wo_other = [shifted(piece, "segment", 1) for piece in after(wo_own, across)]
        hidden = output(meta, atts, wo_own, wo_other, hidden, gates)

    late = exchanged(join(kv, hidden.reshape(kv.shape)))
    keys, features = slice(0, rows_core), slice(rows_core, 2 * rows_core)
    got1 = shifted(jnp.where(core == 0, early[:, features], early[:, keys]), "segment", 1)
    got2 = shifted(jnp.where(core == 0, late[:, keys], late[:, features]), "segment", 1)
    handed, new_cache = collect(core_scalar, early, late, got1, got2)
    return (handed[None], new_cache[None])


def solution(mesh):
    in_specs = (
        P(None, "seq", "tp"),
        P("segment", None, None, "tp"),
        P("segment", "tp", None),
        P("segment", None, None),
        P("segment", None, None),
        P("segment", None, None, "seq", "tp"),
        P("segment", None, None),
        P("segment", None),
        P(),
    )
    out_specs = (P("segment", None, "seq", "tp"), P("segment", None, None, "seq", "tp"))
    return jax.shard_map(local, mesh=mesh, in_specs=in_specs, out_specs=out_specs, check_vma=False)
```

```python
import jax
import jax.numpy as jnp
from jax import lax
from jax.experimental import pallas as pl
from jax.experimental.pallas import tpu as pltpu
from jax.sharding import PartitionSpec as P

EPS = 1e-06
HEAD_DIM = 128
REACH = 3
MIB = 1024 * 1024
ON_CHIP = pl.BlockSpec(memory_space=pltpu.VMEM)
SCALARS = pl.BlockSpec(memory_space=pltpu.SMEM)
ANYWHERE = pl.BlockSpec(memory_space=pl.ANY)


def shifted(block, axis, distance):
    devices = range(lax.axis_size(axis))
    route = [((i - distance) % len(devices), i) for i in devices]
    return lax.ppermute(block, axis, route)


def after(values, *gates):
    return lax.optimization_barrier((values, gates))[0]


def params(mib):
    return pltpu.CompilerParams(vmem_limit_bytes=mib * MIB)


def struct(shape, dtype=jnp.bfloat16):
    return jax.ShapeDtypeStruct(shape, dtype)


def exchanged(tiles):
    group = tiles.shape[0]
    groups = [list(range(i, i + group)) for i in range(0, lax.axis_size("seq"), group)]
    return lax.all_to_all(tiles, "seq", 0, 0, axis_index_groups=groups)


def along_ring(block, distance, per_chip):
    size = lax.axis_size("seq")
    share = size // per_chip
    place = [per_chip * (i % share) + i // share for i in range(size)]
    route = [(place[(i + distance) % size], place[i]) for i in range(size)]
    return lax.ppermute(block, "seq", route)


def halve_kernel(core, stale, mine, theirs, sems):
    rows, cols = mine.shape[1], stale.shape[-1]
    copies = []
    for place, out in enumerate((mine, theirs)):
        first = core[0] if place == 0 else 1 - core[0]
        first = pl.multiple_of(first * rows, rows)
        for half in range(2):
            copies.append(
                pltpu.make_async_copy(
                    stale.at[half, :, pl.ds(first, rows)],
                    out.at[:, :, half * cols : (half + 1) * cols],
                    sems.at[2 * place + half],
                )
            )
    for copy in copies:
        copy.start()
    for copy in copies:
        copy.wait()


def halve(core, stale):
    _, patches, rows, cols = stale.shape
    return pl.pallas_call(
        halve_kernel,
        in_specs=[SCALARS, ANYWHERE],
        out_specs=[ON_CHIP] * 2,
        out_shape=[struct((patches, rows // 2, 2 * cols))] * 2,
        scratch_shapes=[pltpu.SemaphoreType.DMA((4,))],
        compiler_params=params(8),
        name="halve",
    )(core, stale)


def join_kernel(*refs):
    *parts, out, sems = refs
    rows = parts[0].shape[1]
    copies = [
        pltpu.make_async_copy(part, out.at[:, i * rows : (i + 1) * rows], sems.at[i])
        for i, part in enumerate(parts)
    ]
    for copy in copies:
        copy.start()
    for copy in copies:
        copy.wait()


def join(*parts):
    tiles, rows, cols = parts[0].shape
    return pl.pallas_call(
        join_kernel,
        in_specs=[ANYWHERE] * len(parts),
        out_specs=ON_CHIP,
        out_shape=struct((tiles, len(parts) * rows, cols)),
        scratch_shapes=[pltpu.SemaphoreType.DMA((len(parts),))],
        compiler_params=params(8),
        name="join",
    )(*parts)


def collect_kernel(core, early, got_early, late, got_late, handed, cache):
    rows, cols = early.shape[1], cache.shape[-1]
    features1, keys1, features2 = (slice(i * rows, (i + 1) * rows) for i in range(3))
    whole = slice(0, rows)

    def collect(features, keys):
        for half in range(2):
            here = slice(half * rows, (half + 1) * rows)
            ref, there = features[half]
            handed[:, here] = ref[:, there]
            ref, there = keys[half]
            for which in range(2):
                cache[which, :, here] = ref[:, there, which * cols : (which + 1) * cols]

    @pl.when(core[0] == 0)
    def _():
        collect(((late, features2), (got_late, features2)), ((early, whole), (got_early, whole)))

    @pl.when(core[0] == 1)
    def _():
        collect(((got_late, features1), (late, features1)), ((got_late, keys1), (late, keys1)))


def collect(core, early, got_early, late, got_late):
    patches, rows, cols = early.shape
    return pl.pallas_call(
        collect_kernel,
        in_specs=[SCALARS] + [ON_CHIP] * 4,
        out_specs=[ON_CHIP] * 2,
        out_shape=[
            struct((patches, 2 * rows, cols)),
            struct((2, patches, 2 * rows, cols // 2)),
        ],
        compiler_params=params(8),
        name="collect",
    )(core, early, got_early, late, got_late)


def choose(meta, kv, stale_own, stale_other, outs):
    tiles = kv.shape[0]
    for place, out in enumerate(outs):
        first = tiles - REACH if place == 1 else 0
        cut = slice(first, first + out.shape[0])
        fresh = meta[2 + place] == 1

        @pl.when(fresh)
        def _():
            out[...] = kv[cut]

        for chosen, stale in enumerate((stale_other, stale_own)):

            @pl.when(jnp.logical_not(fresh) & (meta[1] == chosen))
            def _():
                out[...] = stale[cut]


def choose_kernel(meta, kv, stale_own, stale_other, lo_out, hi_out, far_out):
    choose(meta, kv, stale_own, stale_other, (lo_out, hi_out, far_out))


def payloads(kv_shape):
    edge = struct((REACH,) + kv_shape[1:])
    return [edge, edge, struct(kv_shape)]


def choose_alone(meta, kv, stale):
    return pl.pallas_call(
        choose_kernel,
        in_specs=[SCALARS] + [ON_CHIP] * 3,
        out_specs=[ON_CHIP] * 3,
        out_shape=payloads(kv.shape),
        compiler_params=params(8),
        name="choose",
    )(meta, kv, *stale)


def project_kernel(meta, *refs, with_stale):
    blocks = refs[:4]
    shift, scale, gain, w_own, w_other = refs[4:9]
    refs = refs[9:]
    if with_stale:
        stale_own, stale_other, q_out, kv_out, *outs = refs[:-4]
    else:
        q_out, kv_out = refs[:-4]
    xs, modded, weights, sems = refs[-4:]
    _, rows, cols = xs.shape
    tiles, rows_tile, kv_cols = kv_out.shape
    heads_cols = kv_cols // 2
    parts = shift.shape[0]
    width = cols * parts
    features = [lax.rem(meta[0] + j, parts) for j in (2, 1, 3, 0)]

    def fetch(j, source):
        first = pl.multiple_of(features[j] * cols, cols)
        return pltpu.make_async_copy(
            source.at[:, pl.ds(first, cols)],
            weights.at[:, j * cols : (j + 1) * cols],
            sems.at[j],
        )

    arriving = [
        pltpu.make_async_copy(blocks[j], xs.at[j], sems.at[parts + j]) for j in range(parts)
    ]
    for copy in arriving:
        copy.start()
    for chosen, source in enumerate((w_other, w_own)):

        @pl.when(meta[1] == chosen)
        def _():
            for j in range(parts):
                fetch(j, source).start()

    for copy in arriving:
        copy.wait()
    total = jnp.zeros((rows, 1), jnp.float32)
    for j in range(parts):
        total += jnp.sum(xs[j].astype(jnp.float32), axis=-1, keepdims=True)
    mean = total / width
    square = jnp.zeros((rows, 1), jnp.float32)
    for j in range(parts):
        centred = xs[j].astype(jnp.float32) - mean
        square += jnp.sum(centred * centred, axis=-1, keepdims=True)
    spread = lax.rsqrt(square / width + EPS)
    for j in range(parts):
        normed = (xs[j].astype(jnp.float32) - mean) * spread
        modded[:, j * cols : (j + 1) * cols] = (
            normed * (1.0 + scale[features[j]]) + shift[features[j]]
        ).astype(jnp.bfloat16)
    for j in range(parts):
        fetch(j, w_own).wait()

    for part in (1, 2, 0):
        product = jnp.dot(modded[...], weights[part], preferred_element_type=jnp.float32)
        if part == 2:
            kv_out[:, :, heads_cols:] = product.astype(jnp.bfloat16).reshape(
                tiles, rows_tile, heads_cols
            )
            continue
        for head in range(heads_cols // HEAD_DIM):
            cut = slice(head * HEAD_DIM, (head + 1) * HEAD_DIM)
            vec = product[:, cut]
            mean_sq = jnp.mean(vec * vec, axis=-1, keepdims=True)
            vec = vec * lax.rsqrt(mean_sq + EPS) * gain[part : part + 1]
            vec = vec.astype(jnp.bfloat16).reshape(tiles, rows_tile, HEAD_DIM)
            if part == 0:
                q_out[:, :, cut] = vec
            else:
                kv_out[:, :, cut] = vec
    if with_stale:
        choose(meta, kv_out, stale_own, stale_other, outs)


def project(meta, blocks, shift, scale, gain, w_own, w_other, stale, kv_shape):
    rows, cols = blocks[0].shape
    tiles, rows_tile, kv_cols = kv_shape
    heads_cols = kv_cols // 2
    parts = shift.shape[0]
    shapes = [struct((tiles, rows_tile, heads_cols)), struct(kv_shape)]
    extra = []
    if stale is not None:
        shapes += payloads(kv_shape)
        extra = list(stale)

    def kernel(*refs):
        project_kernel(*refs, with_stale=stale is not None)

    return pl.pallas_call(
        kernel,
        in_specs=[SCALARS]
        + [ANYWHERE] * len(blocks)
        + [ON_CHIP] * 3
        + [ANYWHERE] * 2
        + [ON_CHIP] * len(extra),
        out_specs=[ON_CHIP] * len(shapes),
        out_shape=shapes,
        scratch_shapes=[
            pltpu.VMEM((parts, rows, cols), jnp.bfloat16),
            pltpu.VMEM((rows, parts * cols), jnp.bfloat16),
            pltpu.VMEM((3, parts * cols, heads_cols), jnp.bfloat16),
            pltpu.SemaphoreType.DMA((2 * parts,)),
        ],
        compiler_params=params(52),
        name="project",
    )(meta, *blocks, shift, scale, gain, w_own, w_other, *extra)


def soften(queries, keys, values, times, floors):
    scores = [
        lax.dot_general(q, k, (((1,), (1,)), ((), ())), preferred_element_type=jnp.float32)
        for q, k in zip(queries, keys)
    ]
    scores = [
        jnp.where(count > 0.0, each * HEAD_DIM ** (-0.5), -1e30)
        for each, count in zip(scores, times)
    ]
    peaks = [jnp.max(each, axis=-1, keepdims=True) for each in scores]
    if floors is not None:
        peaks = [jnp.maximum(peak, floor) for peak, floor in zip(peaks, floors)]
    weights = [
        jnp.exp(each - peak) * count for each, peak, count in zip(scores, peaks, times)
    ]
    totals = [jnp.sum(each, axis=-1, keepdims=True) for each in weights]
    summed = [
        jnp.dot(each.astype(jnp.bfloat16), v, preferred_element_type=jnp.float32)
        for each, v in zip(weights, values)
    ]
    return peaks, totals, summed


def head_cuts(heads_cols):
    return [slice(first, first + HEAD_DIM) for first in range(0, heads_cols, HEAD_DIM)]


def packed(peaks, totals):
    lane = lax.broadcasted_iota(jnp.int32, (peaks[0].shape[0], HEAD_DIM), 1)
    out = jnp.zeros((peaks[0].shape[0], HEAD_DIM), jnp.float32)
    for head, (peak, total) in enumerate(zip(peaks, totals)):
        out = jnp.where(lane == head, peak, out)
        out = jnp.where(lane == 64 + head, total, out)
    return out


def attend_own_kernel(q_own, q_other, own, multiple, out):
    tiles, rows, heads_cols = q_own.shape
    cuts = head_cuts(heads_cols)
    for tile in range(tiles):
        first, last = max(0, tile - REACH), min(tiles, tile + REACH + 1)
        count = (last - first) * rows
        both = own[first:last].reshape(count, 2 * heads_cols)
        queries = jnp.concatenate([q_own[tile], q_other[tile]], axis=0)
        peaks, totals, summed = soften(
            [queries[:, cut] for cut in cuts],
            [both[:, cut] for cut in cuts],
            [both[:, heads_cols + cut.start : heads_cols + cut.stop] for cut in cuts],
            [multiple[tile, :, :count]] * len(cuts),
            None,
        )
        for cut, each in zip(cuts, summed):
            out[tile, :, cut] = each
        out[tile, :, heads_cols:] = packed(peaks, totals)


def attend_own(q_own, q_other, own, multiple):
    tiles, rows, heads_cols = q_own.shape
    return pl.pallas_call(
        attend_own_kernel,
        in_specs=[ON_CHIP] * 4,
        out_specs=ON_CHIP,
        out_shape=struct((tiles, 2 * rows, heads_cols + HEAD_DIM), jnp.float32),
        compiler_params=params(8),
        name="attend_own",
    )(q_own, q_other, own, multiple)


def attend_rest_kernel(q_own, q_other, below, above, far, multiple, before, out_own, out_other):
    tiles, rows, heads_cols = q_own.shape
    cuts = head_cuts(heads_cols)
    heads = len(cuts)
    for pair in range(0, tiles, 2):
        queries, keys, values, times, floors, earlier = [], [], [], [], [], []
        for tile in (pair, pair + 1):
            pieces = [below[place] for place in range(tile, REACH)]
            pieces += [above[place] for place in range(tile + REACH + 1 - tiles)]
            pieces += [far[tile]]
            both = jnp.concatenate(pieces, axis=0)
            asked = jnp.concatenate([q_own[tile], q_other[tile]], axis=0)
            extra = before[tile, :, heads_cols:]
            queries += [asked[:, cut] for cut in cuts]
            keys += [both[:, cut] for cut in cuts]
            values += [both[:, heads_cols + cut.start : heads_cols + cut.stop] for cut in cuts]
            times += [multiple[tile, :, : both.shape[0]]] * heads
            floors += [extra[:, head : head + 1] for head in range(heads)]
            earlier += [extra[:, 64 + head : 65 + head] for head in range(heads)]
        peaks, totals, summed = soften(queries, keys, values, times, floors)
        shrink = [jnp.exp(floor - peak) for floor, peak in zip(floors, peaks)]
        totals = [total + old * less for total, old, less in zip(totals, earlier, shrink)]
        for place, tile in enumerate((pair, pair + 1)):
            here = slice(place * heads, (place + 1) * heads)
            for cut, each, less in zip(cuts, summed[here], shrink[here]):
                result = each + before[tile, :, cut] * less
                out_own[tile, :, cut] = result[:rows]
                out_other[tile, :, cut] = result[rows:]
            extra = packed(peaks[here], totals[here])
            out_own[tile, :, heads_cols:] = extra[:rows]
            out_other[tile, :, heads_cols:] = extra[rows:]


def attend_rest(q_own, q_other, below, above, far, multiple, before):
    tiles, rows, heads_cols = q_own.shape
    return pl.pallas_call(
        attend_rest_kernel,
        in_specs=[ON_CHIP] * 7,
        out_specs=[ON_CHIP] * 2,
        out_shape=[struct((tiles, rows, heads_cols + HEAD_DIM), jnp.float32)] * 2,
        compiler_params=params(8),
        name="attend_rest",
    )(q_own, q_other, below, above, far, multiple, before)


def merge_kernel(part_a, part_b, att):
    tiles, rows, _ = part_a.shape
    heads_cols = att.shape[-1]
    extra_a = part_a[:, :, heads_cols:].reshape(tiles * rows, HEAD_DIM)
    extra_b = part_b[:, :, heads_cols:].reshape(tiles * rows, HEAD_DIM)
    for head, cut in enumerate(head_cuts(heads_cols)):
        peak_a, total_a = extra_a[:, head : head + 1], extra_a[:, 64 + head : 65 + head]
        peak_b, total_b = extra_b[:, head : head + 1], extra_b[:, 64 + head : 65 + head]
        peak = jnp.maximum(peak_a, peak_b)
        grow_a, grow_b = jnp.exp(peak_a - peak), jnp.exp(peak_b - peak)
        total = total_a * grow_a + total_b * grow_b
        summed_a = part_a[:, :, cut].reshape(tiles * rows, HEAD_DIM)
        summed_b = part_b[:, :, cut].reshape(tiles * rows, HEAD_DIM)
        att[:, cut] = (summed_a * (grow_a / total) + summed_b * (grow_b / total)).astype(
            jnp.bfloat16
        )


def merge(part_a, part_b):
    tiles, rows, cols = part_a.shape
    return pl.pallas_call(
        merge_kernel,
        in_specs=[ON_CHIP] * 2,
        out_specs=ON_CHIP,
        out_shape=struct((tiles * rows, cols - HEAD_DIM)),
        compiler_params=params(8),
        name="merge",
    )(part_a, part_b)


def output_kernel(meta, *refs):
    atts, own, other = refs[:4], refs[4:6], refs[6:8]
    hidden, gates, out, weights, sems = refs[8:]
    rows = atts[0].shape[1]

    def fetch(pair, sources):
        return pltpu.make_async_copy(sources[pair], weights.at[pair], sems.at[pair])

    for chosen, sources in enumerate((other, own)):

        @pl.when(meta[1] == chosen)
        def _():
            for pair in range(2):
                fetch(pair, sources).start()

    product = jnp.zeros(out.shape, jnp.float32)
    for j, att in enumerate(atts):
        if j % 2 == 0:
            fetch(j // 2, own).wait()
        weight = weights[j // 2, (j % 2) * rows : (j % 2 + 1) * rows]
        product += jnp.dot(att[...], weight, preferred_element_type=jnp.float32)
    out[...] = (hidden[...].astype(jnp.float32) + gates[meta[0]] * product).astype(out.dtype)


def output(meta, atts, own, other, hidden, gates):
    return pl.pallas_call(
        output_kernel,
        in_specs=[SCALARS] + [ON_CHIP] * 4 + [ANYWHERE] * 4 + [ON_CHIP] * 2,
        out_specs=ON_CHIP,
        out_shape=struct(hidden.shape),
        scratch_shapes=[
            pltpu.VMEM((2,) + own[0].shape, jnp.bfloat16),
            pltpu.SemaphoreType.DMA((2,)),
        ],
        compiler_params=params(12),
        name="output",
    )(meta, *atts, *own, *other, hidden, gates)


def paired(first, second):
    rows, cols = first.shape
    return join(first[None], second[None]).reshape(2 * rows, cols)


def count_tiles(table, counts, chip, per_chip, repeat):
    tiles, slots = table.shape
    table = lax.dynamic_slice_in_dim(table, chip * per_chip, per_chip, 0)
    counts = lax.dynamic_slice_in_dim(counts, chip * per_chip, per_chip, 0)
    query_tiles = jnp.arange(per_chip, dtype=jnp.int32) + chip * per_chip
    across = tiles // 2 + (tiles // per_chip) // 2
    rows = []
    for tile in range(per_chip):
        first, last = max(0, tile - REACH), min(per_chip, tile + REACH + 1)
        own = [place - tile for place in range(first, last)]
        rest = [place - REACH - tile for place in range(tile, REACH)]
        rest += [per_chip + place - tile for place in range(tile + REACH + 1 - per_chip)]
        rest += [across]
        own = [d % tiles for d in own] + [-1] * (256 // repeat - len(own))
        rest = [d % tiles for d in rest] + [-1] * (128 // repeat - len(rest))
        rows.append([d for d in own + rest for _ in range(repeat)])
    reach = jnp.array(rows, jnp.int32)
    relative = (table - query_tiles[:, None]) % tiles
    live = jnp.arange(slots, dtype=jnp.int32)[None] < counts[:, None]
    hits = (relative[:, :, None] == reach[:, None]) & live[:, :, None]
    return jnp.sum(hits.astype(jnp.float32), axis=1)[:, None]


def gather_features(hidden):
    across = shifted(hidden, "tp", 2)
    return across, shifted(hidden, "tp", -1), shifted(hidden, "tp", 1), hidden


def local(
    latents, w_qkv, w_out, modulation, qk_gain, stale_cache, kv_tiles, tile_counts, patch_order
):
    core = lax.axis_index("segment")
    seq_size = lax.axis_size("seq")
    seq_pos = lax.axis_index("seq")
    tp_size = lax.axis_size("tp")
    tp_pos = lax.axis_index("tp")
    patches, patch_rows, part_cols = latents.shape
    rows_core = patch_rows // 2
    rows = patches * rows_core
    share = seq_size // patches
    chip = share * lax.rem(seq_pos, patches) + seq_pos // patches
    w_own = jnp.transpose(w_qkv[0], (1, 0, 2))
    heads_cols, width = w_out.shape[1:]
    head_dim = qk_gain.shape[-1]

    core_scalar = core.astype(jnp.int32)[None]
    mine = lax.dynamic_slice_in_dim(latents, core * rows_core, rows_core, 1)
    hidden = exchanged(mine).reshape(rows, part_cols)
    stale_own, stale_send = halve(core_scalar, after(stale_cache[0], mine))
    stale_other = shifted(stale_send, "segment", 1)

    def columns(j):
        first = lax.rem(tp_pos + j, tp_size) * part_cols
        return lax.dynamic_slice_in_dim(w_out[0], first, part_cols, 1)

    wo_across = shifted(columns(2), "tp", 2)
    hidden, stale_own, stale_other, wo_across = lax.optimization_barrier(
        (hidden, stale_own, stale_other, wo_across)
    )
    w_other = shifted(w_own, "segment", 1)
    small_own = jnp.concatenate([modulation[0].reshape(-1), qk_gain[0].reshape(-1)])
    small_other = shifted(small_own, "segment", 1)
    kv_tiles, tile_counts = after((kv_tiles, tile_counts), small_other)
    turns = jnp.arange(patches, dtype=jnp.int32)
    asked = jnp.stack([chip, chip - 1, chip + 1, chip - seq_size // 2 - 1]) % seq_size // share
    ranks = jnp.sum(jnp.where(patch_order[None] == asked[:, None], turns[None], 0), axis=-1)
    fresh = (ranks[0] <= ranks[1:]).astype(jnp.int32)
    multiple_own = count_tiles(kv_tiles[0], tile_counts[0], chip, patches, rows_core)
    multiple_other = shifted(multiple_own, "segment", 1)
    given = []
    for section in range(2):
        is_own = core == section
        meta = jnp.concatenate(
            [jnp.stack([tp_pos, is_own.astype(tp_pos.dtype)]).astype(jnp.int32), fresh]
        )
        small = jnp.where(is_own, small_own, small_other)
        modul = small[: 3 * width].reshape(3, tp_size, 1, part_cols)
        gain = small[3 * width :].reshape(2, head_dim)
        multiple = jnp.where(is_own, multiple_own, multiple_other)
        given.append(
            (meta, modul[0], modul[1], modul[2], gain, multiple[..., :256], multiple[..., 256:])
        )
    slices = [columns(j) for j in (1, 3)]
    wo_own = [paired(columns(0), wo_across)]
    wo_other = [shifted(wo_own[0], "segment", 1)]

    for section in range(2):
        blocks = gather_features(hidden)
        if section == 0:
            stale = [exchanged(each) for each in after([stale_own, stale_other], blocks[0])]
            blocks, given, slices, wo_other = lax.optimization_barrier(
                (blocks, given, slices, wo_other)
            )
        else:
            early = exchanged(after(kv, blocks[0]))
            blocks, early = lax.optimization_barrier((blocks, early))
            hidden1 = hidden.reshape(kv.shape)
        meta, shift, scale, gates, gain, times_own, times_rest = given[section]
        q_own, kv, *going = project(
            meta,
            blocks,
            shift,
            scale,
            gain,
            w_own,
            w_other,
            stale if section > 0 else None,
            (patches, rows_core, 2 * heads_cols),
        )
        if section == 0:
            going = choose_alone(meta, kv, stale)
        to_below, to_above, to_far = going
        far = along_ring(to_far, seq_size // 2 + 1, patches)
        above = along_ring(to_below, 1, patches)
        below = along_ring(to_above, -1, patches)
        q_other = shifted(q_own, "segment", 1)
        if section == 0:
            wo_prev, wo_next = after(slices, q_other)
            wo_prev, wo_next = shifted(wo_prev, "tp", 1), shifted(wo_next, "tp", 3)
            far, wo_prev, wo_next = lax.optimization_barrier((far, wo_prev, wo_next))
            wo_own.append(paired(wo_prev, wo_next))
        before = attend_own(q_own, q_other, kv, times_own)
        part_own, part_other = attend_rest(
            q_own, q_other, below, above, far, times_rest, before
        )
        part_back = shifted(part_other, "segment", 1)
        if section == 0:
            wo_other.append(shifted(after(wo_own[1], part_back), "segment", 1))
        att = merge(part_own, part_back)
        across = shifted(att, "tp", 2)
        atts = [att, across, shifted(att, "tp", 1), shifted(att, "tp", 3)]
        hidden = output(meta, atts, wo_own, wo_other, hidden, gates)

    late = exchanged(join(hidden1, kv, hidden.reshape(kv.shape)))
    got_early, got_late = shifted(early, "segment", 1), shifted(late, "segment", 1)
    handed, new_cache = collect(core_scalar, early, got_early, late, got_late)
    return (handed[None], new_cache[None])


def solution(mesh):
    in_specs = (
        P(None, "seq", "tp"),
        P("segment", None, None, "tp"),
        P("segment", "tp", None),
        P("segment", None, None),
        P("segment", None, None),
        P("segment", None, None, "seq", "tp"),
        P("segment", None, None),
        P("segment", None),
        P(),
    )
    out_specs = (P("segment", None, "seq", "tp"), P("segment", None, None, "seq", "tp"))
    return jax.shard_map(local, mesh=mesh, in_specs=in_specs, out_specs=out_specs, check_vma=False)
```

```python
import jax
import jax.numpy as jnp
from jax import lax
from jax.experimental import pallas as pl
from jax.experimental.pallas import tpu as pltpu
from jax.sharding import PartitionSpec as P

EPS = 1e-06
HEAD_DIM = 128
REACH = 3
MIB = 1024 * 1024
ON_CHIP = pl.BlockSpec(memory_space=pltpu.VMEM)
SCALARS = pl.BlockSpec(memory_space=pltpu.SMEM)
ANYWHERE = pl.BlockSpec(memory_space=pl.ANY)


def shifted(block, axis, distance):
    devices = range(lax.axis_size(axis))
    route = [((i - distance) % len(devices), i) for i in devices]
    return lax.ppermute(block, axis, route)


def after(values, *gates):
    return lax.optimization_barrier((values, gates))[0]


def params(mib):
    return pltpu.CompilerParams(vmem_limit_bytes=mib * MIB)


def struct(shape, dtype=jnp.bfloat16):
    return jax.ShapeDtypeStruct(shape, dtype)


def exchanged(tiles):
    group = tiles.shape[0]
    groups = [list(range(i, i + group)) for i in range(0, lax.axis_size("seq"), group)]
    return lax.all_to_all(tiles, "seq", 0, 0, axis_index_groups=groups)


def along_ring(block, distance, per_chip):
    size = lax.axis_size("seq")
    share = size // per_chip
    place = [per_chip * (i % share) + i // share for i in range(size)]
    route = [(place[(i + distance) % size], place[i]) for i in range(size)]
    return lax.ppermute(block, "seq", route)


def halve_kernel(core, stale, mine, theirs, sems):
    rows, cols = mine.shape[1], stale.shape[-1]
    copies = []
    for place, out in enumerate((mine, theirs)):
        first = core[0] if place == 0 else 1 - core[0]
        first = pl.multiple_of(first * rows, rows)
        for half in range(2):
            copies.append(
                pltpu.make_async_copy(
                    stale.at[half, :, pl.ds(first, rows)],
                    out.at[:, :, half * cols : (half + 1) * cols],
                    sems.at[2 * place + half],
                )
            )
    for copy in copies:
        copy.start()
    for copy in copies:
        copy.wait()


def halve(core, stale):
    _, patches, rows, cols = stale.shape
    return pl.pallas_call(
        halve_kernel,
        in_specs=[SCALARS, ANYWHERE],
        out_specs=[ON_CHIP] * 2,
        out_shape=[struct((patches, rows // 2, 2 * cols))] * 2,
        scratch_shapes=[pltpu.SemaphoreType.DMA((4,))],
        compiler_params=params(8),
        name="halve",
    )(core, stale)


def join_kernel(*refs):
    *parts, out, sems = refs
    rows = parts[0].shape[1]
    copies = [
        pltpu.make_async_copy(part, out.at[:, i * rows : (i + 1) * rows], sems.at[i])
        for i, part in enumerate(parts)
    ]
    for copy in copies:
        copy.start()
    for copy in copies:
        copy.wait()


def join(*parts):
    tiles, rows, cols = parts[0].shape
    return pl.pallas_call(
        join_kernel,
        in_specs=[ANYWHERE] * len(parts),
        out_specs=ON_CHIP,
        out_shape=struct((tiles, len(parts) * rows, cols)),
        scratch_shapes=[pltpu.SemaphoreType.DMA((len(parts),))],
        compiler_params=params(8),
        name="join",
    )(*parts)


def collect_kernel(core, home, got, handed, cache):
    rows, cols = home.shape[1] // 4, cache.shape[-1]
    features1, keys1, features2, keys0 = (slice(i * rows, (i + 1) * rows) for i in range(4))

    def collect(features, keys, refs):
        for half, ref in enumerate(refs):
            here = slice(half * rows, (half + 1) * rows)
            handed[:, here] = ref[:, features]
            for which in range(2):
                cache[which, :, here] = ref[:, keys, which * cols : (which + 1) * cols]

    @pl.when(core[0] == 0)
    def _():
        collect(features2, keys0, (home, got))

    @pl.when(core[0] == 1)
    def _():
        collect(features1, keys1, (got, home))


def collect(core, home, got):
    patches, rows, cols = home.shape
    return pl.pallas_call(
        collect_kernel,
        in_specs=[SCALARS] + [ON_CHIP] * 2,
        out_specs=[ON_CHIP] * 2,
        out_shape=[
            struct((patches, rows // 2, cols)),
            struct((2, patches, rows // 2, cols // 2)),
        ],
        compiler_params=params(8),
        name="collect",
    )(core, home, got)


def choose(meta, kv, stale, outs):
    tiles, rows, _ = kv.shape
    old = pl.ds(pl.multiple_of((1 - meta[1]) * rows, rows), rows)
    for place, out in enumerate(outs):
        first = tiles - REACH if place == 1 else 0
        cut = slice(first, first + out.shape[0])

        @pl.when(meta[2 + place] == 1)
        def _():
            out[...] = kv[cut]

        @pl.when(meta[2 + place] == 0)
        def _():
            out[...] = stale[cut, old]


def choose_kernel(meta, kv, stale, lo_out, hi_out, far_out):
    choose(meta, kv, stale, (lo_out, hi_out, far_out))


def payloads(kv_shape):
    edge = struct((REACH,) + kv_shape[1:])
    return [edge, edge, struct(kv_shape)]


def choose_alone(meta, kv, stale):
    return pl.pallas_call(
        choose_kernel,
        in_specs=[SCALARS] + [ON_CHIP] * 2,
        out_specs=[ON_CHIP] * 3,
        out_shape=payloads(kv.shape),
        compiler_params=params(8),
        name="choose",
    )(meta, kv, stale)


def project_kernel(meta, *refs, with_stale):
    blocks = refs[:4]
    shift, scale, gain, w_own, w_other = refs[4:9]
    refs = refs[9:]
    if with_stale:
        stale, q_out, kv_out, *outs = refs[:-4]
    else:
        q_out, kv_out = refs[:-4]
    xs, modded, weights, sems = refs[-4:]
    _, rows, cols = xs.shape
    tiles, rows_tile, kv_cols = kv_out.shape
    heads_cols = kv_cols // 2
    parts = shift.shape[0]
    width = cols * parts
    features = [lax.rem(meta[0] + j, parts) for j in (2, 1, 3, 0)]

    def fetch(j, source):
        first = pl.multiple_of(features[j] * cols, cols)
        return pltpu.make_async_copy(
            source.at[:, pl.ds(first, cols)],
            weights.at[:, j * cols : (j + 1) * cols],
            sems.at[j],
        )

    arriving = [
        pltpu.make_async_copy(blocks[j], xs.at[j], sems.at[parts + j]) for j in range(parts)
    ]
    for copy in arriving:
        copy.start()
    for chosen, source in enumerate((w_other, w_own)):

        @pl.when(meta[1] == chosen)
        def _():
            for j in range(parts):
                fetch(j, source).start()

    for copy in arriving:
        copy.wait()
    total = jnp.zeros((rows, 1), jnp.float32)
    for j in range(parts):
        total += jnp.sum(xs[j].astype(jnp.float32), axis=-1, keepdims=True)
    mean = total / width
    square = jnp.zeros((rows, 1), jnp.float32)
    for j in range(parts):
        centred = xs[j].astype(jnp.float32) - mean
        square += jnp.sum(centred * centred, axis=-1, keepdims=True)
    spread = lax.rsqrt(square / width + EPS)
    for j in range(parts):
        normed = (xs[j].astype(jnp.float32) - mean) * spread
        modded[:, j * cols : (j + 1) * cols] = (
            normed * (1.0 + scale[features[j]]) + shift[features[j]]
        ).astype(jnp.bfloat16)
    for j in range(parts):
        fetch(j, w_own).wait()

    for part in (1, 2, 0):
        product = jnp.dot(modded[...], weights[part], preferred_element_type=jnp.float32)
        if part == 2:
            kv_out[:, :, heads_cols:] = product.astype(jnp.bfloat16).reshape(
                tiles, rows_tile, heads_cols
            )
            continue
        for head in range(heads_cols // HEAD_DIM):
            cut = slice(head * HEAD_DIM, (head + 1) * HEAD_DIM)
            vec = product[:, cut]
            mean_sq = jnp.mean(vec * vec, axis=-1, keepdims=True)
            vec = vec * lax.rsqrt(mean_sq + EPS) * gain[part : part + 1]
            vec = vec.astype(jnp.bfloat16).reshape(tiles, rows_tile, HEAD_DIM)
            if part == 0:
                q_out[:, :, cut] = vec
            else:
                kv_out[:, :, cut] = vec
    if with_stale:
        choose(meta, kv_out, stale, outs)


def project(meta, blocks, shift, scale, gain, w_own, w_other, stale, kv_shape):
    rows, cols = blocks[0].shape
    tiles, rows_tile, kv_cols = kv_shape
    heads_cols = kv_cols // 2
    parts = shift.shape[0]
    shapes = [struct((tiles, rows_tile, heads_cols)), struct(kv_shape)]
    extra = []
    if stale is not None:
        shapes += payloads(kv_shape)
        extra = [stale]

    def kernel(*refs):
        project_kernel(*refs, with_stale=stale is not None)

    return pl.pallas_call(
        kernel,
        in_specs=[SCALARS]
        + [ANYWHERE] * len(blocks)
        + [ON_CHIP] * 3
        + [ANYWHERE] * 2
        + [ON_CHIP] * len(extra),
        out_specs=[ON_CHIP] * len(shapes),
        out_shape=shapes,
        scratch_shapes=[
            pltpu.VMEM((parts, rows, cols), jnp.bfloat16),
            pltpu.VMEM((rows, parts * cols), jnp.bfloat16),
            pltpu.VMEM((3, parts * cols, heads_cols), jnp.bfloat16),
            pltpu.SemaphoreType.DMA((2 * parts,)),
        ],
        compiler_params=params(52),
        name="project",
    )(meta, *blocks, shift, scale, gain, w_own, w_other, *extra)


def soften(queries, keys, values, times, floors):
    scores = [
        lax.dot_general(q, k, (((1,), (1,)), ((), ())), preferred_element_type=jnp.float32)
        for q, k in zip(queries, keys)
    ]
    scores = [
        jnp.where(count > 0.0, each * HEAD_DIM ** (-0.5), -1e30)
        for each, count in zip(scores, times)
    ]
    peaks = [jnp.max(each, axis=-1, keepdims=True) for each in scores]
    if floors is not None:
        peaks = [jnp.maximum(peak, floor) for peak, floor in zip(peaks, floors)]
    weights = [
        jnp.exp(each - peak) * count for each, peak, count in zip(scores, peaks, times)
    ]
    totals = [jnp.sum(each, axis=-1, keepdims=True) for each in weights]
    summed = [
        jnp.dot(each.astype(jnp.bfloat16), v, preferred_element_type=jnp.float32)
        for each, v in zip(weights, values)
    ]
    return peaks, totals, summed


def head_cuts(heads_cols):
    return [slice(first, first + HEAD_DIM) for first in range(0, heads_cols, HEAD_DIM)]


def packed(peaks, totals):
    lane = lax.broadcasted_iota(jnp.int32, (peaks[0].shape[0], HEAD_DIM), 1)
    out = jnp.zeros((peaks[0].shape[0], HEAD_DIM), jnp.float32)
    for head, (peak, total) in enumerate(zip(peaks, totals)):
        out = jnp.where(lane == head, peak, out)
        out = jnp.where(lane == 64 + head, total, out)
    return out


def attend_own_kernel(q_own, q_other, own, multiple, out):
    tiles, rows, heads_cols = q_own.shape
    cuts = head_cuts(heads_cols)
    for tile in range(tiles):
        first, last = max(0, tile - REACH), min(tiles, tile + REACH + 1)
        count = (last - first) * rows
        both = own[first:last].reshape(count, 2 * heads_cols)
        queries = jnp.concatenate([q_own[tile], q_other[tile]], axis=0)
        peaks, totals, summed = soften(
            [queries[:, cut] for cut in cuts],
            [both[:, cut] for cut in cuts],
            [both[:, heads_cols + cut.start : heads_cols + cut.stop] for cut in cuts],
            [multiple[tile, :, :count]] * len(cuts),
            None,
        )
        for cut, each in zip(cuts, summed):
            out[tile, :, cut] = each
        out[tile, :, heads_cols:] = packed(peaks, totals)


def attend_own(q_own, q_other, own, multiple):
    tiles, rows, heads_cols = q_own.shape
    return pl.pallas_call(
        attend_own_kernel,
        in_specs=[ON_CHIP] * 4,
        out_specs=ON_CHIP,
        out_shape=struct((tiles, 2 * rows, heads_cols + HEAD_DIM), jnp.float32),
        compiler_params=params(8),
        name="attend_own",
    )(q_own, q_other, own, multiple)


def attend_rest_kernel(q_own, q_other, below, above, far, multiple, before, out_own, out_other):
    tiles, rows, heads_cols = q_own.shape
    cuts = head_cuts(heads_cols)
    heads = len(cuts)
    for pair in range(0, tiles, 2):
        queries, keys, values, times, floors, earlier = [], [], [], [], [], []
        for tile in (pair, pair + 1):
            pieces = [below[place] for place in range(tile, REACH)]
            pieces += [above[place] for place in range(tile + REACH + 1 - tiles)]
            pieces += [far[tile]]
            both = jnp.concatenate(pieces, axis=0)
            asked = jnp.concatenate([q_own[tile], q_other[tile]], axis=0)
            extra = before[tile, :, heads_cols:]
            queries += [asked[:, cut] for cut in cuts]
            keys += [both[:, cut] for cut in cuts]
            values += [both[:, heads_cols + cut.start : heads_cols + cut.stop] for cut in cuts]
            times += [multiple[tile, :, : both.shape[0]]] * heads
            floors += [extra[:, head : head + 1] for head in range(heads)]
            earlier += [extra[:, 64 + head : 65 + head] for head in range(heads)]
        peaks, totals, summed = soften(queries, keys, values, times, floors)
        shrink = [jnp.exp(floor - peak) for floor, peak in zip(floors, peaks)]
        totals = [total + old * less for total, old, less in zip(totals, earlier, shrink)]
        for place, tile in enumerate((pair, pair + 1)):
            here = slice(place * heads, (place + 1) * heads)
            for cut, each, less in zip(cuts, summed[here], shrink[here]):
                result = each + before[tile, :, cut] * less
                out_own[tile, :, cut] = result[:rows]
                out_other[tile, :, cut] = result[rows:]
            extra = packed(peaks[here], totals[here])
            out_own[tile, :, heads_cols:] = extra[:rows]
            out_other[tile, :, heads_cols:] = extra[rows:]


def attend_rest(q_own, q_other, below, above, far, multiple, before):
    tiles, rows, heads_cols = q_own.shape
    return pl.pallas_call(
        attend_rest_kernel,
        in_specs=[ON_CHIP] * 7,
        out_specs=[ON_CHIP] * 2,
        out_shape=[struct((tiles, rows, heads_cols + HEAD_DIM), jnp.float32)] * 2,
        compiler_params=params(8),
        name="attend_rest",
    )(q_own, q_other, below, above, far, multiple, before)


def merge_kernel(part_a, part_b, att):
    tiles, rows, _ = part_a.shape
    heads_cols = att.shape[-1]
    extra_a = part_a[:, :, heads_cols:].reshape(tiles * rows, HEAD_DIM)
    extra_b = part_b[:, :, heads_cols:].reshape(tiles * rows, HEAD_DIM)
    for head, cut in enumerate(head_cuts(heads_cols)):
        peak_a, total_a = extra_a[:, head : head + 1], extra_a[:, 64 + head : 65 + head]
        peak_b, total_b = extra_b[:, head : head + 1], extra_b[:, 64 + head : 65 + head]
        peak = jnp.maximum(peak_a, peak_b)
        grow_a, grow_b = jnp.exp(peak_a - peak), jnp.exp(peak_b - peak)
        total = total_a * grow_a + total_b * grow_b
        summed_a = part_a[:, :, cut].reshape(tiles * rows, HEAD_DIM)
        summed_b = part_b[:, :, cut].reshape(tiles * rows, HEAD_DIM)
        att[:, cut] = (summed_a * (grow_a / total) + summed_b * (grow_b / total)).astype(
            jnp.bfloat16
        )


def merge(part_a, part_b):
    tiles, rows, cols = part_a.shape
    return pl.pallas_call(
        merge_kernel,
        in_specs=[ON_CHIP] * 2,
        out_specs=ON_CHIP,
        out_shape=struct((tiles * rows, cols - HEAD_DIM)),
        compiler_params=params(8),
        name="merge",
    )(part_a, part_b)


def output_kernel(meta, *refs):
    atts, own, other = refs[:4], refs[4:6], refs[6:8]
    hidden, gates, out, weights, sems = refs[8:]
    rows = atts[0].shape[1]

    def fetch(pair, sources):
        return pltpu.make_async_copy(sources[pair], weights.at[pair], sems.at[pair])

    for chosen, sources in enumerate((other, own)):

        @pl.when(meta[1] == chosen)
        def _():
            for pair in range(2):
                fetch(pair, sources).start()

    product = jnp.zeros(out.shape, jnp.float32)
    for j, att in enumerate(atts):
        if j % 2 == 0:
            fetch(j // 2, own).wait()
        weight = weights[j // 2, (j % 2) * rows : (j % 2 + 1) * rows]
        product += jnp.dot(att[...], weight, preferred_element_type=jnp.float32)
    out[...] = (hidden[...].astype(jnp.float32) + gates[meta[0]] * product).astype(out.dtype)


def output(meta, atts, own, other, hidden, gates):
    return pl.pallas_call(
        output_kernel,
        in_specs=[SCALARS] + [ON_CHIP] * 4 + [ANYWHERE] * 4 + [ON_CHIP] * 2,
        out_specs=ON_CHIP,
        out_shape=struct(hidden.shape),
        scratch_shapes=[
            pltpu.VMEM((2,) + own[0].shape, jnp.bfloat16),
            pltpu.SemaphoreType.DMA((2,)),
        ],
        compiler_params=params(12),
        name="output",
    )(meta, *atts, *own, *other, hidden, gates)


def paired(first, second):
    rows, cols = first.shape
    return join(first[None], second[None]).reshape(2 * rows, cols)


def count_tiles(table, counts, chip, per_chip, repeat):
    tiles, slots = table.shape
    table = lax.dynamic_slice_in_dim(table, chip * per_chip, per_chip, 0)
    counts = lax.dynamic_slice_in_dim(counts, chip * per_chip, per_chip, 0)
    query_tiles = jnp.arange(per_chip, dtype=jnp.int32) + chip * per_chip
    across = tiles // 2 + (tiles // per_chip) // 2
    rows = []
    for tile in range(per_chip):
        first, last = max(0, tile - REACH), min(per_chip, tile + REACH + 1)
        own = [place - tile for place in range(first, last)]
        rest = [place - REACH - tile for place in range(tile, REACH)]
        rest += [per_chip + place - tile for place in range(tile + REACH + 1 - per_chip)]
        rest += [across]
        own = [d % tiles for d in own] + [-1] * (256 // repeat - len(own))
        rest = [d % tiles for d in rest] + [-1] * (128 // repeat - len(rest))
        rows.append([d for d in own + rest for _ in range(repeat)])
    reach = jnp.array(rows, jnp.int32)
    relative = (table - query_tiles[:, None]) % tiles
    live = jnp.arange(slots, dtype=jnp.int32)[None] < counts[:, None]
    hits = (relative[:, :, None] == reach[:, None]) & live[:, :, None]
    return jnp.sum(hits.astype(jnp.float32), axis=1)[:, None]


def gather_features(hidden):
    across = shifted(hidden, "tp", 2)
    return across, shifted(hidden, "tp", -1), shifted(hidden, "tp", 1), hidden


def local(
    latents, w_qkv, w_out, modulation, qk_gain, stale_cache, kv_tiles, tile_counts, patch_order
):
    core = lax.axis_index("segment")
    seq_size = lax.axis_size("seq")
    seq_pos = lax.axis_index("seq")
    tp_size = lax.axis_size("tp")
    tp_pos = lax.axis_index("tp")
    patches, patch_rows, part_cols = latents.shape
    rows_core = patch_rows // 2
    rows = patches * rows_core
    share = seq_size // patches
    chip = share * lax.rem(seq_pos, patches) + seq_pos // patches
    w_own = jnp.transpose(w_qkv[0], (1, 0, 2))
    heads_cols, width = w_out.shape[1:]
    head_dim = qk_gain.shape[-1]

    core_scalar = core.astype(jnp.int32)[None]
    def columns(weight, j):
        first = lax.rem(tp_pos + j, tp_size) * part_cols
        return lax.dynamic_slice_in_dim(weight, first, part_cols, 1)

    wo_across = columns(w_out[0], 2)
    mine = lax.dynamic_slice_in_dim(after(latents, wo_across), core * rows_core, rows_core, 1)
    wo_across = shifted(wo_across, "tp", 2)
    hidden = exchanged(mine).reshape(rows, part_cols)
    stale, stale_send = halve(core_scalar, after(stale_cache[0], mine))
    stale = join(stale, shifted(stale_send, "segment", 1))
    hidden, stale, wo_across, weight = lax.optimization_barrier(
        (hidden, stale, wo_across, w_out[0])
    )
    w_other = shifted(w_own, "segment", 1)
    small_own = jnp.concatenate([modulation[0].reshape(-1), qk_gain[0].reshape(-1)])
    small_other = shifted(small_own, "segment", 1)
    blocks = gather_features(hidden)
    stale, weight, kv_tiles, tile_counts, patch_order, small_own, small_other = after(
        (stale, weight, kv_tiles, tile_counts, patch_order, small_own, small_other), blocks[0]
    )
    stale = exchanged(stale)
    turns = jnp.arange(patches, dtype=jnp.int32)
    asked = jnp.stack([chip, chip - 1, chip + 1, chip - seq_size // 2 - 1]) % seq_size // share
    ranks = jnp.sum(jnp.where(patch_order[None] == asked[:, None], turns[None], 0), axis=-1)
    fresh = (ranks[0] <= ranks[1:]).astype(jnp.int32)
    multiple_own = count_tiles(kv_tiles[0], tile_counts[0], chip, patches, rows_core)
    multiple_other = shifted(multiple_own, "segment", 1)
    given = []
    for section in range(2):
        is_own = core == section
        meta = jnp.concatenate(
            [jnp.stack([tp_pos, is_own.astype(tp_pos.dtype)]).astype(jnp.int32), fresh]
        )
        small = jnp.where(is_own, small_own, small_other)
        modul = small[: 3 * width].reshape(3, tp_size, 1, part_cols)
        gain = small[3 * width :].reshape(2, head_dim)
        multiple = jnp.where(is_own, multiple_own, multiple_other)
        given.append(
            (meta, modul[0], modul[1], modul[2], gain, multiple[..., :256], multiple[..., 256:])
        )
    slices = [columns(weight, j) for j in (1, 3)]
    wo_own = [paired(columns(weight, 0), wo_across)]
    wo_other = [shifted(wo_own[0], "segment", 1)]

    for section in range(2):
        if section == 0:
            blocks, given, slices, wo_other = lax.optimization_barrier(
                (blocks, given, slices, wo_other)
            )
        else:
            blocks = gather_features(hidden)
            hidden1, keys0 = hidden.reshape(kv.shape), kv
        meta, shift, scale, gates, gain, times_own, times_rest = given[section]
        q_own, kv, *going = project(
            meta,
            blocks,
            shift,
            scale,
            gain,
            w_own,
            w_other,
            stale if section > 0 else None,
            (patches, rows_core, 2 * heads_cols),
        )
        if section == 0:
            going = choose_alone(meta, kv, stale)
        to_below, to_above, to_far = going
        far = along_ring(to_far, seq_size // 2 + 1, patches)
        above = along_ring(to_below, 1, patches)
        below = along_ring(to_above, -1, patches)
        q_other = shifted(q_own, "segment", 1)
        if section == 0:
            wo_prev, wo_next = after(slices, q_other)
            wo_prev, wo_next = shifted(wo_prev, "tp", 1), shifted(wo_next, "tp", 3)
            far, wo_prev, wo_next = lax.optimization_barrier((far, wo_prev, wo_next))
            wo_own.append(paired(wo_prev, wo_next))
        before = attend_own(q_own, q_other, kv, times_own)
        part_own, part_other = attend_rest(
            q_own, q_other, below, above, far, times_rest, before
        )
        part_back = shifted(part_other, "segment", 1)
        if section == 0:
            wo_other.append(shifted(after(wo_own[1], part_back), "segment", 1))
        att = merge(part_own, part_back)
        across = shifted(att, "tp", 2)
        atts = [att, across, shifted(att, "tp", 1), shifted(att, "tp", 3)]
        hidden = output(meta, atts, wo_own, wo_other, hidden, gates)

    home = exchanged(join(hidden1, kv, hidden.reshape(kv.shape), keys0))
    handed, new_cache = collect(core_scalar, home, shifted(home, "segment", 1))
    return (handed[None], new_cache[None])


def solution(mesh):
    in_specs = (
        P(None, "seq", "tp"),
        P("segment", None, None, "tp"),
        P("segment", "tp", None),
        P("segment", None, None),
        P("segment", None, None),
        P("segment", None, None, "seq", "tp"),
        P("segment", None, None),
        P("segment", None),
        P(),
    )
    out_specs = (P("segment", None, "seq", "tp"), P("segment", None, None, "seq", "tp"))
    return jax.shard_map(local, mesh=mesh, in_specs=in_specs, out_specs=out_specs, check_vma=False)
```

```python
import jax
import jax.numpy as jnp
from jax import lax
from jax.experimental import pallas as pl
from jax.experimental.pallas import tpu as pltpu
from jax.sharding import PartitionSpec as P

EPS = 1e-06
HEAD_DIM = 128
REACH = 3
MIB = 1024 * 1024
ON_CHIP = pl.BlockSpec(memory_space=pltpu.VMEM)
SCALARS = pl.BlockSpec(memory_space=pltpu.SMEM)
ANYWHERE = pl.BlockSpec(memory_space=pl.ANY)


def shifted(block, axis, distance):
    devices = range(lax.axis_size(axis))
    route = [((i - distance) % len(devices), i) for i in devices]
    return lax.ppermute(block, axis, route)


def after(values, *gates):
    return lax.optimization_barrier((values, gates))[0]


def params(mib):
    return pltpu.CompilerParams(vmem_limit_bytes=mib * MIB)


def struct(shape, dtype=jnp.bfloat16):
    return jax.ShapeDtypeStruct(shape, dtype)


def exchanged(tiles):
    group = tiles.shape[0]
    groups = [list(range(i, i + group)) for i in range(0, lax.axis_size("seq"), group)]
    return lax.all_to_all(tiles, "seq", 0, 0, axis_index_groups=groups)


def along_ring(block, distance, per_chip):
    size = lax.axis_size("seq")
    share = size // per_chip
    place = [per_chip * (i % share) + i // share for i in range(size)]
    route = [(place[(i + distance) % size], place[i]) for i in range(size)]
    return lax.ppermute(block, "seq", route)


def halve_kernel(core, stale, mine, theirs, sems):
    rows, cols = mine.shape[1], stale.shape[-1]
    copies = []
    for place, out in enumerate((mine, theirs)):
        first = core[0] if place == 0 else 1 - core[0]
        first = pl.multiple_of(first * rows, rows)
        for half in range(2):
            copies.append(
                pltpu.make_async_copy(
                    stale.at[half, :, pl.ds(first, rows)],
                    out.at[:, :, half * cols : (half + 1) * cols],
                    sems.at[2 * place + half],
                )
            )
    for copy in copies:
        copy.start()
    for copy in copies:
        copy.wait()


def halve(core, stale):
    _, patches, rows, cols = stale.shape
    return pl.pallas_call(
        halve_kernel,
        in_specs=[SCALARS, ANYWHERE],
        out_specs=[ON_CHIP] * 2,
        out_shape=[struct((patches, rows // 2, 2 * cols))] * 2,
        scratch_shapes=[pltpu.SemaphoreType.DMA((4,))],
        compiler_params=params(8),
        name="halve",
    )(core, stale)


def join_kernel(*refs):
    *parts, out, sems = refs
    rows = parts[0].shape[1]
    copies = [
        pltpu.make_async_copy(part, out.at[:, i * rows : (i + 1) * rows], sems.at[i])
        for i, part in enumerate(parts)
    ]
    for copy in copies:
        copy.start()
    for copy in copies:
        copy.wait()


def join(*parts):
    tiles, rows, cols = parts[0].shape
    return pl.pallas_call(
        join_kernel,
        in_specs=[ANYWHERE] * len(parts),
        out_specs=ON_CHIP,
        out_shape=struct((tiles, len(parts) * rows, cols)),
        scratch_shapes=[pltpu.SemaphoreType.DMA((len(parts),))],
        compiler_params=params(8),
        name="join",
    )(*parts)


def collect_kernel(core, early, got_early, home, got, handed, cache):
    rows, cols = early.shape[1], cache.shape[-1]
    features1, keys1, features2 = (slice(i * rows, (i + 1) * rows) for i in range(3))

    def collect(features, feature_refs, keys, key_refs):
        for half in range(2):
            here = slice(half * rows, (half + 1) * rows)
            handed[:, here] = feature_refs[half][:, features]
            for which in range(2):
                cut = slice(which * cols, (which + 1) * cols)
                cache[which, :, here] = key_refs[half][:, keys, cut]

    @pl.when(core[0] == 0)
    def _():
        collect(features2, (home, got), slice(0, rows), (early, got_early))

    @pl.when(core[0] == 1)
    def _():
        collect(features1, (got, home), keys1, (got, home))


def collect(core, early, got_early, home, got):
    patches, rows, cols = early.shape
    return pl.pallas_call(
        collect_kernel,
        in_specs=[SCALARS] + [ON_CHIP] * 4,
        out_specs=[ON_CHIP] * 2,
        out_shape=[
            struct((patches, 2 * rows, cols)),
            struct((2, patches, 2 * rows, cols // 2)),
        ],
        compiler_params=params(8),
        name="collect",
    )(core, early, got_early, home, got)


def choose(meta, kv, stale, outs):
    tiles, rows, _ = kv.shape
    old = pl.ds(pl.multiple_of((1 - meta[1]) * rows, rows), rows)
    for place, out in enumerate(outs):
        first = tiles - REACH if place == 1 else 0
        cut = slice(first, first + out.shape[0])

        @pl.when(meta[2 + place] == 1)
        def _():
            out[...] = kv[cut]

        @pl.when(meta[2 + place] == 0)
        def _():
            out[...] = stale[cut, old]


def payloads(kv_shape):
    edge = struct((REACH,) + kv_shape[1:])
    return [edge, edge, struct(kv_shape)]


def project_kernel(meta, *refs):
    blocks = refs[:4]
    shift, scale, gain, w_own, w_other, _ = refs[4:10]
    refs = refs[10:]
    stale, q_out, kv_out, *outs = refs[:-4]
    xs, modded, weights, sems = refs[-4:]
    _, rows, cols = xs.shape
    tiles, rows_tile, kv_cols = kv_out.shape
    heads_cols = kv_cols // 2
    parts = shift.shape[0]
    width = cols * parts
    features = [lax.rem(meta[0] + j, parts) for j in (2, 1, 3, 0)]

    def fetch(j, source):
        first = pl.multiple_of(features[j] * cols, cols)
        return pltpu.make_async_copy(
            source.at[:, pl.ds(first, cols)],
            weights.at[:, j * cols : (j + 1) * cols],
            sems.at[j],
        )

    arriving = [
        pltpu.make_async_copy(blocks[j], xs.at[j], sems.at[parts + j]) for j in range(parts)
    ]
    for copy in arriving:
        copy.start()
    for chosen, source in enumerate((w_other, w_own)):

        @pl.when(meta[1] == chosen)
        def _():
            for j in range(parts):
                fetch(j, source).start()

    for copy in arriving:
        copy.wait()
    total = jnp.zeros((rows, 1), jnp.float32)
    for j in range(parts):
        total += jnp.sum(xs[j].astype(jnp.float32), axis=-1, keepdims=True)
    mean = total / width
    square = jnp.zeros((rows, 1), jnp.float32)
    for j in range(parts):
        centred = xs[j].astype(jnp.float32) - mean
        square += jnp.sum(centred * centred, axis=-1, keepdims=True)
    spread = lax.rsqrt(square / width + EPS)
    for j in range(parts):
        normed = (xs[j].astype(jnp.float32) - mean) * spread
        modded[:, j * cols : (j + 1) * cols] = (
            normed * (1.0 + scale[features[j]]) + shift[features[j]]
        ).astype(jnp.bfloat16)
    for j in range(parts):
        fetch(j, w_own).wait()

    for part in (1, 2, 0):
        product = jnp.dot(modded[...], weights[part], preferred_element_type=jnp.float32)
        if part == 2:
            kv_out[:, :, heads_cols:] = product.astype(jnp.bfloat16).reshape(
                tiles, rows_tile, heads_cols
            )
            continue
        for head in range(heads_cols // HEAD_DIM):
            cut = slice(head * HEAD_DIM, (head + 1) * HEAD_DIM)
            vec = product[:, cut]
            mean_sq = jnp.mean(vec * vec, axis=-1, keepdims=True)
            vec = vec * lax.rsqrt(mean_sq + EPS) * gain[part : part + 1]
            vec = vec.astype(jnp.bfloat16).reshape(tiles, rows_tile, HEAD_DIM)
            if part == 0:
                q_out[:, :, cut] = vec
            else:
                kv_out[:, :, cut] = vec
    choose(meta, kv_out, stale, outs)


def project(meta, blocks, shift, scale, gain, w_own, w_other, begun, stale):
    rows, cols = blocks[0].shape
    tiles, rows_tile, kv_cols = stale.shape[0], stale.shape[1] // 2, stale.shape[2]
    kv_shape = (tiles, rows_tile, kv_cols)
    parts = shift.shape[0]
    heads_cols = kv_cols // 2
    shapes = [struct((tiles, rows_tile, heads_cols)), struct(kv_shape)] + payloads(kv_shape)
    return pl.pallas_call(
        project_kernel,
        in_specs=[SCALARS]
        + [ANYWHERE] * len(blocks)
        + [ON_CHIP] * 3
        + [ANYWHERE] * 3
        + [ON_CHIP],
        out_specs=[ON_CHIP] * len(shapes),
        out_shape=shapes,
        scratch_shapes=[
            pltpu.VMEM((parts, rows, cols), jnp.bfloat16),
            pltpu.VMEM((rows, parts * cols), jnp.bfloat16),
            pltpu.VMEM((3, parts * cols, heads_cols), jnp.bfloat16),
            pltpu.SemaphoreType.DMA((2 * parts,)),
        ],
        compiler_params=params(52),
        name="project",
    )(meta, *blocks, shift, scale, gain, w_own, w_other, begun, stale)


def soften(queries, keys, values, times, floors):
    scores = [
        lax.dot_general(q, k, (((1,), (1,)), ((), ())), preferred_element_type=jnp.float32)
        for q, k in zip(queries, keys)
    ]
    scores = [
        jnp.where(count > 0.0, each * HEAD_DIM ** (-0.5), -1e30)
        for each, count in zip(scores, times)
    ]
    peaks = [jnp.max(each, axis=-1, keepdims=True) for each in scores]
    if floors is not None:
        peaks = [jnp.maximum(peak, floor) for peak, floor in zip(peaks, floors)]
    weights = [
        jnp.exp(each - peak) * count for each, peak, count in zip(scores, peaks, times)
    ]
    totals = [jnp.sum(each, axis=-1, keepdims=True) for each in weights]
    summed = [
        jnp.dot(each.astype(jnp.bfloat16), v, preferred_element_type=jnp.float32)
        for each, v in zip(weights, values)
    ]
    return peaks, totals, summed


def head_cuts(heads_cols):
    return [slice(first, first + HEAD_DIM) for first in range(0, heads_cols, HEAD_DIM)]


def packed(peaks, totals):
    lane = lax.broadcasted_iota(jnp.int32, (peaks[0].shape[0], HEAD_DIM), 1)
    out = jnp.zeros((peaks[0].shape[0], HEAD_DIM), jnp.float32)
    for head, (peak, total) in enumerate(zip(peaks, totals)):
        out = jnp.where(lane == head, peak, out)
        out = jnp.where(lane == 64 + head, total, out)
    return out


def attend_own_kernel(q_own, q_other, own, multiple, out):
    tiles, rows, heads_cols = q_own.shape
    cuts = head_cuts(heads_cols)
    for tile in range(tiles):
        first, last = max(0, tile - REACH), min(tiles, tile + REACH + 1)
        count = (last - first) * rows
        both = own[first:last].reshape(count, 2 * heads_cols)
        queries = jnp.concatenate([q_own[tile], q_other[tile]], axis=0)
        peaks, totals, summed = soften(
            [queries[:, cut] for cut in cuts],
            [both[:, cut] for cut in cuts],
            [both[:, heads_cols + cut.start : heads_cols + cut.stop] for cut in cuts],
            [multiple[tile, :, :count]] * len(cuts),
            None,
        )
        for cut, each in zip(cuts, summed):
            out[tile, :, cut] = each
        out[tile, :, heads_cols:] = packed(peaks, totals)


def attend_own(q_own, q_other, own, multiple):
    tiles, rows, heads_cols = q_own.shape
    return pl.pallas_call(
        attend_own_kernel,
        in_specs=[ON_CHIP] * 4,
        out_specs=ON_CHIP,
        out_shape=struct((tiles, 2 * rows, heads_cols + HEAD_DIM), jnp.float32),
        compiler_params=params(8),
        name="attend_own",
    )(q_own, q_other, own, multiple)


def attend_rest_kernel(q_own, q_other, below, above, far, multiple, before, out_own, out_other):
    tiles, rows, heads_cols = q_own.shape
    cuts = head_cuts(heads_cols)
    heads = len(cuts)
    for pair in range(0, tiles, 2):
        queries, keys, values, times, floors, earlier = [], [], [], [], [], []
        for tile in (pair, pair + 1):
            pieces = [below[place] for place in range(tile, REACH)]
            pieces += [above[place] for place in range(tile + REACH + 1 - tiles)]
            pieces += [far[tile]]
            both = jnp.concatenate(pieces, axis=0)
            asked = jnp.concatenate([q_own[tile], q_other[tile]], axis=0)
            extra = before[tile, :, heads_cols:]
            queries += [asked[:, cut] for cut in cuts]
            keys += [both[:, cut] for cut in cuts]
            values += [both[:, heads_cols + cut.start : heads_cols + cut.stop] for cut in cuts]
            times += [multiple[tile, :, 256 : 256 + both.shape[0]]] * heads
            floors += [extra[:, head : head + 1] for head in range(heads)]
            earlier += [extra[:, 64 + head : 65 + head] for head in range(heads)]
        peaks, totals, summed = soften(queries, keys, values, times, floors)
        shrink = [jnp.exp(floor - peak) for floor, peak in zip(floors, peaks)]
        totals = [total + old * less for total, old, less in zip(totals, earlier, shrink)]
        for place, tile in enumerate((pair, pair + 1)):
            here = slice(place * heads, (place + 1) * heads)
            for cut, each, less in zip(cuts, summed[here], shrink[here]):
                result = each + before[tile, :, cut] * less
                out_own[tile, :, cut] = result[:rows]
                out_other[tile, :, cut] = result[rows:]
            extra = packed(peaks[here], totals[here])
            out_own[tile, :, heads_cols:] = extra[:rows]
            out_other[tile, :, heads_cols:] = extra[rows:]


def attend_rest(q_own, q_other, below, above, far, multiple, before):
    tiles, rows, heads_cols = q_own.shape
    return pl.pallas_call(
        attend_rest_kernel,
        in_specs=[ON_CHIP] * 7,
        out_specs=[ON_CHIP] * 2,
        out_shape=[struct((tiles, rows, heads_cols + HEAD_DIM), jnp.float32)] * 2,
        compiler_params=params(8),
        name="attend_rest",
    )(q_own, q_other, below, above, far, multiple, before)


def merge_kernel(part_a, part_b, att):
    tiles, rows, _ = part_a.shape
    heads_cols = att.shape[-1]
    extra_a = part_a[:, :, heads_cols:].reshape(tiles * rows, HEAD_DIM)
    extra_b = part_b[:, :, heads_cols:].reshape(tiles * rows, HEAD_DIM)
    for head, cut in enumerate(head_cuts(heads_cols)):
        peak_a, total_a = extra_a[:, head : head + 1], extra_a[:, 64 + head : 65 + head]
        peak_b, total_b = extra_b[:, head : head + 1], extra_b[:, 64 + head : 65 + head]
        peak = jnp.maximum(peak_a, peak_b)
        grow_a, grow_b = jnp.exp(peak_a - peak), jnp.exp(peak_b - peak)
        total = total_a * grow_a + total_b * grow_b
        summed_a = part_a[:, :, cut].reshape(tiles * rows, HEAD_DIM)
        summed_b = part_b[:, :, cut].reshape(tiles * rows, HEAD_DIM)
        att[:, cut] = (summed_a * (grow_a / total) + summed_b * (grow_b / total)).astype(
            jnp.bfloat16
        )


def merge(part_a, part_b):
    tiles, rows, cols = part_a.shape
    return pl.pallas_call(
        merge_kernel,
        in_specs=[ON_CHIP] * 2,
        out_specs=ON_CHIP,
        out_shape=struct((tiles * rows, cols - HEAD_DIM)),
        compiler_params=params(8),
        name="merge",
    )(part_a, part_b)


def output_kernel(meta, *refs):
    atts, own, other = refs[:4], refs[4:6], refs[6:8]
    hidden, gates, out, weights, sems = refs[8:]
    rows = atts[0].shape[1]

    def fetch(pair, sources):
        return pltpu.make_async_copy(sources[pair], weights.at[pair], sems.at[pair])

    for chosen, sources in enumerate((other, own)):

        @pl.when(meta[1] == chosen)
        def _():
            for pair in range(2):
                fetch(pair, sources).start()

    product = jnp.zeros(out.shape, jnp.float32)
    for j, att in enumerate(atts):
        if j % 2 == 0:
            fetch(j // 2, own).wait()
        weight = weights[j // 2, (j % 2) * rows : (j % 2 + 1) * rows]
        product += jnp.dot(att[...], weight, preferred_element_type=jnp.float32)
    out[...] = (hidden[...].astype(jnp.float32) + gates[meta[0]] * product).astype(out.dtype)


def output(meta, atts, own, other, hidden, gates):
    return pl.pallas_call(
        output_kernel,
        in_specs=[SCALARS] + [ON_CHIP] * 4 + [ANYWHERE] * 4 + [ON_CHIP] * 2,
        out_specs=ON_CHIP,
        out_shape=struct(hidden.shape),
        scratch_shapes=[
            pltpu.VMEM((2,) + own[0].shape, jnp.bfloat16),
            pltpu.SemaphoreType.DMA((2,)),
        ],
        compiler_params=params(12),
        name="output",
    )(meta, *atts, *own, *other, hidden, gates)


def paired(first, second):
    rows, cols = first.shape
    return join(first[None], second[None]).reshape(2 * rows, cols)


def count_tiles(table, counts, chip, per_chip, repeat):
    tiles, slots = table.shape
    table = lax.dynamic_slice_in_dim(table, chip * per_chip, per_chip, 0)
    counts = lax.dynamic_slice_in_dim(counts, chip * per_chip, per_chip, 0)
    query_tiles = jnp.arange(per_chip, dtype=jnp.int32) + chip * per_chip
    across = tiles // 2 + (tiles // per_chip) // 2
    rows = []
    for tile in range(per_chip):
        first, last = max(0, tile - REACH), min(per_chip, tile + REACH + 1)
        own = [place - tile for place in range(first, last)]
        rest = [place - REACH - tile for place in range(tile, REACH)]
        rest += [per_chip + place - tile for place in range(tile + REACH + 1 - per_chip)]
        rest += [across]
        own = [d % tiles for d in own] + [-1] * (256 // repeat - len(own))
        rest = [d % tiles for d in rest] + [-1] * (128 // repeat - len(rest))
        rows.append([d for d in own + rest for _ in range(repeat)])
    reach = jnp.array(rows, jnp.int32)
    relative = (table - query_tiles[:, None]) % tiles
    live = jnp.arange(slots, dtype=jnp.int32)[None] < counts[:, None]
    hits = (relative[:, :, None] == reach[:, None]) & live[:, :, None]
    return jnp.sum(hits.astype(jnp.float32), axis=1)[:, None]


def gather_features(hidden):
    across = shifted(hidden, "tp", 2)
    return across, shifted(hidden, "tp", -1), shifted(hidden, "tp", 1), hidden


def local(
    latents, w_qkv, w_out, modulation, qk_gain, stale_cache, kv_tiles, tile_counts, patch_order
):
    core = lax.axis_index("segment")
    seq_size = lax.axis_size("seq")
    seq_pos = lax.axis_index("seq")
    tp_size = lax.axis_size("tp")
    tp_pos = lax.axis_index("tp")
    patches, patch_rows, part_cols = latents.shape
    rows_core = patch_rows // 2
    rows = patches * rows_core
    share = seq_size // patches
    chip = share * lax.rem(seq_pos, patches) + seq_pos // patches
    w_own = jnp.transpose(w_qkv[0], (1, 0, 2))
    heads_cols, width = w_out.shape[1:]
    head_dim = qk_gain.shape[-1]

    core_scalar = core.astype(jnp.int32)[None]
    def columns(weight, j):
        first = lax.rem(tp_pos + j, tp_size) * part_cols
        return lax.dynamic_slice_in_dim(weight, first, part_cols, 1)

    wo_across = columns(w_out[0], 2)
    mine = lax.dynamic_slice_in_dim(after(latents, wo_across), core * rows_core, rows_core, 1)
    wo_across = shifted(wo_across, "tp", 2)
    hidden = exchanged(mine).reshape(rows, part_cols)
    stale, stale_send = halve(core_scalar, after(stale_cache[0], mine))
    stale_got = shifted(stale_send, "segment", 1)
    w_other = shifted(w_own, "segment", 1)
    modulation, qk_gain, kv_tiles, tile_counts, patch_order = after(
        (modulation, qk_gain, kv_tiles, tile_counts, patch_order), stale_got
    )
    stale = exchanged(join(stale, stale_got))
    weight = after(w_out[0], stale_got)
    slices = [columns(weight, j) for j in (1, 3)]
    wo_own = [paired(columns(weight, 0), wo_across)]
    wo_other = [shifted(wo_own[0], "segment", 1)]
    small_own = jnp.concatenate([modulation[0].reshape(-1), qk_gain[0].reshape(-1)])
    small_other = shifted(small_own, "segment", 1)
    turns = jnp.arange(patches, dtype=jnp.int32)
    asked = jnp.stack([chip, chip - 1, chip + 1, chip - seq_size // 2 - 1]) % seq_size // share
    ranks = jnp.sum(jnp.where(patch_order[None] == asked[:, None], turns[None], 0), axis=-1)
    fresh = (ranks[0] <= ranks[1:]).astype(jnp.int32)
    multiple_own = count_tiles(kv_tiles[0], tile_counts[0], chip, patches, rows_core)
    multiple_other = shifted(multiple_own, "segment", 1)
    given = []
    for section in range(2):
        is_own = core == section
        meta = jnp.concatenate(
            [jnp.stack([tp_pos, is_own.astype(tp_pos.dtype)]).astype(jnp.int32), fresh]
        )
        small = jnp.where(is_own, small_own, small_other)
        modul = small[: 3 * width].reshape(3, tp_size, 1, part_cols)
        gain = small[3 * width :].reshape(2, head_dim)
        multiple = jnp.where(is_own, multiple_own, multiple_other)
        given.append(
            (meta, modul[0], modul[1], modul[2], gain, multiple)
        )
    hidden, stale, slices, wo_own, wo_other, given = lax.optimization_barrier(
        (hidden, stale, slices, wo_own, wo_other, given)
    )

    for section in range(2):
        blocks = gather_features(hidden)
        begun = meta = given[section][0]
        if section > 0:
            hidden1 = hidden.reshape(kv.shape)
            begun = shifted(hidden[:16, :HEAD_DIM], "segment", 1)
            early = exchanged(after(kv, begun))
            blocks, early = lax.optimization_barrier((blocks, early))
            got_early = shifted(early, "segment", 1)
        meta, shift, scale, gates, gain, times = given[section]
        q_own, kv, to_below, to_above, to_far = project(
            meta,
            blocks,
            shift,
            scale,
            gain,
            w_own,
            w_other,
            begun,
            stale,
        )
        far = along_ring(to_far, seq_size // 2 + 1, patches)
        above = along_ring(to_below, 1, patches)
        below = along_ring(to_above, -1, patches)
        q_other = shifted(q_own, "segment", 1)
        if section == 0:
            wo_prev, wo_next = after(slices, q_other, to_far)
            wo_prev, wo_next = shifted(wo_prev, "tp", 1), shifted(wo_next, "tp", 3)
            far, wo_prev, wo_next = lax.optimization_barrier((far, wo_prev, wo_next))
            wo_own.append(paired(wo_prev, wo_next))
        before = attend_own(q_own, q_other, kv, times)
        part_own, part_other = attend_rest(
            q_own, q_other, below, above, far, times, before
        )
        part_back = shifted(part_other, "segment", 1)
        if section == 0:
            wo_other.append(shifted(after(wo_own[1], part_back), "segment", 1))
        else:
            part_back, got_early = lax.optimization_barrier((part_back, got_early))
        att = merge(part_own, part_back)
        across = shifted(att, "tp", 2)
        atts = [att, across, shifted(att, "tp", 1), shifted(att, "tp", 3)]
        hidden = output(meta, atts, wo_own, wo_other, hidden, gates)

    home = exchanged(join(hidden1, kv, hidden.reshape(kv.shape)))
    got = shifted(home, "segment", 1)
    handed, new_cache = collect(core_scalar, early, got_early, home, got)
    return (handed[None], new_cache[None])


def solution(mesh):
    in_specs = (
        P(None, "seq", "tp"),
        P("segment", None, None, "tp"),
        P("segment", "tp", None),
        P("segment", None, None),
        P("segment", None, None),
        P("segment", None, None, "seq", "tp"),
        P("segment", None, None),
        P("segment", None),
        P(),
    )
    out_specs = (P("segment", None, "seq", "tp"), P("segment", None, None, "seq", "tp"))
    return jax.shard_map(local, mesh=mesh, in_specs=in_specs, out_specs=out_specs, check_vma=False)
```

```python
import jax
import jax.numpy as jnp
from jax import lax
from jax.experimental import pallas as pl
from jax.experimental.pallas import tpu as pltpu
from jax.sharding import PartitionSpec as P

EPS = 1e-06
HEAD_DIM = 128
REACH = 3
MIB = 1024 * 1024
ON_CHIP = pl.BlockSpec(memory_space=pltpu.VMEM)
SCALARS = pl.BlockSpec(memory_space=pltpu.SMEM)
ANYWHERE = pl.BlockSpec(memory_space=pl.ANY)


def shifted(block, axis, distance):
    devices = range(lax.axis_size(axis))
    route = [((i - distance) % len(devices), i) for i in devices]
    return lax.ppermute(block, axis, route)


def after(values, *gates):
    return lax.optimization_barrier((values, gates))[0]


def params(mib):
    return pltpu.CompilerParams(vmem_limit_bytes=mib * MIB)


def struct(shape, dtype=jnp.bfloat16):
    return jax.ShapeDtypeStruct(shape, dtype)


def exchanged(tiles):
    group = tiles.shape[0]
    groups = [list(range(i, i + group)) for i in range(0, lax.axis_size("seq"), group)]
    return lax.all_to_all(tiles, "seq", 0, 0, axis_index_groups=groups)


def along_ring(block, distance, per_chip):
    size = lax.axis_size("seq")
    share = size // per_chip
    place = [per_chip * (i % share) + i // share for i in range(size)]
    route = [(place[(i + distance) % size], place[i]) for i in range(size)]
    return lax.ppermute(block, "seq", route)


def halve_kernel(core, stale, mine, theirs, sems):
    rows, cols = mine.shape[1], stale.shape[-1]
    copies = []
    for place, out in enumerate((mine, theirs)):
        first = core[0] if place == 0 else 1 - core[0]
        first = pl.multiple_of(first * rows, rows)
        for half in range(2):
            copies.append(
                pltpu.make_async_copy(
                    stale.at[half, :, pl.ds(first, rows)],
                    out.at[:, :, half * cols : (half + 1) * cols],
                    sems.at[2 * place + half],
                )
            )
    for copy in copies:
        copy.start()
    for copy in copies:
        copy.wait()


def halve(core, stale):
    _, patches, rows, cols = stale.shape
    return pl.pallas_call(
        halve_kernel,
        in_specs=[SCALARS, ANYWHERE],
        out_specs=[ON_CHIP] * 2,
        out_shape=[struct((patches, rows // 2, 2 * cols))] * 2,
        scratch_shapes=[pltpu.SemaphoreType.DMA((4,))],
        compiler_params=params(8),
        name="halve",
    )(core, stale)


def join_kernel(*refs):
    *parts, out, sems = refs
    rows = parts[0].shape[1]
    copies = [
        pltpu.make_async_copy(part, out.at[:, i * rows : (i + 1) * rows], sems.at[i])
        for i, part in enumerate(parts)
    ]
    for copy in copies:
        copy.start()
    for copy in copies:
        copy.wait()


def join(*parts):
    tiles, rows, cols = parts[0].shape
    return pl.pallas_call(
        join_kernel,
        in_specs=[ANYWHERE] * len(parts),
        out_specs=ON_CHIP,
        out_shape=struct((tiles, len(parts) * rows, cols)),
        scratch_shapes=[pltpu.SemaphoreType.DMA((len(parts),))],
        compiler_params=params(8),
        name="join",
    )(*parts)


def collect_kernel(core, early, got_early, home, got, handed, cache):
    rows, cols = early.shape[1], cache.shape[-1]
    features1, keys1, features2 = (slice(i * rows, (i + 1) * rows) for i in range(3))

    def collect(features, feature_refs, keys, key_refs):
        for half in range(2):
            here = slice(half * rows, (half + 1) * rows)
            handed[:, here] = feature_refs[half][:, features]
            for which in range(2):
                cut = slice(which * cols, (which + 1) * cols)
                cache[which, :, here] = key_refs[half][:, keys, cut]

    @pl.when(core[0] == 0)
    def _():
        collect(features2, (home, got), slice(0, rows), (early, got_early))

    @pl.when(core[0] == 1)
    def _():
        collect(features1, (got, home), keys1, (got, home))


def collect(core, early, got_early, home, got):
    patches, rows, cols = early.shape
    return pl.pallas_call(
        collect_kernel,
        in_specs=[SCALARS] + [ON_CHIP] * 4,
        out_specs=[ON_CHIP] * 2,
        out_shape=[
            struct((patches, 2 * rows, cols)),
            struct((2, patches, 2 * rows, cols // 2)),
        ],
        compiler_params=params(8),
        name="collect",
    )(core, early, got_early, home, got)


def choose(meta, kv, stale, outs):
    tiles, rows, _ = kv.shape
    old = pl.ds(pl.multiple_of((1 - meta[1]) * rows, rows), rows)
    for place, out in enumerate(outs):
        first = tiles - REACH if place == 1 else 0
        cut = slice(first, first + out.shape[0])

        @pl.when(meta[2 + place] == 1)
        def _():
            out[...] = kv[cut]

        @pl.when(meta[2 + place] == 0)
        def _():
            out[...] = stale[cut, old]


def choose_kernel(meta, kv, stale, lo_out, hi_out, far_out):
    choose(meta, kv, stale, (lo_out, hi_out, far_out))


def payloads(kv_shape):
    edge = struct((REACH,) + kv_shape[1:])
    return [edge, edge, struct(kv_shape)]


def choose_alone(meta, kv, stale):
    return pl.pallas_call(
        choose_kernel,
        in_specs=[SCALARS] + [ON_CHIP] * 2,
        out_specs=[ON_CHIP] * 3,
        out_shape=payloads(kv.shape),
        compiler_params=params(8),
        name="choose",
    )(meta, kv, stale)


def project_kernel(meta, *refs, with_stale):
    blocks = refs[:4]
    shift, scale, gain, w_own, w_other, _ = refs[4:10]
    refs = refs[10:]
    if with_stale:
        stale, q_out, kv_out, *outs = refs[:-4]
    else:
        q_out, kv_out = refs[:-4]
    xs, modded, weights, sems = refs[-4:]
    _, rows, cols = xs.shape
    tiles, rows_tile, kv_cols = kv_out.shape
    heads_cols = kv_cols // 2
    parts = shift.shape[0]
    width = cols * parts
    features = [lax.rem(meta[0] + j, parts) for j in (2, 1, 3, 0)]

    def fetch(j, source):
        first = pl.multiple_of(features[j] * cols, cols)
        return pltpu.make_async_copy(
            source.at[:, pl.ds(first, cols)],
            weights.at[:, j * cols : (j + 1) * cols],
            sems.at[j],
        )

    arriving = [
        pltpu.make_async_copy(blocks[j], xs.at[j], sems.at[parts + j]) for j in range(parts)
    ]
    for copy in arriving:
        copy.start()
    for chosen, source in enumerate((w_other, w_own)):

        @pl.when(meta[1] == chosen)
        def _():
            for j in range(parts):
                fetch(j, source).start()

    for copy in arriving:
        copy.wait()
    total = jnp.zeros((rows, 1), jnp.float32)
    for j in range(parts):
        total += jnp.sum(xs[j].astype(jnp.float32), axis=-1, keepdims=True)
    mean = total / width
    square = jnp.zeros((rows, 1), jnp.float32)
    for j in range(parts):
        centred = xs[j].astype(jnp.float32) - mean
        square += jnp.sum(centred * centred, axis=-1, keepdims=True)
    spread = lax.rsqrt(square / width + EPS)
    for j in range(parts):
        normed = (xs[j].astype(jnp.float32) - mean) * spread
        modded[:, j * cols : (j + 1) * cols] = (
            normed * (1.0 + scale[features[j]]) + shift[features[j]]
        ).astype(jnp.bfloat16)
    for j in range(parts):
        fetch(j, w_own).wait()

    for part in (1, 2, 0):
        product = jnp.dot(modded[...], weights[part], preferred_element_type=jnp.float32)
        if part == 2:
            kv_out[:, :, heads_cols:] = product.astype(jnp.bfloat16).reshape(
                tiles, rows_tile, heads_cols
            )
            continue
        for head in range(heads_cols // HEAD_DIM):
            cut = slice(head * HEAD_DIM, (head + 1) * HEAD_DIM)
            vec = product[:, cut]
            mean_sq = jnp.mean(vec * vec, axis=-1, keepdims=True)
            vec = vec * lax.rsqrt(mean_sq + EPS) * gain[part : part + 1]
            vec = vec.astype(jnp.bfloat16).reshape(tiles, rows_tile, HEAD_DIM)
            if part == 0:
                q_out[:, :, cut] = vec
            else:
                kv_out[:, :, cut] = vec
    if with_stale:
        choose(meta, kv_out, stale, outs)


def project(meta, blocks, shift, scale, gain, w_own, w_other, begun, stale, kv_shape):
    rows, cols = blocks[0].shape
    tiles, rows_tile, kv_cols = kv_shape
    parts = shift.shape[0]
    heads_cols = kv_cols // 2
    shapes = [struct((tiles, rows_tile, heads_cols)), struct(kv_shape)]
    extra = []
    if stale is not None:
        shapes += payloads(kv_shape)
        extra = [stale]

    def kernel(*refs):
        project_kernel(*refs, with_stale=stale is not None)

    return pl.pallas_call(
        kernel,
        in_specs=[SCALARS]
        + [ANYWHERE] * len(blocks)
        + [ON_CHIP] * 3
        + [ANYWHERE] * 3
        + [ON_CHIP] * len(extra),
        out_specs=[ON_CHIP] * len(shapes),
        out_shape=shapes,
        scratch_shapes=[
            pltpu.VMEM((parts, rows, cols), jnp.bfloat16),
            pltpu.VMEM((rows, parts * cols), jnp.bfloat16),
            pltpu.VMEM((3, parts * cols, heads_cols), jnp.bfloat16),
            pltpu.SemaphoreType.DMA((2 * parts,)),
        ],
        compiler_params=params(52),
        name="project",
    )(meta, *blocks, shift, scale, gain, w_own, w_other, begun, *extra)


def soften(queries, keys, values, times, floors):
    scores = [
        lax.dot_general(q, k, (((1,), (1,)), ((), ())), preferred_element_type=jnp.float32)
        for q, k in zip(queries, keys)
    ]
    scores = [
        jnp.where(count > 0.0, each * HEAD_DIM ** (-0.5), -1e30)
        for each, count in zip(scores, times)
    ]
    peaks = [jnp.max(each, axis=-1, keepdims=True) for each in scores]
    if floors is not None:
        peaks = [jnp.maximum(peak, floor) for peak, floor in zip(peaks, floors)]
    weights = [
        jnp.exp(each - peak) * count for each, peak, count in zip(scores, peaks, times)
    ]
    totals = [jnp.sum(each, axis=-1, keepdims=True) for each in weights]
    summed = [
        jnp.dot(each.astype(jnp.bfloat16), v, preferred_element_type=jnp.float32)
        for each, v in zip(weights, values)
    ]
    return peaks, totals, summed


def head_cuts(heads_cols):
    return [slice(first, first + HEAD_DIM) for first in range(0, heads_cols, HEAD_DIM)]


def packed(peaks, totals):
    lane = lax.broadcasted_iota(jnp.int32, (peaks[0].shape[0], HEAD_DIM), 1)
    out = jnp.zeros((peaks[0].shape[0], HEAD_DIM), jnp.float32)
    for head, (peak, total) in enumerate(zip(peaks, totals)):
        out = jnp.where(lane == head, peak, out)
        out = jnp.where(lane == 64 + head, total, out)
    return out


def attend_own_kernel(q_own, q_other, own, multiple, out):
    tiles, rows, heads_cols = q_own.shape
    cuts = head_cuts(heads_cols)
    for tile in range(tiles):
        first, last = max(0, tile - REACH), min(tiles, tile + REACH + 1)
        count = (last - first) * rows
        both = own[first:last].reshape(count, 2 * heads_cols)
        queries = jnp.concatenate([q_own[tile], q_other[tile]], axis=0)
        peaks, totals, summed = soften(
            [queries[:, cut] for cut in cuts],
            [both[:, cut] for cut in cuts],
            [both[:, heads_cols + cut.start : heads_cols + cut.stop] for cut in cuts],
            [multiple[tile, :, :count]] * len(cuts),
            None,
        )
        for cut, each in zip(cuts, summed):
            out[tile, :, cut] = each
        out[tile, :, heads_cols:] = packed(peaks, totals)


def attend_own(q_own, q_other, own, multiple):
    tiles, rows, heads_cols = q_own.shape
    return pl.pallas_call(
        attend_own_kernel,
        in_specs=[ON_CHIP] * 4,
        out_specs=ON_CHIP,
        out_shape=struct((tiles, 2 * rows, heads_cols + HEAD_DIM), jnp.float32),
        compiler_params=params(8),
        name="attend_own",
    )(q_own, q_other, own, multiple)


def attend_rest_kernel(q_own, q_other, below, above, far, multiple, before, out_own, out_other):
    tiles, rows, heads_cols = q_own.shape
    cuts = head_cuts(heads_cols)
    heads = len(cuts)
    for pair in range(0, tiles, 2):
        queries, keys, values, times, floors, earlier = [], [], [], [], [], []
        for tile in (pair, pair + 1):
            pieces = [below[place] for place in range(tile, REACH)]
            pieces += [above[place] for place in range(tile + REACH + 1 - tiles)]
            pieces += [far[tile]]
            both = jnp.concatenate(pieces, axis=0)
            asked = jnp.concatenate([q_own[tile], q_other[tile]], axis=0)
            extra = before[tile, :, heads_cols:]
            queries += [asked[:, cut] for cut in cuts]
            keys += [both[:, cut] for cut in cuts]
            values += [both[:, heads_cols + cut.start : heads_cols + cut.stop] for cut in cuts]
            times += [multiple[tile, :, 256 : 256 + both.shape[0]]] * heads
            floors += [extra[:, head : head + 1] for head in range(heads)]
            earlier += [extra[:, 64 + head : 65 + head] for head in range(heads)]
        peaks, totals, summed = soften(queries, keys, values, times, floors)
        shrink = [jnp.exp(floor - peak) for floor, peak in zip(floors, peaks)]
        totals = [total + old * less for total, old, less in zip(totals, earlier, shrink)]
        for place, tile in enumerate((pair, pair + 1)):
            here = slice(place * heads, (place + 1) * heads)
            for cut, each, less in zip(cuts, summed[here], shrink[here]):
                result = each + before[tile, :, cut] * less
                out_own[tile, :, cut] = result[:rows]
                out_other[tile, :, cut] = result[rows:]
            extra = packed(peaks[here], totals[here])
            out_own[tile, :, heads_cols:] = extra[:rows]
            out_other[tile, :, heads_cols:] = extra[rows:]


def attend_rest(q_own, q_other, below, above, far, multiple, before):
    tiles, rows, heads_cols = q_own.shape
    return pl.pallas_call(
        attend_rest_kernel,
        in_specs=[ON_CHIP] * 7,
        out_specs=[ON_CHIP] * 2,
        out_shape=[struct((tiles, rows, heads_cols + HEAD_DIM), jnp.float32)] * 2,
        compiler_params=params(8),
        name="attend_rest",
    )(q_own, q_other, below, above, far, multiple, before)


def merge_kernel(part_a, part_b, att):
    tiles, rows, _ = part_a.shape
    heads_cols = att.shape[-1]
    extra_a = part_a[:, :, heads_cols:].reshape(tiles * rows, HEAD_DIM)
    extra_b = part_b[:, :, heads_cols:].reshape(tiles * rows, HEAD_DIM)
    for head, cut in enumerate(head_cuts(heads_cols)):
        peak_a, total_a = extra_a[:, head : head + 1], extra_a[:, 64 + head : 65 + head]
        peak_b, total_b = extra_b[:, head : head + 1], extra_b[:, 64 + head : 65 + head]
        peak = jnp.maximum(peak_a, peak_b)
        grow_a, grow_b = jnp.exp(peak_a - peak), jnp.exp(peak_b - peak)
        total = total_a * grow_a + total_b * grow_b
        summed_a = part_a[:, :, cut].reshape(tiles * rows, HEAD_DIM)
        summed_b = part_b[:, :, cut].reshape(tiles * rows, HEAD_DIM)
        att[:, cut] = (summed_a * (grow_a / total) + summed_b * (grow_b / total)).astype(
            jnp.bfloat16
        )


def merge(part_a, part_b):
    tiles, rows, cols = part_a.shape
    return pl.pallas_call(
        merge_kernel,
        in_specs=[ON_CHIP] * 2,
        out_specs=ON_CHIP,
        out_shape=struct((tiles * rows, cols - HEAD_DIM)),
        compiler_params=params(8),
        name="merge",
    )(part_a, part_b)


def output_kernel(meta, *refs):
    atts, own, other = refs[:4], refs[4:6], refs[6:8]
    hidden, gates, out, weights, sems = refs[8:]
    rows = atts[0].shape[1]

    def fetch(pair, sources):
        return pltpu.make_async_copy(sources[pair], weights.at[pair], sems.at[pair])

    for chosen, sources in enumerate((other, own)):

        @pl.when(meta[1] == chosen)
        def _():
            for pair in range(2):
                fetch(pair, sources).start()

    product = jnp.zeros(out.shape, jnp.float32)
    for j, att in enumerate(atts):
        if j % 2 == 0:
            fetch(j // 2, own).wait()
        weight = weights[j // 2, (j % 2) * rows : (j % 2 + 1) * rows]
        product += jnp.dot(att[...], weight, preferred_element_type=jnp.float32)
    out[...] = (hidden[...].astype(jnp.float32) + gates[meta[0]] * product).astype(out.dtype)


def output(meta, atts, own, other, hidden, gates):
    return pl.pallas_call(
        output_kernel,
        in_specs=[SCALARS] + [ON_CHIP] * 4 + [ANYWHERE] * 4 + [ON_CHIP] * 2,
        out_specs=ON_CHIP,
        out_shape=struct(hidden.shape),
        scratch_shapes=[
            pltpu.VMEM((2,) + own[0].shape, jnp.bfloat16),
            pltpu.SemaphoreType.DMA((2,)),
        ],
        compiler_params=params(12),
        name="output",
    )(meta, *atts, *own, *other, hidden, gates)


def paired(first, second):
    rows, cols = first.shape
    return join(first[None], second[None]).reshape(2 * rows, cols)


def count_tiles(table, counts, chip, per_chip, repeat):
    tiles, slots = table.shape
    table = lax.dynamic_slice_in_dim(table, chip * per_chip, per_chip, 0)
    counts = lax.dynamic_slice_in_dim(counts, chip * per_chip, per_chip, 0)
    query_tiles = jnp.arange(per_chip, dtype=jnp.int32) + chip * per_chip
    across = tiles // 2 + (tiles // per_chip) // 2
    rows = []
    for tile in range(per_chip):
        first, last = max(0, tile - REACH), min(per_chip, tile + REACH + 1)
        own = [place - tile for place in range(first, last)]
        rest = [place - REACH - tile for place in range(tile, REACH)]
        rest += [per_chip + place - tile for place in range(tile + REACH + 1 - per_chip)]
        rest += [across]
        own = [d % tiles for d in own] + [-1] * (256 // repeat - len(own))
        rest = [d % tiles for d in rest] + [-1] * (128 // repeat - len(rest))
        rows.append([d for d in own + rest for _ in range(repeat)])
    reach = jnp.array(rows, jnp.int32)
    relative = (table - query_tiles[:, None]) % tiles
    live = jnp.arange(slots, dtype=jnp.int32)[None] < counts[:, None]
    hits = (relative[:, :, None] == reach[:, None]) & live[:, :, None]
    return jnp.sum(hits.astype(jnp.float32), axis=1)[:, None]


def gather_features(hidden):
    across = shifted(hidden, "tp", 2)
    return across, shifted(hidden, "tp", -1), shifted(hidden, "tp", 1), hidden


def local(
    latents, w_qkv, w_out, modulation, qk_gain, stale_cache, kv_tiles, tile_counts, patch_order
):
    core = lax.axis_index("segment")
    seq_size = lax.axis_size("seq")
    seq_pos = lax.axis_index("seq")
    tp_size = lax.axis_size("tp")
    tp_pos = lax.axis_index("tp")
    patches, patch_rows, part_cols = latents.shape
    rows_core = patch_rows // 2
    rows = patches * rows_core
    share = seq_size // patches
    chip = share * lax.rem(seq_pos, patches) + seq_pos // patches
    w_own = jnp.transpose(w_qkv[0], (1, 0, 2))
    heads_cols, width = w_out.shape[1:]
    head_dim = qk_gain.shape[-1]

    core_scalar = core.astype(jnp.int32)[None]
    def columns(weight, j):
        first = lax.rem(tp_pos + j, tp_size) * part_cols
        return lax.dynamic_slice_in_dim(weight, first, part_cols, 1)

    wo_across = columns(w_out[0], 2)
    mine = lax.dynamic_slice_in_dim(after(latents, wo_across), core * rows_core, rows_core, 1)
    wo_across = shifted(wo_across, "tp", 2)
    hidden = exchanged(mine).reshape(rows, part_cols)
    stale, stale_send = halve(core_scalar, after(stale_cache[0], mine))
    stale_got = shifted(stale_send, "segment", 1)
    w_other = shifted(w_own, "segment", 1)
    stale = join(stale, stale_got)
    kv_tiles, tile_counts = after((kv_tiles, tile_counts), stale_got)
    multiple_own = count_tiles(kv_tiles[0], tile_counts[0], chip, patches, rows_core)
    hidden, stale, wo_across, multiple_own = lax.optimization_barrier(
        (hidden, stale, wo_across, multiple_own)
    )
    small_own = jnp.concatenate([modulation[0].reshape(-1), qk_gain[0].reshape(-1)])
    small_other = shifted(small_own, "segment", 1)
    blocks = gather_features(hidden)
    stale, weight, multiple_own, patch_order, small_own, small_other = after(
        (stale, w_out[0], multiple_own, patch_order, small_own, small_other), blocks[0]
    )
    stale = exchanged(stale)
    slices = [columns(weight, j) for j in (1, 3)]
    wo_own = [paired(columns(weight, 0), wo_across)]
    wo_other = [shifted(wo_own[0], "segment", 1)]
    turns = jnp.arange(patches, dtype=jnp.int32)
    asked = jnp.stack([chip, chip - 1, chip + 1, chip - seq_size // 2 - 1]) % seq_size // share
    ranks = jnp.sum(jnp.where(patch_order[None] == asked[:, None], turns[None], 0), axis=-1)
    fresh = (ranks[0] <= ranks[1:]).astype(jnp.int32)
    multiple_other = shifted(multiple_own, "segment", 1)
    given = []
    for section in range(2):
        is_own = core == section
        meta = jnp.concatenate(
            [jnp.stack([tp_pos, is_own.astype(tp_pos.dtype)]).astype(jnp.int32), fresh]
        )
        small = jnp.where(is_own, small_own, small_other)
        modul = small[: 3 * width].reshape(3, tp_size, 1, part_cols)
        gain = small[3 * width :].reshape(2, head_dim)
        multiple = jnp.where(is_own, multiple_own, multiple_other)
        given.append(
            (meta, modul[0], modul[1], modul[2], gain, multiple)
        )

    for section in range(2):
        begun = given[section][0]
        if section == 0:
            blocks, given, slices, wo_other = lax.optimization_barrier(
                (blocks, given, slices, wo_other)
            )
        else:
            blocks = gather_features(hidden)
            hidden1 = hidden.reshape(kv.shape)
            begun = shifted(hidden[:16, :HEAD_DIM], "segment", 1)
            early = exchanged(after(kv, begun))
            blocks, early = lax.optimization_barrier((blocks, early))
            got_early = shifted(early, "segment", 1)
        meta, shift, scale, gates, gain, times = given[section]
        q_own, kv, *going = project(
            meta,
            blocks,
            shift,
            scale,
            gain,
            w_own,
            w_other,
            begun,
            stale if section > 0 else None,
            (patches, rows_core, 2 * heads_cols),
        )
        if section == 0:
            going = choose_alone(meta, kv, stale)
        to_below, to_above, to_far = going
        far = along_ring(to_far, seq_size // 2 + 1, patches)
        above = along_ring(to_below, 1, patches)
        below = along_ring(to_above, -1, patches)
        q_other = shifted(q_own, "segment", 1)
        if section == 0:
            wo_prev, wo_next = after(slices, q_other, to_far)
            wo_prev, wo_next = shifted(wo_prev, "tp", 1), shifted(wo_next, "tp", 3)
            far, wo_prev, wo_next = lax.optimization_barrier((far, wo_prev, wo_next))
            wo_own.append(paired(wo_prev, wo_next))
        before = attend_own(q_own, q_other, kv, times)
        part_own, part_other = attend_rest(
            q_own, q_other, below, above, far, times, before
        )
        part_back = shifted(part_other, "segment", 1)
        if section == 0:
            wo_other.append(shifted(after(wo_own[1], part_back), "segment", 1))
        else:
            part_back, got_early = lax.optimization_barrier((part_back, got_early))
        att = merge(part_own, part_back)
        across = shifted(att, "tp", 2)
        atts = [att, across, shifted(att, "tp", 1), shifted(att, "tp", 3)]
        hidden = output(meta, atts, wo_own, wo_other, hidden, gates)

    home = exchanged(join(hidden1, kv, hidden.reshape(kv.shape)))
    got = shifted(home, "segment", 1)
    handed, new_cache = collect(core_scalar, early, got_early, home, got)
    return (handed[None], new_cache[None])


def solution(mesh):
    in_specs = (
        P(None, "seq", "tp"),
        P("segment", None, None, "tp"),
        P("segment", "tp", None),
        P("segment", None, None),
        P("segment", None, None),
        P("segment", None, None, "seq", "tp"),
        P("segment", None, None),
        P("segment", None),
        P(),
    )
    out_specs = (P("segment", None, "seq", "tp"), P("segment", None, None, "seq", "tp"))
    return jax.shard_map(local, mesh=mesh, in_specs=in_specs, out_specs=out_specs, check_vma=False)
```

```python
import jax
import jax.numpy as jnp
from jax import lax
from jax.experimental import pallas as pl
from jax.experimental.pallas import tpu as pltpu
from jax.sharding import PartitionSpec as P

EPS = 1e-06
HEAD_DIM = 128
REACH = 3
MIB = 1024 * 1024
ON_CHIP = pl.BlockSpec(memory_space=pltpu.VMEM)
SCALARS = pl.BlockSpec(memory_space=pltpu.SMEM)
ANYWHERE = pl.BlockSpec(memory_space=pl.ANY)


def shifted(block, axis, distance):
    devices = range(lax.axis_size(axis))
    route = [((i - distance) % len(devices), i) for i in devices]
    return lax.ppermute(block, axis, route)


def after(values, *gates):
    return lax.optimization_barrier((values, gates))[0]


def params(mib):
    return pltpu.CompilerParams(vmem_limit_bytes=mib * MIB)


def struct(shape, dtype=jnp.bfloat16):
    return jax.ShapeDtypeStruct(shape, dtype)


def exchanged(tiles):
    group = tiles.shape[0]
    groups = [list(range(i, i + group)) for i in range(0, lax.axis_size("seq"), group)]
    return lax.all_to_all(tiles, "seq", 0, 0, axis_index_groups=groups)


def along_ring(block, distance, per_chip):
    size = lax.axis_size("seq")
    share = size // per_chip
    place = [per_chip * (i % share) + i // share for i in range(size)]
    route = [(place[(i + distance) % size], place[i]) for i in range(size)]
    return lax.ppermute(block, "seq", route)


def halve_kernel(core, stale, mine, theirs, sems):
    rows, cols = mine.shape[1], stale.shape[-1]
    copies = []
    for place, out in enumerate((mine, theirs)):
        first = core[0] if place == 0 else 1 - core[0]
        first = pl.multiple_of(first * rows, rows)
        for half in range(2):
            copies.append(
                pltpu.make_async_copy(
                    stale.at[half, :, pl.ds(first, rows)],
                    out.at[:, :, half * cols : (half + 1) * cols],
                    sems.at[2 * place + half],
                )
            )
    for copy in copies:
        copy.start()
    for copy in copies:
        copy.wait()


def halve(core, stale):
    _, patches, rows, cols = stale.shape
    return pl.pallas_call(
        halve_kernel,
        in_specs=[SCALARS, ANYWHERE],
        out_specs=[ON_CHIP] * 2,
        out_shape=[struct((patches, rows // 2, 2 * cols))] * 2,
        scratch_shapes=[pltpu.SemaphoreType.DMA((4,))],
        compiler_params=params(8),
        name="halve",
    )(core, stale)


def join_kernel(*refs):
    *parts, out, sems = refs
    rows = parts[0].shape[1]
    copies = [
        pltpu.make_async_copy(part, out.at[:, i * rows : (i + 1) * rows], sems.at[i])
        for i, part in enumerate(parts)
    ]
    for copy in copies:
        copy.start()
    for copy in copies:
        copy.wait()


def join(*parts):
    tiles, rows, cols = parts[0].shape
    return pl.pallas_call(
        join_kernel,
        in_specs=[ANYWHERE] * len(parts),
        out_specs=ON_CHIP,
        out_shape=struct((tiles, len(parts) * rows, cols)),
        scratch_shapes=[pltpu.SemaphoreType.DMA((len(parts),))],
        compiler_params=params(8),
        name="join",
    )(*parts)


def collect_kernel(core, early, got_early, home, got, handed, cache):
    rows, cols = early.shape[1], cache.shape[-1]
    features1, keys1, features2 = (slice(i * rows, (i + 1) * rows) for i in range(3))

    def collect(features, feature_refs, keys, key_refs):
        for half in range(2):
            here = slice(half * rows, (half + 1) * rows)
            handed[:, here] = feature_refs[half][:, features]
            for which in range(2):
                cut = slice(which * cols, (which + 1) * cols)
                cache[which, :, here] = key_refs[half][:, keys, cut]

    @pl.when(core[0] == 0)
    def _():
        collect(features2, (home, got), slice(0, rows), (early, got_early))

    @pl.when(core[0] == 1)
    def _():
        collect(features1, (got, home), keys1, (got, home))


def collect(core, early, got_early, home, got):
    patches, rows, cols = early.shape
    return pl.pallas_call(
        collect_kernel,
        in_specs=[SCALARS] + [ON_CHIP] * 4,
        out_specs=[ON_CHIP] * 2,
        out_shape=[
            struct((patches, 2 * rows, cols)),
            struct((2, patches, 2 * rows, cols // 2)),
        ],
        compiler_params=params(8),
        name="collect",
    )(core, early, got_early, home, got)


def choose(meta, kv, stale, outs):
    tiles, rows, _ = kv.shape
    old = pl.ds(pl.multiple_of((1 - meta[1]) * rows, rows), rows)
    for place, out in enumerate(outs):
        first = tiles - REACH if place == 1 else 0
        cut = slice(first, first + out.shape[0])

        @pl.when(meta[2 + place] == 1)
        def _():
            out[...] = kv[cut]

        @pl.when(meta[2 + place] == 0)
        def _():
            out[...] = stale[cut, old]


def choose_kernel(meta, kv, stale, lo_out, hi_out, far_out):
    choose(meta, kv, stale, (lo_out, hi_out, far_out))


def payloads(kv_shape):
    edge = struct((REACH,) + kv_shape[1:])
    return [edge, edge, struct(kv_shape)]


def choose_alone(meta, kv, stale):
    return pl.pallas_call(
        choose_kernel,
        in_specs=[SCALARS] + [ON_CHIP] * 2,
        out_specs=[ON_CHIP] * 3,
        out_shape=payloads(kv.shape),
        compiler_params=params(8),
        name="choose",
    )(meta, kv, stale)


def project_kernel(meta, *refs, with_stale):
    blocks = refs[:4]
    shift, scale, gain, w_own, w_other, _ = refs[4:10]
    refs = refs[10:]
    if with_stale:
        stale, q_out, kv_out, *outs = refs[:-4]
    else:
        q_out, kv_out = refs[:-4]
    xs, modded, weights, sems = refs[-4:]
    _, rows, cols = xs.shape
    tiles, rows_tile, kv_cols = kv_out.shape
    heads_cols = kv_cols // 2
    parts = shift.shape[0]
    width = cols * parts
    features = [lax.rem(meta[0] + j, parts) for j in (2, 1, 3, 0)]

    def fetch(j, source):
        first = pl.multiple_of(features[j] * cols, cols)
        return pltpu.make_async_copy(
            source.at[:, pl.ds(first, cols)],
            weights.at[:, j * cols : (j + 1) * cols],
            sems.at[j],
        )

    arriving = [
        pltpu.make_async_copy(blocks[j], xs.at[j], sems.at[parts + j]) for j in range(parts)
    ]
    for copy in arriving:
        copy.start()
    for chosen, source in enumerate((w_other, w_own)):

        @pl.when(meta[1] == chosen)
        def _():
            for j in range(parts):
                fetch(j, source).start()

    for copy in arriving:
        copy.wait()
    total = jnp.zeros((rows, 1), jnp.float32)
    for j in range(parts):
        total += jnp.sum(xs[j].astype(jnp.float32), axis=-1, keepdims=True)
    mean = total / width
    square = jnp.zeros((rows, 1), jnp.float32)
    for j in range(parts):
        centred = xs[j].astype(jnp.float32) - mean
        square += jnp.sum(centred * centred, axis=-1, keepdims=True)
    spread = lax.rsqrt(square / width + EPS)
    for j in range(parts):
        normed = (xs[j].astype(jnp.float32) - mean) * spread
        modded[:, j * cols : (j + 1) * cols] = (
            normed * (1.0 + scale[features[j]]) + shift[features[j]]
        ).astype(jnp.bfloat16)
    for j in range(parts):
        fetch(j, w_own).wait()

    for part in (1, 2, 0):
        product = jnp.dot(modded[...], weights[part], preferred_element_type=jnp.float32)
        if part == 2:
            kv_out[:, :, heads_cols:] = product.astype(jnp.bfloat16).reshape(
                tiles, rows_tile, heads_cols
            )
            continue
        for head in range(heads_cols // HEAD_DIM):
            cut = slice(head * HEAD_DIM, (head + 1) * HEAD_DIM)
            vec = product[:, cut]
            mean_sq = jnp.mean(vec * vec, axis=-1, keepdims=True)
            vec = vec * lax.rsqrt(mean_sq + EPS) * gain[part : part + 1]
            vec = vec.astype(jnp.bfloat16).reshape(tiles, rows_tile, HEAD_DIM)
            if part == 0:
                q_out[:, :, cut] = vec
            else:
                kv_out[:, :, cut] = vec
    if with_stale:
        choose(meta, kv_out, stale, outs)


def project(meta, blocks, shift, scale, gain, w_own, w_other, begun, stale, kv_shape):
    rows, cols = blocks[0].shape
    tiles, rows_tile, kv_cols = kv_shape
    parts = shift.shape[0]
    heads_cols = kv_cols // 2
    shapes = [struct((tiles, rows_tile, heads_cols)), struct(kv_shape)]
    extra = []
    if stale is not None:
        shapes += payloads(kv_shape)
        extra = [stale]

    def kernel(*refs):
        project_kernel(*refs, with_stale=stale is not None)

    return pl.pallas_call(
        kernel,
        in_specs=[SCALARS]
        + [ANYWHERE] * len(blocks)
        + [ON_CHIP] * 3
        + [ANYWHERE] * 3
        + [ON_CHIP] * len(extra),
        out_specs=[ON_CHIP] * len(shapes),
        out_shape=shapes,
        scratch_shapes=[
            pltpu.VMEM((parts, rows, cols), jnp.bfloat16),
            pltpu.VMEM((rows, parts * cols), jnp.bfloat16),
            pltpu.VMEM((3, parts * cols, heads_cols), jnp.bfloat16),
            pltpu.SemaphoreType.DMA((2 * parts,)),
        ],
        compiler_params=params(52),
        name="project",
    )(meta, *blocks, shift, scale, gain, w_own, w_other, begun, *extra)


def soften(queries, keys, values, times, floors):
    scores = [
        lax.dot_general(q, k, (((1,), (1,)), ((), ())), preferred_element_type=jnp.float32)
        for q, k in zip(queries, keys)
    ]
    scores = [
        jnp.where(count > 0.0, each * HEAD_DIM ** (-0.5), -1e30)
        for each, count in zip(scores, times)
    ]
    peaks = [jnp.max(each, axis=-1, keepdims=True) for each in scores]
    if floors is not None:
        peaks = [jnp.maximum(peak, floor) for peak, floor in zip(peaks, floors)]
    weights = [
        jnp.exp(each - peak) * count for each, peak, count in zip(scores, peaks, times)
    ]
    totals = [jnp.sum(each, axis=-1, keepdims=True) for each in weights]
    summed = [
        jnp.dot(each.astype(jnp.bfloat16), v, preferred_element_type=jnp.float32)
        for each, v in zip(weights, values)
    ]
    return peaks, totals, summed


def head_cuts(heads_cols):
    return [slice(first, first + HEAD_DIM) for first in range(0, heads_cols, HEAD_DIM)]


def packed(peaks, totals):
    lane = lax.broadcasted_iota(jnp.int32, (peaks[0].shape[0], HEAD_DIM), 1)
    out = jnp.zeros((peaks[0].shape[0], HEAD_DIM), jnp.float32)
    for head, (peak, total) in enumerate(zip(peaks, totals)):
        out = jnp.where(lane == head, peak, out)
        out = jnp.where(lane == 64 + head, total, out)
    return out


def attend_own_kernel(q_own, q_other, own, multiple, out):
    tiles, rows, heads_cols = q_own.shape
    cuts = head_cuts(heads_cols)
    for tile in range(tiles):
        first, last = max(0, tile - REACH), min(tiles, tile + REACH + 1)
        count = (last - first) * rows
        both = own[first:last].reshape(count, 2 * heads_cols)
        queries = jnp.concatenate([q_own[tile], q_other[tile]], axis=0)
        peaks, totals, summed = soften(
            [queries[:, cut] for cut in cuts],
            [both[:, cut] for cut in cuts],
            [both[:, heads_cols + cut.start : heads_cols + cut.stop] for cut in cuts],
            [multiple[tile, :, :count]] * len(cuts),
            None,
        )
        for cut, each in zip(cuts, summed):
            out[tile, :, cut] = each
        out[tile, :, heads_cols:] = packed(peaks, totals)


def attend_own(q_own, q_other, own, multiple):
    tiles, rows, heads_cols = q_own.shape
    return pl.pallas_call(
        attend_own_kernel,
        in_specs=[ON_CHIP] * 4,
        out_specs=ON_CHIP,
        out_shape=struct((tiles, 2 * rows, heads_cols + HEAD_DIM), jnp.float32),
        compiler_params=params(8),
        name="attend_own",
    )(q_own, q_other, own, multiple)


def attend_rest_kernel(q_own, q_other, below, above, far, multiple, before, out_own, out_other):
    tiles, rows, heads_cols = q_own.shape
    cuts = head_cuts(heads_cols)
    heads = len(cuts)
    for pair in range(0, tiles, 2):
        queries, keys, values, times, floors, earlier = [], [], [], [], [], []
        for tile in (pair, pair + 1):
            pieces = [below[place] for place in range(tile, REACH)]
            pieces += [above[place] for place in range(tile + REACH + 1 - tiles)]
            pieces += [far[tile]]
            both = jnp.concatenate(pieces, axis=0)
            asked = jnp.concatenate([q_own[tile], q_other[tile]], axis=0)
            extra = before[tile, :, heads_cols:]
            queries += [asked[:, cut] for cut in cuts]
            keys += [both[:, cut] for cut in cuts]
            values += [both[:, heads_cols + cut.start : heads_cols + cut.stop] for cut in cuts]
            times += [multiple[tile, :, 256 : 256 + both.shape[0]]] * heads
            floors += [extra[:, head : head + 1] for head in range(heads)]
            earlier += [extra[:, 64 + head : 65 + head] for head in range(heads)]
        peaks, totals, summed = soften(queries, keys, values, times, floors)
        shrink = [jnp.exp(floor - peak) for floor, peak in zip(floors, peaks)]
        totals = [total + old * less for total, old, less in zip(totals, earlier, shrink)]
        for place, tile in enumerate((pair, pair + 1)):
            here = slice(place * heads, (place + 1) * heads)
            for cut, each, less in zip(cuts, summed[here], shrink[here]):
                result = each + before[tile, :, cut] * less
                out_own[tile, :, cut] = result[:rows]
                out_other[tile, :, cut] = result[rows:]
            extra = packed(peaks[here], totals[here])
            out_own[tile, :, heads_cols:] = extra[:rows]
            out_other[tile, :, heads_cols:] = extra[rows:]


def attend_rest(q_own, q_other, below, above, far, multiple, before):
    tiles, rows, heads_cols = q_own.shape
    return pl.pallas_call(
        attend_rest_kernel,
        in_specs=[ON_CHIP] * 7,
        out_specs=[ON_CHIP] * 2,
        out_shape=[struct((tiles, rows, heads_cols + HEAD_DIM), jnp.float32)] * 2,
        compiler_params=params(8),
        name="attend_rest",
    )(q_own, q_other, below, above, far, multiple, before)


def merge_kernel(part_a, part_b, att):
    tiles, rows, _ = part_a.shape
    heads_cols = att.shape[-1]
    extra_a = part_a[:, :, heads_cols:].reshape(tiles * rows, HEAD_DIM)
    extra_b = part_b[:, :, heads_cols:].reshape(tiles * rows, HEAD_DIM)
    for head, cut in enumerate(head_cuts(heads_cols)):
        peak_a, total_a = extra_a[:, head : head + 1], extra_a[:, 64 + head : 65 + head]
        peak_b, total_b = extra_b[:, head : head + 1], extra_b[:, 64 + head : 65 + head]
        peak = jnp.maximum(peak_a, peak_b)
        grow_a, grow_b = jnp.exp(peak_a - peak), jnp.exp(peak_b - peak)
        total = total_a * grow_a + total_b * grow_b
        summed_a = part_a[:, :, cut].reshape(tiles * rows, HEAD_DIM)
        summed_b = part_b[:, :, cut].reshape(tiles * rows, HEAD_DIM)
        att[:, cut] = (summed_a * (grow_a / total) + summed_b * (grow_b / total)).astype(
            jnp.bfloat16
        )


def merge(part_a, part_b):
    tiles, rows, cols = part_a.shape
    return pl.pallas_call(
        merge_kernel,
        in_specs=[ON_CHIP] * 2,
        out_specs=ON_CHIP,
        out_shape=struct((tiles * rows, cols - HEAD_DIM)),
        compiler_params=params(8),
        name="merge",
    )(part_a, part_b)


def output_kernel(meta, *refs):
    atts, own, other = refs[:4], refs[4:6], refs[6:8]
    hidden, gates, out, weights, sems = refs[8:]
    rows = atts[0].shape[1]

    def fetch(pair, sources):
        return pltpu.make_async_copy(sources[pair], weights.at[pair], sems.at[pair])

    for chosen, sources in enumerate((other, own)):

        @pl.when(meta[1] == chosen)
        def _():
            for pair in range(2):
                fetch(pair, sources).start()

    product = jnp.zeros(out.shape, jnp.float32)
    for j, att in enumerate(atts):
        if j % 2 == 0:
            fetch(j // 2, own).wait()
        weight = weights[j // 2, (j % 2) * rows : (j % 2 + 1) * rows]
        product += jnp.dot(att[...], weight, preferred_element_type=jnp.float32)
    out[...] = (hidden[...].astype(jnp.float32) + gates[meta[0]] * product).astype(out.dtype)


def output(meta, atts, own, other, hidden, gates):
    return pl.pallas_call(
        output_kernel,
        in_specs=[SCALARS] + [ON_CHIP] * 4 + [ANYWHERE] * 4 + [ON_CHIP] * 2,
        out_specs=ON_CHIP,
        out_shape=struct(hidden.shape),
        scratch_shapes=[
            pltpu.VMEM((2,) + own[0].shape, jnp.bfloat16),
            pltpu.SemaphoreType.DMA((2,)),
        ],
        compiler_params=params(12),
        name="output",
    )(meta, *atts, *own, *other, hidden, gates)


def paired(first, second):
    rows, cols = first.shape
    return join(first[None], second[None]).reshape(2 * rows, cols)


def count_tiles(table, counts, chip, per_chip, repeat):
    tiles, slots = table.shape
    table = lax.dynamic_slice_in_dim(table, chip * per_chip, per_chip, 0)
    counts = lax.dynamic_slice_in_dim(counts, chip * per_chip, per_chip, 0)
    query_tiles = jnp.arange(per_chip, dtype=jnp.int32) + chip * per_chip
    across = tiles // 2 + (tiles // per_chip) // 2
    rows = []
    for tile in range(per_chip):
        first, last = max(0, tile - REACH), min(per_chip, tile + REACH + 1)
        own = [place - tile for place in range(first, last)]
        rest = [place - REACH - tile for place in range(tile, REACH)]
        rest += [per_chip + place - tile for place in range(tile + REACH + 1 - per_chip)]
        rest += [across]
        own = [d % tiles for d in own] + [-1] * (256 // repeat - len(own))
        rest = [d % tiles for d in rest] + [-1] * (128 // repeat - len(rest))
        rows.append([d for d in own + rest for _ in range(repeat)])
    reach = jnp.array(rows, jnp.int32)
    relative = (table - query_tiles[:, None]) % tiles
    live = jnp.arange(slots, dtype=jnp.int32)[None] < counts[:, None]
    hits = (relative[:, :, None] == reach[:, None]) & live[:, :, None]
    return jnp.sum(hits.astype(jnp.float32), axis=1)[:, None]


def gather_features(hidden):
    across = shifted(hidden, "tp", 2)
    return across, shifted(hidden, "tp", -1), shifted(hidden, "tp", 1), hidden


def local(
    latents, w_qkv, w_out, modulation, qk_gain, stale_cache, kv_tiles, tile_counts, patch_order
):
    core = lax.axis_index("segment")
    seq_size = lax.axis_size("seq")
    seq_pos = lax.axis_index("seq")
    tp_size = lax.axis_size("tp")
    tp_pos = lax.axis_index("tp")
    patches, patch_rows, part_cols = latents.shape
    rows_core = patch_rows // 2
    rows = patches * rows_core
    share = seq_size // patches
    chip = share * lax.rem(seq_pos, patches) + seq_pos // patches
    w_own = jnp.transpose(w_qkv[0], (1, 0, 2))
    heads_cols, width = w_out.shape[1:]
    head_dim = qk_gain.shape[-1]

    core_scalar = core.astype(jnp.int32)[None]
    def columns(weight, j):
        first = lax.rem(tp_pos + j, tp_size) * part_cols
        return lax.dynamic_slice_in_dim(weight, first, part_cols, 1)

    wo_across = columns(w_out[0], 2)
    mine = lax.dynamic_slice_in_dim(after(latents, wo_across), core * rows_core, rows_core, 1)
    wo_across = shifted(wo_across, "tp", 2)
    hidden = exchanged(mine).reshape(rows, part_cols)
    stale, stale_send = halve(core_scalar, after(stale_cache[0], mine))
    stale_got = shifted(stale_send, "segment", 1)
    w_other = shifted(w_own, "segment", 1)
    stale = join(stale, stale_got)
    hidden, stale, wo_across = lax.optimization_barrier((hidden, stale, wo_across))
    small_own = jnp.concatenate([modulation[0].reshape(-1), qk_gain[0].reshape(-1)])
    small_other = shifted(small_own, "segment", 1)
    blocks = gather_features(hidden)
    stale, weight, kv_tiles, tile_counts, patch_order, small_own, small_other = after(
        (stale, w_out[0], kv_tiles, tile_counts, patch_order, small_own, small_other), blocks[0]
    )
    stale = exchanged(stale)
    slices = [columns(weight, j) for j in (1, 3)]
    wo_own = [paired(columns(weight, 0), wo_across)]
    wo_other = [shifted(wo_own[0], "segment", 1)]
    turns = jnp.arange(patches, dtype=jnp.int32)
    asked = jnp.stack([chip, chip - 1, chip + 1, chip - seq_size // 2 - 1]) % seq_size // share
    ranks = jnp.sum(jnp.where(patch_order[None] == asked[:, None], turns[None], 0), axis=-1)
    fresh = (ranks[0] <= ranks[1:]).astype(jnp.int32)
    multiple_own = count_tiles(kv_tiles[0], tile_counts[0], chip, patches, rows_core)
    multiple_other = shifted(multiple_own, "segment", 1)
    given = []
    for section in range(2):
        is_own = core == section
        meta = jnp.concatenate(
            [jnp.stack([tp_pos, is_own.astype(tp_pos.dtype)]).astype(jnp.int32), fresh]
        )
        small = jnp.where(is_own, small_own, small_other)
        modul = small[: 3 * width].reshape(3, tp_size, 1, part_cols)
        gain = small[3 * width :].reshape(2, head_dim)
        multiple = jnp.where(is_own, multiple_own, multiple_other)
        given.append(
            (meta, modul[0], modul[1], modul[2], gain, multiple)
        )

    for section in range(2):
        begun = given[section][0]
        if section == 0:
            blocks, given, slices, wo_other = lax.optimization_barrier(
                (blocks, given, slices, wo_other)
            )
        else:
            blocks = gather_features(hidden)
            hidden1 = hidden.reshape(kv.shape)
            begun = shifted(hidden[:16, :HEAD_DIM], "segment", 1)
            early = exchanged(after(kv, begun))
            blocks, early = lax.optimization_barrier((blocks, early))
            got_early = shifted(early, "segment", 1)
        meta, shift, scale, gates, gain, times = given[section]
        q_own, kv, *going = project(
            meta,
            blocks,
            shift,
            scale,
            gain,
            w_own,
            w_other,
            begun,
            stale if section > 0 else None,
            (patches, rows_core, 2 * heads_cols),
        )
        if section == 0:
            going = choose_alone(meta, kv, stale)
        to_below, to_above, to_far = going
        far = along_ring(to_far, seq_size // 2 + 1, patches)
        above = along_ring(to_below, 1, patches)
        below = along_ring(to_above, -1, patches)
        q_other = shifted(q_own, "segment", 1)
        if section == 0:
            wo_prev, wo_next = after(slices, q_other, to_far)
            wo_prev, wo_next = shifted(wo_prev, "tp", 1), shifted(wo_next, "tp", 3)
            far, wo_prev, wo_next = lax.optimization_barrier((far, wo_prev, wo_next))
            wo_own.append(paired(wo_prev, wo_next))
        before = attend_own(q_own, q_other, kv, times)
        part_own, part_other = attend_rest(
            q_own, q_other, below, above, far, times, before
        )
        part_back = shifted(part_other, "segment", 1)
        if section == 0:
            wo_other.append(shifted(after(wo_own[1], part_back), "segment", 1))
        else:
            part_back, got_early = lax.optimization_barrier((part_back, got_early))
        att = merge(part_own, part_back)
        across = shifted(att, "tp", 2)
        atts = [att, across, shifted(att, "tp", 1), shifted(att, "tp", 3)]
        hidden = output(meta, atts, wo_own, wo_other, hidden, gates)

    home = exchanged(join(hidden1, kv, hidden.reshape(kv.shape)))
    got = shifted(home, "segment", 1)
    handed, new_cache = collect(core_scalar, early, got_early, home, got)
    return (handed[None], new_cache[None])


def solution(mesh):
    in_specs = (
        P(None, "seq", "tp"),
        P("segment", None, None, "tp"),
        P("segment", "tp", None),
        P("segment", None, None),
        P("segment", None, None),
        P("segment", None, None, "seq", "tp"),
        P("segment", None, None),
        P("segment", None),
        P(),
    )
    out_specs = (P("segment", None, "seq", "tp"), P("segment", None, None, "seq", "tp"))
    return jax.shard_map(local, mesh=mesh, in_specs=in_specs, out_specs=out_specs, check_vma=False)
```

```python
import jax
import jax.numpy as jnp
from jax import lax
from jax.experimental import pallas as pl
from jax.experimental.pallas import tpu as pltpu
from jax.sharding import PartitionSpec as P

EPS = 1e-06
HEAD_DIM = 128
REACH = 3
MIB = 1024 * 1024
ON_CHIP = pl.BlockSpec(memory_space=pltpu.VMEM)
SCALARS = pl.BlockSpec(memory_space=pltpu.SMEM)
ANYWHERE = pl.BlockSpec(memory_space=pl.ANY)


def shifted(block, axis, distance):
    devices = range(lax.axis_size(axis))
    route = [((i - distance) % len(devices), i) for i in devices]
    return lax.ppermute(block, axis, route)


def after(values, *gates):
    return lax.optimization_barrier((values, gates))[0]


def params(mib):
    return pltpu.CompilerParams(vmem_limit_bytes=mib * MIB)


def struct(shape, dtype=jnp.bfloat16):
    return jax.ShapeDtypeStruct(shape, dtype)


def exchanged(tiles):
    group = tiles.shape[0]
    groups = [list(range(i, i + group)) for i in range(0, lax.axis_size("seq"), group)]
    return lax.all_to_all(tiles, "seq", 0, 0, axis_index_groups=groups)


def along_ring(block, distance, per_chip):
    size = lax.axis_size("seq")
    share = size // per_chip
    place = [per_chip * (i % share) + i // share for i in range(size)]
    route = [(place[(i + distance) % size], place[i]) for i in range(size)]
    return lax.ppermute(block, "seq", route)


def halve_kernel(core, stale, mine, theirs, sems):
    rows, cols = mine.shape[1], stale.shape[-1]
    copies = []
    for place, out in enumerate((mine, theirs)):
        first = core[0] if place == 0 else 1 - core[0]
        first = pl.multiple_of(first * rows, rows)
        for half in range(2):
            copies.append(
                pltpu.make_async_copy(
                    stale.at[half, :, pl.ds(first, rows)],
                    out.at[:, :, half * cols : (half + 1) * cols],
                    sems.at[2 * place + half],
                )
            )
    for copy in copies:
        copy.start()
    for copy in copies:
        copy.wait()


def halve(core, stale):
    _, patches, rows, cols = stale.shape
    return pl.pallas_call(
        halve_kernel,
        in_specs=[SCALARS, ANYWHERE],
        out_specs=[ON_CHIP] * 2,
        out_shape=[struct((patches, rows // 2, 2 * cols))] * 2,
        scratch_shapes=[pltpu.SemaphoreType.DMA((4,))],
        compiler_params=params(8),
        name="halve",
    )(core, stale)


def join_kernel(*refs):
    *parts, out, sems = refs
    rows = parts[0].shape[1]
    copies = [
        pltpu.make_async_copy(part, out.at[:, i * rows : (i + 1) * rows], sems.at[i])
        for i, part in enumerate(parts)
    ]
    for copy in copies:
        copy.start()
    for copy in copies:
        copy.wait()


def join(*parts):
    tiles, rows, cols = parts[0].shape
    return pl.pallas_call(
        join_kernel,
        in_specs=[ANYWHERE] * len(parts),
        out_specs=ON_CHIP,
        out_shape=struct((tiles, len(parts) * rows, cols)),
        scratch_shapes=[pltpu.SemaphoreType.DMA((len(parts),))],
        compiler_params=params(8),
        name="join",
    )(*parts)


def collect_kernel(core, early, got_early, home, got, handed, cache):
    rows, cols = early.shape[1], cache.shape[-1]
    features1, keys1, features2 = (slice(i * rows, (i + 1) * rows) for i in range(3))

    def collect(features, feature_refs, keys, key_refs):
        for half in range(2):
            here = slice(half * rows, (half + 1) * rows)
            handed[:, here] = feature_refs[half][:, features]
            for which in range(2):
                cut = slice(which * cols, (which + 1) * cols)
                cache[which, :, here] = key_refs[half][:, keys, cut]

    @pl.when(core[0] == 0)
    def _():
        collect(features2, (home, got), slice(0, rows), (early, got_early))

    @pl.when(core[0] == 1)
    def _():
        collect(features1, (got, home), keys1, (got, home))


def collect(core, early, got_early, home, got):
    patches, rows, cols = early.shape
    return pl.pallas_call(
        collect_kernel,
        in_specs=[SCALARS] + [ON_CHIP] * 4,
        out_specs=[ON_CHIP] * 2,
        out_shape=[
            struct((patches, 2 * rows, cols)),
            struct((2, patches, 2 * rows, cols // 2)),
        ],
        compiler_params=params(8),
        name="collect",
    )(core, early, got_early, home, got)


def choose(meta, kv, stale, outs):
    tiles, rows, _ = kv.shape
    old = pl.ds(pl.multiple_of((1 - meta[1]) * rows, rows), rows)
    for place, out in enumerate(outs):
        first = tiles - REACH if place == 1 else 0
        cut = slice(first, first + out.shape[0])

        @pl.when(meta[2 + place] == 1)
        def _():
            out[...] = kv[cut]

        @pl.when(meta[2 + place] == 0)
        def _():
            out[...] = stale[cut, old]


def choose_kernel(meta, kv, stale, lo_out, hi_out, far_out):
    choose(meta, kv, stale, (lo_out, hi_out, far_out))


def payloads(kv_shape):
    edge = struct((REACH,) + kv_shape[1:])
    return [edge, edge, struct(kv_shape)]


def choose_alone(meta, kv, stale):
    return pl.pallas_call(
        choose_kernel,
        in_specs=[SCALARS] + [ON_CHIP] * 2,
        out_specs=[ON_CHIP] * 3,
        out_shape=payloads(kv.shape),
        compiler_params=params(8),
        name="choose",
    )(meta, kv, stale)


def project_kernel(meta, *refs, with_stale):
    blocks = refs[:4]
    shift, scale, gain, w_own, w_other, _ = refs[4:10]
    refs = refs[10:]
    if with_stale:
        stale, q_out, kv_out, *outs = refs[:-4]
    else:
        q_out, kv_out = refs[:-4]
    xs, modded, weights, sems = refs[-4:]
    _, rows, cols = xs.shape
    tiles, rows_tile, kv_cols = kv_out.shape
    heads_cols = kv_cols // 2
    parts = shift.shape[0]
    width = cols * parts
    features = [lax.rem(meta[0] + j, parts) for j in (2, 1, 3, 0)]

    def fetch(j, source):
        first = pl.multiple_of(features[j] * cols, cols)
        return pltpu.make_async_copy(
            source.at[:, pl.ds(first, cols)],
            weights.at[:, j * cols : (j + 1) * cols],
            sems.at[j],
        )

    arriving = [
        pltpu.make_async_copy(blocks[j], xs.at[j], sems.at[parts + j]) for j in range(parts)
    ]
    for copy in arriving:
        copy.start()
    for chosen, source in enumerate((w_other, w_own)):

        @pl.when(meta[1] == chosen)
        def _():
            for j in range(parts):
                fetch(j, source).start()

    for copy in arriving:
        copy.wait()
    total = jnp.zeros((rows, 1), jnp.float32)
    for j in range(parts):
        total += jnp.sum(xs[j].astype(jnp.float32), axis=-1, keepdims=True)
    mean = total / width
    square = jnp.zeros((rows, 1), jnp.float32)
    for j in range(parts):
        centred = xs[j].astype(jnp.float32) - mean
        square += jnp.sum(centred * centred, axis=-1, keepdims=True)
    spread = lax.rsqrt(square / width + EPS)
    for j in range(parts):
        normed = (xs[j].astype(jnp.float32) - mean) * spread
        modded[:, j * cols : (j + 1) * cols] = (
            normed * (1.0 + scale[features[j]]) + shift[features[j]]
        ).astype(jnp.bfloat16)
    for j in range(parts):
        fetch(j, w_own).wait()

    for part in (1, 2, 0):
        product = jnp.dot(modded[...], weights[part], preferred_element_type=jnp.float32)
        if part == 2:
            kv_out[:, :, heads_cols:] = product.astype(jnp.bfloat16).reshape(
                tiles, rows_tile, heads_cols
            )
            continue
        for head in range(heads_cols // HEAD_DIM):
            cut = slice(head * HEAD_DIM, (head + 1) * HEAD_DIM)
            vec = product[:, cut]
            mean_sq = jnp.mean(vec * vec, axis=-1, keepdims=True)
            vec = vec * lax.rsqrt(mean_sq + EPS) * gain[part : part + 1]
            vec = vec.astype(jnp.bfloat16).reshape(tiles, rows_tile, HEAD_DIM)
            if part == 0:
                q_out[:, :, cut] = vec
            else:
                kv_out[:, :, cut] = vec
    if with_stale:
        choose(meta, kv_out, stale, outs)


def project(meta, blocks, shift, scale, gain, w_own, w_other, begun, stale, kv_shape):
    rows, cols = blocks[0].shape
    tiles, rows_tile, kv_cols = kv_shape
    parts = shift.shape[0]
    heads_cols = kv_cols // 2
    shapes = [struct((tiles, rows_tile, heads_cols)), struct(kv_shape)]
    extra = []
    if stale is not None:
        shapes += payloads(kv_shape)
        extra = [stale]

    def kernel(*refs):
        project_kernel(*refs, with_stale=stale is not None)

    return pl.pallas_call(
        kernel,
        in_specs=[SCALARS]
        + [ANYWHERE] * len(blocks)
        + [ON_CHIP] * 3
        + [ANYWHERE] * 3
        + [ON_CHIP] * len(extra),
        out_specs=[ON_CHIP] * len(shapes),
        out_shape=shapes,
        scratch_shapes=[
            pltpu.VMEM((parts, rows, cols), jnp.bfloat16),
            pltpu.VMEM((rows, parts * cols), jnp.bfloat16),
            pltpu.VMEM((3, parts * cols, heads_cols), jnp.bfloat16),
            pltpu.SemaphoreType.DMA((2 * parts,)),
        ],
        compiler_params=params(52),
        name="project",
    )(meta, *blocks, shift, scale, gain, w_own, w_other, begun, *extra)


def soften(queries, keys, values, times, floors):
    scores = [
        lax.dot_general(q, k, (((1,), (1,)), ((), ())), preferred_element_type=jnp.float32)
        for q, k in zip(queries, keys)
    ]
    scores = [
        jnp.where(count > 0.0, each * HEAD_DIM ** (-0.5), -1e30)
        for each, count in zip(scores, times)
    ]
    peaks = [jnp.max(each, axis=-1, keepdims=True) for each in scores]
    if floors is not None:
        peaks = [jnp.maximum(peak, floor) for peak, floor in zip(peaks, floors)]
    weights = [
        jnp.exp(each - peak) * count for each, peak, count in zip(scores, peaks, times)
    ]
    totals = [jnp.sum(each, axis=-1, keepdims=True) for each in weights]
    summed = [
        jnp.dot(each.astype(jnp.bfloat16), v, preferred_element_type=jnp.float32)
        for each, v in zip(weights, values)
    ]
    return peaks, totals, summed


def head_cuts(heads_cols):
    return [slice(first, first + HEAD_DIM) for first in range(0, heads_cols, HEAD_DIM)]


def packed(peaks, totals):
    lane = lax.broadcasted_iota(jnp.int32, (peaks[0].shape[0], HEAD_DIM), 1)
    out = jnp.zeros((peaks[0].shape[0], HEAD_DIM), jnp.float32)
    for head, (peak, total) in enumerate(zip(peaks, totals)):
        out = jnp.where(lane == head, peak, out)
        out = jnp.where(lane == 64 + head, total, out)
    return out


def attend_own_kernel(q_own, q_other, own, multiple, out):
    tiles, rows, heads_cols = q_own.shape
    cuts = head_cuts(heads_cols)
    for tile in range(tiles):
        first, last = max(0, tile - REACH), min(tiles, tile + REACH + 1)
        count = (last - first) * rows
        both = own[first:last].reshape(count, 2 * heads_cols)
        queries = jnp.concatenate([q_own[tile], q_other[tile]], axis=0)
        peaks, totals, summed = soften(
            [queries[:, cut] for cut in cuts],
            [both[:, cut] for cut in cuts],
            [both[:, heads_cols + cut.start : heads_cols + cut.stop] for cut in cuts],
            [multiple[tile, :, :count]] * len(cuts),
            None,
        )
        for cut, each in zip(cuts, summed):
            out[tile, :, cut] = each
        out[tile, :, heads_cols:] = packed(peaks, totals)


def attend_own(q_own, q_other, own, multiple):
    tiles, rows, heads_cols = q_own.shape
    return pl.pallas_call(
        attend_own_kernel,
        in_specs=[ON_CHIP] * 4,
        out_specs=ON_CHIP,
        out_shape=struct((tiles, 2 * rows, heads_cols + HEAD_DIM), jnp.float32),
        compiler_params=params(8),
        name="attend_own",
    )(q_own, q_other, own, multiple)


def attend_rest_kernel(q_own, q_other, below, above, far, multiple, before, out_own, out_other):
    tiles, rows, heads_cols = q_own.shape
    cuts = head_cuts(heads_cols)
    heads = len(cuts)
    for pair in range(0, tiles, 2):
        queries, keys, values, times, floors, earlier = [], [], [], [], [], []
        for tile in (pair, pair + 1):
            pieces = [below[place] for place in range(tile, REACH)]
            pieces += [above[place] for place in range(tile + REACH + 1 - tiles)]
            pieces += [far[tile]]
            both = jnp.concatenate(pieces, axis=0)
            asked = jnp.concatenate([q_own[tile], q_other[tile]], axis=0)
            extra = before[tile, :, heads_cols:]
            queries += [asked[:, cut] for cut in cuts]
            keys += [both[:, cut] for cut in cuts]
            values += [both[:, heads_cols + cut.start : heads_cols + cut.stop] for cut in cuts]
            times += [multiple[tile, :, 256 : 256 + both.shape[0]]] * heads
            floors += [extra[:, head : head + 1] for head in range(heads)]
            earlier += [extra[:, 64 + head : 65 + head] for head in range(heads)]
        peaks, totals, summed = soften(queries, keys, values, times, floors)
        shrink = [jnp.exp(floor - peak) for floor, peak in zip(floors, peaks)]
        totals = [total + old * less for total, old, less in zip(totals, earlier, shrink)]
        for place, tile in enumerate((pair, pair + 1)):
            here = slice(place * heads, (place + 1) * heads)
            for cut, each, less in zip(cuts, summed[here], shrink[here]):
                result = each + before[tile, :, cut] * less
                out_own[tile, :, cut] = result[:rows]
                out_other[tile, :, cut] = result[rows:]
            extra = packed(peaks[here], totals[here])
            out_own[tile, :, heads_cols:] = extra[:rows]
            out_other[tile, :, heads_cols:] = extra[rows:]


def attend_rest(q_own, q_other, below, above, far, multiple, before):
    tiles, rows, heads_cols = q_own.shape
    return pl.pallas_call(
        attend_rest_kernel,
        in_specs=[ON_CHIP] * 7,
        out_specs=[ON_CHIP] * 2,
        out_shape=[struct((tiles, rows, heads_cols + HEAD_DIM), jnp.float32)] * 2,
        compiler_params=params(8),
        name="attend_rest",
    )(q_own, q_other, below, above, far, multiple, before)


def merge_kernel(part_a, part_b, att):
    tiles, rows, _ = part_a.shape
    heads_cols = att.shape[-1]
    extra_a = part_a[:, :, heads_cols:].reshape(tiles * rows, HEAD_DIM)
    extra_b = part_b[:, :, heads_cols:].reshape(tiles * rows, HEAD_DIM)
    for head, cut in enumerate(head_cuts(heads_cols)):
        peak_a, total_a = extra_a[:, head : head + 1], extra_a[:, 64 + head : 65 + head]
        peak_b, total_b = extra_b[:, head : head + 1], extra_b[:, 64 + head : 65 + head]
        peak = jnp.maximum(peak_a, peak_b)
        grow_a, grow_b = jnp.exp(peak_a - peak), jnp.exp(peak_b - peak)
        total = total_a * grow_a + total_b * grow_b
        summed_a = part_a[:, :, cut].reshape(tiles * rows, HEAD_DIM)
        summed_b = part_b[:, :, cut].reshape(tiles * rows, HEAD_DIM)
        att[:, cut] = (summed_a * (grow_a / total) + summed_b * (grow_b / total)).astype(
            jnp.bfloat16
        )


def merge(part_a, part_b):
    tiles, rows, cols = part_a.shape
    return pl.pallas_call(
        merge_kernel,
        in_specs=[ON_CHIP] * 2,
        out_specs=ON_CHIP,
        out_shape=struct((tiles * rows, cols - HEAD_DIM)),
        compiler_params=params(8),
        name="merge",
    )(part_a, part_b)


def output_kernel(meta, *refs):
    atts, own, other = refs[:4], refs[4:6], refs[6:8]
    hidden, gates, out, weights, sems = refs[8:]
    rows = atts[0].shape[1]

    def fetch(pair, sources):
        return pltpu.make_async_copy(sources[pair], weights.at[pair], sems.at[pair])

    for chosen, sources in enumerate((other, own)):

        @pl.when(meta[1] == chosen)
        def _():
            for pair in range(2):
                fetch(pair, sources).start()

    product = jnp.zeros(out.shape, jnp.float32)
    for j, att in enumerate(atts):
        if j % 2 == 0:
            fetch(j // 2, own).wait()
        weight = weights[j // 2, (j % 2) * rows : (j % 2 + 1) * rows]
        product += jnp.dot(att[...], weight, preferred_element_type=jnp.float32)
    out[...] = (hidden[...].astype(jnp.float32) + gates[meta[0]] * product).astype(out.dtype)


def output(meta, atts, own, other, hidden, gates):
    return pl.pallas_call(
        output_kernel,
        in_specs=[SCALARS] + [ON_CHIP] * 4 + [ANYWHERE] * 4 + [ON_CHIP] * 2,
        out_specs=ON_CHIP,
        out_shape=struct(hidden.shape),
        scratch_shapes=[
            pltpu.VMEM((2,) + own[0].shape, jnp.bfloat16),
            pltpu.SemaphoreType.DMA((2,)),
        ],
        compiler_params=params(12),
        name="output",
    )(meta, *atts, *own, *other, hidden, gates)


def paired(first, second):
    rows, cols = first.shape
    return join(first[None], second[None]).reshape(2 * rows, cols)


def count_tiles(table, counts, chip, per_chip, repeat):
    tiles, slots = table.shape
    table = lax.dynamic_slice_in_dim(table, chip * per_chip, per_chip, 0)
    counts = lax.dynamic_slice_in_dim(counts, chip * per_chip, per_chip, 0)
    query_tiles = jnp.arange(per_chip, dtype=jnp.int32) + chip * per_chip
    across = tiles // 2 + (tiles // per_chip) // 2
    rows = []
    for tile in range(per_chip):
        first, last = max(0, tile - REACH), min(per_chip, tile + REACH + 1)
        own = [place - tile for place in range(first, last)]
        rest = [place - REACH - tile for place in range(tile, REACH)]
        rest += [per_chip + place - tile for place in range(tile + REACH + 1 - per_chip)]
        rest += [across]
        own = [d % tiles for d in own] + [-1] * (256 // repeat - len(own))
        rest = [d % tiles for d in rest] + [-1] * (128 // repeat - len(rest))
        rows.append([d for d in own + rest for _ in range(repeat)])
    reach = jnp.array(rows, jnp.int32)
    relative = (table - query_tiles[:, None]) % tiles
    live = jnp.arange(slots, dtype=jnp.int32)[None] < counts[:, None]
    hits = (relative[:, :, None] == reach[:, None]) & live[:, :, None]
    return jnp.sum(hits.astype(jnp.float32), axis=1)[:, None]


def gather_features(hidden):
    across = shifted(hidden, "tp", 2)
    return across, shifted(hidden, "tp", -1), shifted(hidden, "tp", 1), hidden


def local(
    latents, w_qkv, w_out, modulation, qk_gain, stale_cache, kv_tiles, tile_counts, patch_order
):
    core = lax.axis_index("segment")
    seq_size = lax.axis_size("seq")
    seq_pos = lax.axis_index("seq")
    tp_size = lax.axis_size("tp")
    tp_pos = lax.axis_index("tp")
    patches, patch_rows, part_cols = latents.shape
    rows_core = patch_rows // 2
    rows = patches * rows_core
    share = seq_size // patches
    chip = share * lax.rem(seq_pos, patches) + seq_pos // patches
    w_own = jnp.transpose(w_qkv[0], (1, 0, 2))
    heads_cols, width = w_out.shape[1:]
    head_dim = qk_gain.shape[-1]

    core_scalar = core.astype(jnp.int32)[None]
    def columns(weight, j):
        first = lax.rem(tp_pos + j, tp_size) * part_cols
        return lax.dynamic_slice_in_dim(weight, first, part_cols, 1)

    wo_across = columns(w_out[0], 2)
    mine = lax.dynamic_slice_in_dim(after(latents, wo_across), core * rows_core, rows_core, 1)
    wo_across = shifted(wo_across, "tp", 2)
    hidden = exchanged(mine).reshape(rows, part_cols)
    stale, stale_send = halve(core_scalar, after(stale_cache[0], mine))
    stale_got = shifted(stale_send, "segment", 1)
    w_other = shifted(w_own, "segment", 1)
    stale = join(stale, stale_got)
    weight = after(w_out[0], stale_got)
    slices = [columns(weight, j) for j in (0, 1, 3)]
    hidden, stale, wo_across, slices = lax.optimization_barrier(
        (hidden, stale, wo_across, slices)
    )
    small_own = jnp.concatenate([modulation[0].reshape(-1), qk_gain[0].reshape(-1)])
    small_other = shifted(small_own, "segment", 1)
    blocks = gather_features(hidden)
    stale, slices, kv_tiles, tile_counts, patch_order, small_own, small_other = after(
        (stale, slices, kv_tiles, tile_counts, patch_order, small_own, small_other), blocks[0]
    )
    stale = exchanged(stale)
    wo_own = [paired(slices[0], wo_across)]
    wo_other = [shifted(wo_own[0], "segment", 1)]
    turns = jnp.arange(patches, dtype=jnp.int32)
    asked = jnp.stack([chip, chip - 1, chip + 1, chip - seq_size // 2 - 1]) % seq_size // share
    ranks = jnp.sum(jnp.where(patch_order[None] == asked[:, None], turns[None], 0), axis=-1)
    fresh = (ranks[0] <= ranks[1:]).astype(jnp.int32)
    multiple_own = count_tiles(kv_tiles[0], tile_counts[0], chip, patches, rows_core)
    multiple_other = shifted(multiple_own, "segment", 1)
    given = []
    for section in range(2):
        is_own = core == section
        meta = jnp.concatenate(
            [jnp.stack([tp_pos, is_own.astype(tp_pos.dtype)]).astype(jnp.int32), fresh]
        )
        small = jnp.where(is_own, small_own, small_other)
        modul = small[: 3 * width].reshape(3, tp_size, 1, part_cols)
        gain = small[3 * width :].reshape(2, head_dim)
        multiple = jnp.where(is_own, multiple_own, multiple_other)
        given.append(
            (meta, modul[0], modul[1], modul[2], gain, multiple)
        )

    for section in range(2):
        begun = given[section][0]
        if section == 0:
            blocks, given, slices, wo_other = lax.optimization_barrier(
                (blocks, given, slices, wo_other)
            )
        else:
            blocks = gather_features(hidden)
            hidden1 = hidden.reshape(kv.shape)
            begun = shifted(hidden[:16, :HEAD_DIM], "segment", 1)
            early = exchanged(after(kv, begun))
            blocks, early = lax.optimization_barrier((blocks, early))
            got_early = shifted(early, "segment", 1)
        meta, shift, scale, gates, gain, times = given[section]
        q_own, kv, *going = project(
            meta,
            blocks,
            shift,
            scale,
            gain,
            w_own,
            w_other,
            begun,
            stale if section > 0 else None,
            (patches, rows_core, 2 * heads_cols),
        )
        if section == 0:
            going = choose_alone(meta, kv, stale)
        to_below, to_above, to_far = going
        far = along_ring(to_far, seq_size // 2 + 1, patches)
        above = along_ring(to_below, 1, patches)
        below = along_ring(to_above, -1, patches)
        q_other = shifted(q_own, "segment", 1)
        if section == 0:
            wo_prev, wo_next = after(slices[1:], q_other, to_far)
            wo_prev, wo_next = shifted(wo_prev, "tp", 1), shifted(wo_next, "tp", 3)
            far, wo_prev, wo_next = lax.optimization_barrier((far, wo_prev, wo_next))
            wo_own.append(paired(wo_prev, wo_next))
        before = attend_own(q_own, q_other, kv, times)
        part_own, part_other = attend_rest(
            q_own, q_other, below, above, far, times, before
        )
        part_back = shifted(part_other, "segment", 1)
        if section == 0:
            wo_other.append(shifted(after(wo_own[1], part_back), "segment", 1))
        else:
            part_back, got_early = lax.optimization_barrier((part_back, got_early))
        att = merge(part_own, part_back)
        across = shifted(att, "tp", 2)
        atts = [att, across, shifted(att, "tp", 1), shifted(att, "tp", 3)]
        hidden = output(meta, atts, wo_own, wo_other, hidden, gates)

    home = exchanged(join(hidden1, kv, hidden.reshape(kv.shape)))
    got = shifted(home, "segment", 1)
    handed, new_cache = collect(core_scalar, early, got_early, home, got)
    return (handed[None], new_cache[None])


def solution(mesh):
    in_specs = (
        P(None, "seq", "tp"),
        P("segment", None, None, "tp"),
        P("segment", "tp", None),
        P("segment", None, None),
        P("segment", None, None),
        P("segment", None, None, "seq", "tp"),
        P("segment", None, None),
        P("segment", None),
        P(),
    )
    out_specs = (P("segment", None, "seq", "tp"), P("segment", None, None, "seq", "tp"))
    return jax.shard_map(local, mesh=mesh, in_specs=in_specs, out_specs=out_specs, check_vma=False)
```

```python
import jax
import jax.numpy as jnp
from jax import lax
from jax.experimental import pallas as pl
from jax.experimental.pallas import tpu as pltpu
from jax.sharding import PartitionSpec as P

EPS = 1e-06
HEAD_DIM = 128
REACH = 3
MIB = 1024 * 1024
ON_CHIP = pl.BlockSpec(memory_space=pltpu.VMEM)
SCALARS = pl.BlockSpec(memory_space=pltpu.SMEM)
ANYWHERE = pl.BlockSpec(memory_space=pl.ANY)


def shifted(block, axis, distance):
    devices = range(lax.axis_size(axis))
    route = [((i - distance) % len(devices), i) for i in devices]
    return lax.ppermute(block, axis, route)


def after(values, *gates):
    return lax.optimization_barrier((values, gates))[0]


def params(mib):
    return pltpu.CompilerParams(vmem_limit_bytes=mib * MIB)


def struct(shape, dtype=jnp.bfloat16):
    return jax.ShapeDtypeStruct(shape, dtype)


def exchanged(tiles):
    group = tiles.shape[0]
    groups = [list(range(i, i + group)) for i in range(0, lax.axis_size("seq"), group)]
    return lax.all_to_all(tiles, "seq", 0, 0, axis_index_groups=groups)


def along_ring(block, distance, per_chip):
    size = lax.axis_size("seq")
    share = size // per_chip
    place = [per_chip * (i % share) + i // share for i in range(size)]
    route = [(place[(i + distance) % size], place[i]) for i in range(size)]
    return lax.ppermute(block, "seq", route)


def halve_kernel(core, stale, mine, theirs, sems):
    rows, cols = mine.shape[1], stale.shape[-1]
    copies = []
    for place, out in enumerate((mine, theirs)):
        first = core[0] if place == 0 else 1 - core[0]
        first = pl.multiple_of(first * rows, rows)
        for half in range(2):
            copies.append(
                pltpu.make_async_copy(
                    stale.at[half, :, pl.ds(first, rows)],
                    out.at[:, :, half * cols : (half + 1) * cols],
                    sems.at[2 * place + half],
                )
            )
    for copy in copies:
        copy.start()
    for copy in copies:
        copy.wait()


def halve(core, stale):
    _, patches, rows, cols = stale.shape
    return pl.pallas_call(
        halve_kernel,
        in_specs=[SCALARS, ANYWHERE],
        out_specs=[ON_CHIP] * 2,
        out_shape=[struct((patches, rows // 2, 2 * cols))] * 2,
        scratch_shapes=[pltpu.SemaphoreType.DMA((4,))],
        compiler_params=params(8),
        name="halve",
    )(core, stale)


def join_kernel(*refs):
    *parts, out, sems = refs
    rows = parts[0].shape[1]
    copies = [
        pltpu.make_async_copy(part, out.at[:, i * rows : (i + 1) * rows], sems.at[i])
        for i, part in enumerate(parts)
    ]
    for copy in copies:
        copy.start()
    for copy in copies:
        copy.wait()


def join(*parts):
    tiles, rows, cols = parts[0].shape
    return pl.pallas_call(
        join_kernel,
        in_specs=[ANYWHERE] * len(parts),
        out_specs=ON_CHIP,
        out_shape=struct((tiles, len(parts) * rows, cols)),
        scratch_shapes=[pltpu.SemaphoreType.DMA((len(parts),))],
        compiler_params=params(8),
        name="join",
    )(*parts)


def collect_kernel(core, early, got_early, home, got, handed, cache):
    rows, cols = early.shape[1], cache.shape[-1]
    features1, keys1, features2 = (slice(i * rows, (i + 1) * rows) for i in range(3))

    def collect(features, feature_refs, keys, key_refs):
        for half in range(2):
            here = slice(half * rows, (half + 1) * rows)
            handed[:, here] = feature_refs[half][:, features]
            for which in range(2):
                cut = slice(which * cols, (which + 1) * cols)
                cache[which, :, here] = key_refs[half][:, keys, cut]

    @pl.when(core[0] == 0)
    def _():
        collect(features2, (home, got), slice(0, rows), (early, got_early))

    @pl.when(core[0] == 1)
    def _():
        collect(features1, (got, home), keys1, (got, home))


def collect(core, early, got_early, home, got):
    patches, rows, cols = early.shape
    return pl.pallas_call(
        collect_kernel,
        in_specs=[SCALARS] + [ON_CHIP] * 4,
        out_specs=[ON_CHIP] * 2,
        out_shape=[
            struct((patches, 2 * rows, cols)),
            struct((2, patches, 2 * rows, cols // 2)),
        ],
        compiler_params=params(8),
        name="collect",
    )(core, early, got_early, home, got)


def choose(meta, kv, stale, outs):
    tiles, rows, _ = kv.shape
    old = pl.ds(pl.multiple_of((1 - meta[1]) * rows, rows), rows)
    for place, out in enumerate(outs):
        first = tiles - REACH if place == 1 else 0
        cut = slice(first, first + out.shape[0])

        @pl.when(meta[2 + place] == 1)
        def _():
            out[...] = kv[cut]

        @pl.when(meta[2 + place] == 0)
        def _():
            out[...] = stale[cut, old]


def choose_kernel(meta, kv, stale, lo_out, hi_out, far_out):
    choose(meta, kv, stale, (lo_out, hi_out, far_out))


def payloads(kv_shape):
    edge = struct((REACH,) + kv_shape[1:])
    return [edge, edge, struct(kv_shape)]


def choose_alone(meta, kv, stale):
    return pl.pallas_call(
        choose_kernel,
        in_specs=[SCALARS] + [ON_CHIP] * 2,
        out_specs=[ON_CHIP] * 3,
        out_shape=payloads(kv.shape),
        compiler_params=params(8),
        name="choose",
    )(meta, kv, stale)


def project_kernel(meta, *refs, with_stale):
    blocks = refs[:4]
    shift, scale, gain, w_own, w_other, _ = refs[4:10]
    refs = refs[10:]
    if with_stale:
        stale, q_out, kv_out, *outs = refs[:-4]
    else:
        q_out, kv_out = refs[:-4]
    xs, modded, weights, sems = refs[-4:]
    _, rows, cols = xs.shape
    tiles, rows_tile, kv_cols = kv_out.shape
    heads_cols = kv_cols // 2
    parts = shift.shape[0]
    width = cols * parts
    features = [lax.rem(meta[0] + j, parts) for j in (2, 1, 3, 0)]

    def fetch(j, source):
        first = pl.multiple_of(features[j] * cols, cols)
        return pltpu.make_async_copy(
            source.at[:, pl.ds(first, cols)],
            weights.at[:, j * cols : (j + 1) * cols],
            sems.at[j],
        )

    arriving = [
        pltpu.make_async_copy(blocks[j], xs.at[j], sems.at[parts + j]) for j in range(parts)
    ]
    for copy in arriving:
        copy.start()
    for chosen, source in enumerate((w_other, w_own)):

        @pl.when(meta[1] == chosen)
        def _():
            for j in range(parts):
                fetch(j, source).start()

    for copy in arriving:
        copy.wait()
    total = jnp.zeros((rows, 1), jnp.float32)
    for j in range(parts):
        total += jnp.sum(xs[j].astype(jnp.float32), axis=-1, keepdims=True)
    mean = total / width
    square = jnp.zeros((rows, 1), jnp.float32)
    for j in range(parts):
        centred = xs[j].astype(jnp.float32) - mean
        square += jnp.sum(centred * centred, axis=-1, keepdims=True)
    spread = lax.rsqrt(square / width + EPS)
    for j in range(parts):
        normed = (xs[j].astype(jnp.float32) - mean) * spread
        modded[:, j * cols : (j + 1) * cols] = (
            normed * (1.0 + scale[features[j]]) + shift[features[j]]
        ).astype(jnp.bfloat16)
    for j in range(parts):
        fetch(j, w_own).wait()

    for part in (1, 2, 0):
        product = jnp.dot(modded[...], weights[part], preferred_element_type=jnp.float32)
        if part == 2:
            kv_out[:, :, heads_cols:] = product.astype(jnp.bfloat16).reshape(
                tiles, rows_tile, heads_cols
            )
            continue
        for head in range(heads_cols // HEAD_DIM):
            cut = slice(head * HEAD_DIM, (head + 1) * HEAD_DIM)
            vec = product[:, cut]
            mean_sq = jnp.mean(vec * vec, axis=-1, keepdims=True)
            vec = vec * lax.rsqrt(mean_sq + EPS) * gain[part : part + 1]
            vec = vec.astype(jnp.bfloat16).reshape(tiles, rows_tile, HEAD_DIM)
            if part == 0:
                q_out[:, :, cut] = vec
            else:
                kv_out[:, :, cut] = vec
    if with_stale:
        choose(meta, kv_out, stale, outs)


def project(meta, blocks, shift, scale, gain, w_own, w_other, begun, stale, kv_shape):
    rows, cols = blocks[0].shape
    tiles, rows_tile, kv_cols = kv_shape
    parts = shift.shape[0]
    heads_cols = kv_cols // 2
    shapes = [struct((tiles, rows_tile, heads_cols)), struct(kv_shape)]
    extra = []
    if stale is not None:
        shapes += payloads(kv_shape)
        extra = [stale]

    def kernel(*refs):
        project_kernel(*refs, with_stale=stale is not None)

    return pl.pallas_call(
        kernel,
        in_specs=[SCALARS]
        + [ANYWHERE] * len(blocks)
        + [ON_CHIP] * 3
        + [ANYWHERE] * 3
        + [ON_CHIP] * len(extra),
        out_specs=[ON_CHIP] * len(shapes),
        out_shape=shapes,
        scratch_shapes=[
            pltpu.VMEM((parts, rows, cols), jnp.bfloat16),
            pltpu.VMEM((rows, parts * cols), jnp.bfloat16),
            pltpu.VMEM((3, parts * cols, heads_cols), jnp.bfloat16),
            pltpu.SemaphoreType.DMA((2 * parts,)),
        ],
        compiler_params=params(52),
        name="project",
    )(meta, *blocks, shift, scale, gain, w_own, w_other, begun, *extra)


def soften(queries, keys, values, times, floors):
    scores = [
        lax.dot_general(q, k, (((1,), (1,)), ((), ())), preferred_element_type=jnp.float32)
        for q, k in zip(queries, keys)
    ]
    scores = [
        jnp.where(count > 0.0, each * HEAD_DIM ** (-0.5), -1e30)
        for each, count in zip(scores, times)
    ]
    peaks = [jnp.max(each, axis=-1, keepdims=True) for each in scores]
    if floors is not None:
        peaks = [jnp.maximum(peak, floor) for peak, floor in zip(peaks, floors)]
    weights = [
        jnp.exp(each - peak) * count for each, peak, count in zip(scores, peaks, times)
    ]
    totals = [jnp.sum(each, axis=-1, keepdims=True) for each in weights]
    summed = [
        jnp.dot(each.astype(jnp.bfloat16), v, preferred_element_type=jnp.float32)
        for each, v in zip(weights, values)
    ]
    return peaks, totals, summed


def head_cuts(heads_cols):
    return [slice(first, first + HEAD_DIM) for first in range(0, heads_cols, HEAD_DIM)]


def packed(peaks, totals):
    lane = lax.broadcasted_iota(jnp.int32, (peaks[0].shape[0], HEAD_DIM), 1)
    out = jnp.zeros((peaks[0].shape[0], HEAD_DIM), jnp.float32)
    for head, (peak, total) in enumerate(zip(peaks, totals)):
        out = jnp.where(lane == head, peak, out)
        out = jnp.where(lane == 64 + head, total, out)
    return out


def attend_own_kernel(q_own, q_other, own, multiple, out):
    tiles, rows, heads_cols = q_own.shape
    cuts = head_cuts(heads_cols)
    for tile in range(tiles):
        first, last = max(0, tile - REACH), min(tiles, tile + REACH + 1)
        count = (last - first) * rows
        both = own[first:last].reshape(count, 2 * heads_cols)
        queries = jnp.concatenate([q_own[tile], q_other[tile]], axis=0)
        peaks, totals, summed = soften(
            [queries[:, cut] for cut in cuts],
            [both[:, cut] for cut in cuts],
            [both[:, heads_cols + cut.start : heads_cols + cut.stop] for cut in cuts],
            [multiple[tile, :, :count]] * len(cuts),
            None,
        )
        for cut, each in zip(cuts, summed):
            out[tile, :, cut] = each
        out[tile, :, heads_cols:] = packed(peaks, totals)


def attend_own(q_own, q_other, own, multiple):
    tiles, rows, heads_cols = q_own.shape
    return pl.pallas_call(
        attend_own_kernel,
        in_specs=[ON_CHIP] * 4,
        out_specs=ON_CHIP,
        out_shape=struct((tiles, 2 * rows, heads_cols + HEAD_DIM), jnp.float32),
        compiler_params=params(8),
        name="attend_own",
    )(q_own, q_other, own, multiple)


def attend_rest_kernel(q_own, q_other, below, above, far, multiple, before, out_own, out_other):
    tiles, rows, heads_cols = q_own.shape
    cuts = head_cuts(heads_cols)
    heads = len(cuts)
    for pair in range(0, tiles, 2):
        queries, keys, values, times, floors, earlier = [], [], [], [], [], []
        for tile in (pair, pair + 1):
            pieces = [below[place] for place in range(tile, REACH)]
            pieces += [above[place] for place in range(tile + REACH + 1 - tiles)]
            pieces += [far[tile]]
            both = jnp.concatenate(pieces, axis=0)
            asked = jnp.concatenate([q_own[tile], q_other[tile]], axis=0)
            extra = before[tile, :, heads_cols:]
            queries += [asked[:, cut] for cut in cuts]
            keys += [both[:, cut] for cut in cuts]
            values += [both[:, heads_cols + cut.start : heads_cols + cut.stop] for cut in cuts]
            times += [multiple[tile, :, 256 : 256 + both.shape[0]]] * heads
            floors += [extra[:, head : head + 1] for head in range(heads)]
            earlier += [extra[:, 64 + head : 65 + head] for head in range(heads)]
        peaks, totals, summed = soften(queries, keys, values, times, floors)
        shrink = [jnp.exp(floor - peak) for floor, peak in zip(floors, peaks)]
        totals = [total + old * less for total, old, less in zip(totals, earlier, shrink)]
        for place, tile in enumerate((pair, pair + 1)):
            here = slice(place * heads, (place + 1) * heads)
            for cut, each, less in zip(cuts, summed[here], shrink[here]):
                result = each + before[tile, :, cut] * less
                out_own[tile, :, cut] = result[:rows]
                out_other[tile, :, cut] = result[rows:]
            extra = packed(peaks[here], totals[here])
            out_own[tile, :, heads_cols:] = extra[:rows]
            out_other[tile, :, heads_cols:] = extra[rows:]


def attend_rest(q_own, q_other, below, above, far, multiple, before):
    tiles, rows, heads_cols = q_own.shape
    return pl.pallas_call(
        attend_rest_kernel,
        in_specs=[ON_CHIP] * 7,
        out_specs=[ON_CHIP] * 2,
        out_shape=[struct((tiles, rows, heads_cols + HEAD_DIM), jnp.float32)] * 2,
        compiler_params=params(8),
        name="attend_rest",
    )(q_own, q_other, below, above, far, multiple, before)


def merge_kernel(part_a, part_b, att):
    tiles, rows, _ = part_a.shape
    heads_cols = att.shape[-1]
    extra_a = part_a[:, :, heads_cols:].reshape(tiles * rows, HEAD_DIM)
    extra_b = part_b[:, :, heads_cols:].reshape(tiles * rows, HEAD_DIM)
    for head, cut in enumerate(head_cuts(heads_cols)):
        peak_a, total_a = extra_a[:, head : head + 1], extra_a[:, 64 + head : 65 + head]
        peak_b, total_b = extra_b[:, head : head + 1], extra_b[:, 64 + head : 65 + head]
        peak = jnp.maximum(peak_a, peak_b)
        grow_a, grow_b = jnp.exp(peak_a - peak), jnp.exp(peak_b - peak)
        total = total_a * grow_a + total_b * grow_b
        summed_a = part_a[:, :, cut].reshape(tiles * rows, HEAD_DIM)
        summed_b = part_b[:, :, cut].reshape(tiles * rows, HEAD_DIM)
        att[:, cut] = (summed_a * (grow_a / total) + summed_b * (grow_b / total)).astype(
            jnp.bfloat16
        )


def merge(part_a, part_b):
    tiles, rows, cols = part_a.shape
    return pl.pallas_call(
        merge_kernel,
        in_specs=[ON_CHIP] * 2,
        out_specs=ON_CHIP,
        out_shape=struct((tiles * rows, cols - HEAD_DIM)),
        compiler_params=params(8),
        name="merge",
    )(part_a, part_b)


def output_kernel(meta, *refs):
    atts, own, other = refs[:4], refs[4:6], refs[6:8]
    hidden, gates, out, weights, sems = refs[8:]
    rows = atts[0].shape[1]

    def fetch(pair, sources):
        return pltpu.make_async_copy(sources[pair], weights.at[pair], sems.at[pair])

    for chosen, sources in enumerate((other, own)):

        @pl.when(meta[1] == chosen)
        def _():
            for pair in range(2):
                fetch(pair, sources).start()

    product = jnp.zeros(out.shape, jnp.float32)
    for j, att in enumerate(atts):
        if j % 2 == 0:
            fetch(j // 2, own).wait()
        weight = weights[j // 2, (j % 2) * rows : (j % 2 + 1) * rows]
        product += jnp.dot(att[...], weight, preferred_element_type=jnp.float32)
    out[...] = (hidden[...].astype(jnp.float32) + gates[meta[0]] * product).astype(out.dtype)


def output(meta, atts, own, other, hidden, gates):
    return pl.pallas_call(
        output_kernel,
        in_specs=[SCALARS] + [ON_CHIP] * 4 + [ANYWHERE] * 4 + [ON_CHIP] * 2,
        out_specs=ON_CHIP,
        out_shape=struct(hidden.shape),
        scratch_shapes=[
            pltpu.VMEM((2,) + own[0].shape, jnp.bfloat16),
            pltpu.SemaphoreType.DMA((2,)),
        ],
        compiler_params=params(12),
        name="output",
    )(meta, *atts, *own, *other, hidden, gates)


def paired(first, second):
    rows, cols = first.shape
    return join(first[None], second[None]).reshape(2 * rows, cols)


def count_tiles(table, counts, chip, per_chip, repeat):
    tiles, slots = table.shape
    table = lax.dynamic_slice_in_dim(table, chip * per_chip, per_chip, 0)
    counts = lax.dynamic_slice_in_dim(counts, chip * per_chip, per_chip, 0)
    query_tiles = jnp.arange(per_chip, dtype=jnp.int32) + chip * per_chip
    across = tiles // 2 + (tiles // per_chip) // 2
    rows = []
    for tile in range(per_chip):
        first, last = max(0, tile - REACH), min(per_chip, tile + REACH + 1)
        own = [place - tile for place in range(first, last)]
        rest = [place - REACH - tile for place in range(tile, REACH)]
        rest += [per_chip + place - tile for place in range(tile + REACH + 1 - per_chip)]
        rest += [across]
        own = [d % tiles for d in own] + [-1] * (256 // repeat - len(own))
        rest = [d % tiles for d in rest] + [-1] * (128 // repeat - len(rest))
        rows.append([d for d in own + rest for _ in range(repeat)])
    reach = jnp.array(rows, jnp.int32)
    relative = (table - query_tiles[:, None]) % tiles
    live = jnp.arange(slots, dtype=jnp.int32)[None] < counts[:, None]
    hits = (relative[:, :, None] == reach[:, None]) & live[:, :, None]
    return jnp.sum(hits.astype(jnp.float32), axis=1)[:, None]


def gather_features(hidden):
    across = shifted(hidden, "tp", 2)
    return across, shifted(hidden, "tp", -1), shifted(hidden, "tp", 1), hidden


def local(
    latents, w_qkv, w_out, modulation, qk_gain, stale_cache, kv_tiles, tile_counts, patch_order
):
    core = lax.axis_index("segment")
    seq_size = lax.axis_size("seq")
    seq_pos = lax.axis_index("seq")
    tp_size = lax.axis_size("tp")
    tp_pos = lax.axis_index("tp")
    patches, patch_rows, part_cols = latents.shape
    rows_core = patch_rows // 2
    rows = patches * rows_core
    share = seq_size // patches
    chip = share * lax.rem(seq_pos, patches) + seq_pos // patches
    w_own = jnp.transpose(w_qkv[0], (1, 0, 2))
    heads_cols, width = w_out.shape[1:]
    head_dim = qk_gain.shape[-1]

    core_scalar = core.astype(jnp.int32)[None]
    def columns(weight, j):
        first = lax.rem(tp_pos + j, tp_size) * part_cols
        return lax.dynamic_slice_in_dim(weight, first, part_cols, 1)

    wo_across = columns(w_out[0], 2)
    mine = lax.dynamic_slice_in_dim(after(latents, wo_across), core * rows_core, rows_core, 1)
    wo_across = shifted(wo_across, "tp", 2)
    hidden = exchanged(mine).reshape(rows, part_cols)
    stale, stale_send = halve(core_scalar, after(stale_cache[0], mine))
    stale_got = shifted(stale_send, "segment", 1)
    w_other = shifted(w_own, "segment", 1)
    stale = join(stale, stale_got)
    weight = after(w_out[0], stale_got)
    slices = [columns(weight, j) for j in (0, 1, 3)]
    hidden, stale, wo_across, slices = lax.optimization_barrier(
        (hidden, stale, wo_across, slices)
    )
    small_own = jnp.concatenate([modulation[0].reshape(-1), qk_gain[0].reshape(-1)])
    small_other = shifted(small_own, "segment", 1)
    blocks = gather_features(hidden)
    stale, slices, kv_tiles, tile_counts, patch_order, small_own, small_other = after(
        (stale, slices, kv_tiles, tile_counts, patch_order, small_own, small_other), blocks[0]
    )
    stale = exchanged(stale)
    wo_own = [paired(slices[0], wo_across)]
    wo_other = [shifted(wo_own[0], "segment", 1)]
    turns = jnp.arange(patches, dtype=jnp.int32)
    asked = jnp.stack([chip, chip - 1, chip + 1, chip - seq_size // 2 - 1]) % seq_size // share
    ranks = jnp.sum(jnp.where(patch_order[None] == asked[:, None], turns[None], 0), axis=-1)
    fresh = (ranks[0] <= ranks[1:]).astype(jnp.int32)
    multiple_own = count_tiles(kv_tiles[0], tile_counts[0], chip, patches, rows_core)
    multiple_other = shifted(multiple_own, "segment", 1)
    given = []
    for section in range(2):
        is_own = core == section
        meta = jnp.concatenate(
            [jnp.stack([tp_pos, is_own.astype(tp_pos.dtype)]).astype(jnp.int32), fresh]
        )
        small = jnp.where(is_own, small_own, small_other)
        modul = small[: 3 * width].reshape(3, tp_size, 1, part_cols)
        gain = small[3 * width :].reshape(2, head_dim)
        multiple = jnp.where(is_own, multiple_own, multiple_other)
        given.append(
            (meta, modul[0], modul[1], modul[2], gain, multiple)
        )

    for section in range(2):
        begun = given[section][0]
        if section == 0:
            blocks, given, slices, wo_other = lax.optimization_barrier(
                (blocks, given, slices, wo_other)
            )
        else:
            blocks = gather_features(hidden)
            hidden1 = hidden.reshape(kv.shape)
            begun = shifted(hidden[:16, :HEAD_DIM], "segment", 1)
            early = exchanged(after(kv, begun))
            blocks, early = lax.optimization_barrier((blocks, early))
            got_early = shifted(early, "segment", 1)
        meta, shift, scale, gates, gain, times = given[section]
        q_own, kv, *going = project(
            meta,
            blocks,
            shift,
            scale,
            gain,
            w_own,
            w_other,
            begun,
            stale if section > 0 else None,
            (patches, rows_core, 2 * heads_cols),
        )
        if section == 0:
            going = choose_alone(meta, kv, stale)
        to_below, to_above, to_far = going
        far = along_ring(to_far, seq_size // 2 + 1, patches)
        above = along_ring(to_below, 1, patches)
        below = along_ring(to_above, -1, patches)
        q_other = shifted(q_own, "segment", 1)
        if section == 0:
            wo_prev, wo_next = after(slices[1:], q_other, to_far)
            wo_prev, wo_next = shifted(wo_prev, "tp", 1), shifted(wo_next, "tp", 3)
        before = attend_own(q_own, q_other, kv, times)
        part_own, part_other = attend_rest(
            q_own, q_other, below, above, far, times, before
        )
        part_back = shifted(part_other, "segment", 1)
        if section == 0:
            part_back, wo_prev, wo_next = lax.optimization_barrier((part_back, wo_prev, wo_next))
            wo_own.append(paired(wo_prev, wo_next))
            wo_other.append(shifted(after(wo_own[1], part_back), "segment", 1))
        else:
            part_back, got_early = lax.optimization_barrier((part_back, got_early))
        att = merge(part_own, part_back)
        across = shifted(att, "tp", 2)
        atts = [att, across, shifted(att, "tp", 1), shifted(att, "tp", 3)]
        hidden = output(meta, atts, wo_own, wo_other, hidden, gates)

    home = exchanged(join(hidden1, kv, hidden.reshape(kv.shape)))
    got = shifted(home, "segment", 1)
    handed, new_cache = collect(core_scalar, early, got_early, home, got)
    return (handed[None], new_cache[None])


def solution(mesh):
    in_specs = (
        P(None, "seq", "tp"),
        P("segment", None, None, "tp"),
        P("segment", "tp", None),
        P("segment", None, None),
        P("segment", None, None),
        P("segment", None, None, "seq", "tp"),
        P("segment", None, None),
        P("segment", None),
        P(),
    )
    out_specs = (P("segment", None, "seq", "tp"), P("segment", None, None, "seq", "tp"))
    return jax.shard_map(local, mesh=mesh, in_specs=in_specs, out_specs=out_specs, check_vma=False)
```
